128 devices in a mesh: row: 8 (over y_lo, z), col: 16 (over x, y_hi, core).
Axes of the slice: x: 4, y: 4 (y_hi: 2, y_lo: 2; y = y_hi * 2 + y_lo), z: 4, core: 2. Of those that a mesh axis runs over, the one named last changes fastest.
Arguments:
- inputs: bfloat16 [12288, 8192], P('row', 'col'), may hold values from -6 to 6
- cotangent: bfloat16 [12288, 8192], P('row', 'col'), may hold values from -6 to 6
- conv_out: bfloat16 [12288, 8192], P('row', 'col'), may hold values from -6 to 6
- pre_act: bfloat16 [12288, 2048], P('row', 'col'), may hold values from -6 to 6
- weight_in: bfloat16 [8192, 2048], P('col', 'row'), may hold values from -0.0625 to 0.0625
- weight_out: bfloat16 [2048, 8192], P('row', 'col'), may hold values from -0.125 to 0.125
- scale_mid: float32 [2048], P('col'), may hold values from 0.3 to 3
- scale_wide: float32 [8192], P('col'), may hold values from 0.3 to 3
- keep_mid: int32 [2048], P('col'), may hold values 0 or 1
- keep_wide: int32 [8192], P('col'), may hold values 0 or 1
Outputs:
- grad_x: bfloat16 [12288, 8192], P('row', 'col')
- grad_win: float32 [8192, 2048], P('col', 'row')
- grad_wout: float32 [2048, 8192], P('row', 'col')
- grad_smid: float32 [2048], P('col')
- grad_swide: float32 [8192], P('col')
The draws below stay inside these ranges and needn't reach their ends.
All inputs are finite; a program needn't handle non-finite values. No bound on the sum of `keep_mid` or of `keep_wide` on one device may be relied on, other than what follows from the above.
Results may differ from the reference program's by a relative error of at most 0.03.
Values may be sent and summed in bfloat16 or wider, within the bound.
No kernel may reach another device: no remote copies, remote signals or barrier semaphores. Data moves between devices by JAX's collectives and lax.ppermute only.
A program may use at most 128 MiB of HBM per device.

```python
import math
import jax
import jax.numpy as jnp
from jax import lax

C = 8192
F = 2048
ROWS = 12288
N_COL = 16


def place_ends(array, own_key, low, top_value):
    place = [jax.random.randint(jax.random.fold_in(own_key, axis), (), 0, length) for axis, length in enumerate(array.shape)]
    widest = array.shape.index(max(array.shape))
    beside = place[:widest] + [(place[widest] + 1) % array.shape[widest]] + place[widest + 1:]
    return array.at[tuple(place)].set(low).at[tuple(beside)].set(top_value)


def block_levels(own_key, shape, pieces, low, largest):
    factor_of, own = 1.0, jax.random.fold_in(own_key, 6)
    for dim, parts in pieces:
        steps = jnp.exp(jax.random.uniform(jax.random.fold_in(own, dim), (parts,), jnp.float32, low / len(pieces), largest / len(pieces)))
        factor_of = factor_of * jnp.repeat(steps, shape[dim] // parts).reshape([-1 if axis == dim else 1 for axis in range(len(shape))])
    return factor_of


def gaussian(own_key, extent, scale, bound, pieces=(), held_as=jnp.bfloat16):
    result = jax.random.normal(own_key, extent, jnp.float32) * scale
    if len(pieces) > 0:
        result = block_levels(own_key, extent, pieces, -0.22, 0.18) * result
    return jnp.clip(result, min=-bound, max=bound).astype(held_as)


def setup_inputs(seed: int = 0) -> dict:
    key_list = jax.random.split(jax.random.key(seed), 11)
    return {
        "inputs": gaussian(key_list[0], (ROWS, C), 1.0, 6.0, ((0, 8), (1, 16))),
        "cotangent": gaussian(key_list[1], (ROWS, C), 1.0, 6.0, ((0, 8), (1, 16))),
        "conv_out": gaussian(key_list[2], (ROWS, C), 1.0, 6.0, ((0, 8), (1, 16))),
        "pre_act": gaussian(key_list[3], (ROWS, F), 1.0, 6.0, ((0, 8), (1, 16))),
        "weight_in": gaussian(key_list[4], (C, F), C ** -0.5, 0.0625, ((0, 16), (1, 8))),
        "weight_out": gaussian(key_list[5], (F, C), F ** -0.5, 0.125, ((0, 8), (1, 16))),
        "scale_mid": jnp.clip(jnp.exp(math.log(3.0) - 2.3025851 * jax.random.uniform(key_list[6], (F,), jnp.float32) ** block_levels(key_list[6], (F,), ((0, 16),), -0.2, 0.2)), 0.3, 3.0),
        "scale_wide": jnp.clip(jnp.exp(math.log(3.0) - 2.3025851 * jax.random.uniform(key_list[7], (C,), jnp.float32) ** block_levels(key_list[7], (C,), ((0, 16),), -0.2, 0.2)), 0.3, 3.0),
        "keep_mid": place_ends((jax.random.randint(key_list[8], (F,), 0, 4) < 3).astype(jnp.int32), jax.random.fold_in(key_list[8], 1), 0, 1),
        "keep_wide": place_ends((jax.random.randint(key_list[9], (C,), 0, 4) < 3).astype(jnp.int32), jax.random.fold_in(key_list[9], 1), 0, 1),
    }


def reference(inputs, cotangent, conv_out, pre_act, weight_in, weight_out, scale_mid, scale_wide, keep_mid, keep_wide):
    scaling = 1.0 / math.sqrt(ROWS)
    wide_gain = scale_wide * keep_wide.astype(jnp.float32)
    grad_conv = (cotangent.astype(jnp.float32) * wide_gain).astype(jnp.bfloat16)
    grad_swide = keep_wide.astype(jnp.float32) * scaling * lax.optimization_barrier(jnp.sum(cotangent.astype(jnp.float32) * conv_out.astype(jnp.float32), axis=0))
    mid_gain = scale_mid * keep_mid.astype(jnp.float32)
    pre_float = pre_act.astype(jnp.float32)
    hidden = jnp.maximum(pre_float * mid_gain, 0.0).astype(jnp.bfloat16)
    block_width = C // N_COL
    conv_blocks = jnp.transpose(grad_conv.reshape(ROWS, N_COL, block_width), (1, 0, 2))
    weight_blocks = jnp.transpose(weight_out.reshape(F, N_COL, block_width), (1, 0, 2))

    def add_block(total, pair):
        partial_sum = jnp.dot(pair[0], pair[1].T, preferred_element_type=jnp.float32)
        return (total + partial_sum.astype(jnp.bfloat16).astype(total.dtype), None)
    grad_hid, _ = lax.scan(add_block, jnp.zeros((ROWS, F), jnp.float32), (conv_blocks, weight_blocks))
    alive_mask = (pre_act > 0) & (keep_mid > 0)[None, :]
    grad_pre = jnp.where(alive_mask, grad_hid, 0.0)
    grad_smid = keep_mid.astype(jnp.float32) * scaling * lax.optimization_barrier(jnp.sum(grad_pre * pre_float, axis=0))
    grad_act = (grad_pre * mid_gain).astype(jnp.bfloat16)
    grad_wout = jnp.dot(hidden.T, grad_conv, preferred_element_type=jnp.float32) * scaling
    grad_x = (cotangent.astype(jnp.float32) + jnp.dot(grad_act, weight_in.T, preferred_element_type=jnp.float32)).astype(jnp.bfloat16)
    grad_win = jnp.dot(inputs.T, grad_act, preferred_element_type=jnp.float32) * scaling
    return (grad_x, grad_win, grad_wout, grad_smid, grad_swide)
```

```python
import math

import jax
import jax.numpy as jnp
from jax import lax
from jax.sharding import PartitionSpec as P

F32 = jnp.float32
BF16 = jnp.bfloat16
AXES = ("row", "col")


def flat_pairs(target):
    pairs = []
    for row in range(8):
        for col in range(16):
            where = target(row // 4, row % 4, col // 4, (col // 2) % 2, col % 2)
            y_lo, z, x, y_hi, core = where
            pairs.append(
                (row * 16 + col, (y_lo * 4 + z % 4) * 16 + (x % 4) * 4 + y_hi * 2 + core)
            )
    return pairs


def core_swap(v):
    return lax.ppermute(v, AXES, flat_pairs(lambda yl, z, x, yh, c: (yl, z, x, yh, 1 - c)))


def y_hi_swap(v):
    return lax.ppermute(v, AXES, flat_pairs(lambda yl, z, x, yh, c: (yl, z, x, 1 - yh, c)))


def y_lo_swap(v):
    return lax.ppermute(v, AXES, flat_pairs(lambda yl, z, x, yh, c: (1 - yl, z, x, yh, c)))


def x_shift(v, step):
    return lax.ppermute(v, AXES, flat_pairs(lambda yl, z, x, yh, c: (yl, z, x + step, yh, c)))


def x_split_shift(v):
    return lax.ppermute(
        v, AXES, flat_pairs(lambda yl, z, x, yh, c: (yl, z, x + 1 - 2 * c, yh, c))
    )


def z_shift(v, step):
    return lax.ppermute(v, AXES, flat_pairs(lambda yl, z, x, yh, c: (yl, z + step, x, yh, c)))


def z_flip(v, mask):
    return lax.ppermute(v, AXES, flat_pairs(lambda yl, z, x, yh, c: (yl, z ^ mask, x, yh, c)))


def dot(a, b, ca, cb):
    return lax.dot_general(a, b, (((ca,), (cb,)), ((), ())), preferred_element_type=F32)


def gather_x(block, y_hi, core):
    beside = y_hi_swap(block)
    first = y_hi == 0
    here = jnp.concatenate(
        [jnp.where(first, block, beside), jnp.where(first, beside, block)], axis=1
    )
    below = x_shift(here, 1)
    above = x_shift(here, -1)
    across = x_split_shift(jnp.where(core == 0, below, above))
    return {0: here, -1: below, 1: above, 2: across}


def reduce_z(whole, z, y_lo):
    parts = whole.reshape(2, 4, 256, 512)

    def take(step):
        return lax.dynamic_index_in_dim(parts, (z + step) % 4, 1, keepdims=False)

    total = take(0).astype(F32)
    for step in (1, 3, 2):
        total = total + z_shift(take(step), step).astype(F32)
    mine = lax.dynamic_index_in_dim(total, y_lo, 0, keepdims=False)
    other = lax.dynamic_index_in_dim(total, 1 - y_lo, 0, keepdims=False)
    return mine + y_lo_swap(other.astype(BF16)).astype(F32)


def local(
    inputs,
    cotangent,
    conv_out,
    pre_act,
    weight_in,
    weight_out,
    scale_mid,
    scale_wide,
    keep_mid,
    keep_wide,
):
    rows, width = inputs.shape
    half = rows // 2
    scaling = 1.0 / math.sqrt(rows * lax.axis_size("row"))
    row, col = lax.axis_index("row"), lax.axis_index("col")
    y_lo, z = row // 4, row % 4
    x, y_hi, core = col // 4, (col // 2) % 2, col % 2

    def mine(v):
        return lax.dynamic_slice_in_dim(v, core * half, half, 0)

    def theirs(v):
        return lax.dynamic_slice_in_dim(v, (1 - core) * half, half, 0)

    out_full = lax.all_gather(weight_out, "row", axis=0, tiled=True)
    in_full = lax.all_gather(weight_in, "row", axis=1, tiled=True)

    wide_gain = scale_wide * keep_wide.astype(F32)
    cot_float = cotangent.astype(F32)
    grad_conv = (cot_float * wide_gain).astype(BF16)
    wide_part = jnp.sum(cot_float * conv_out.astype(F32), axis=0)
    conv_mine, conv_theirs = mine(grad_conv), theirs(grad_conv)
    conv_beside = core_swap(conv_theirs)

    gain_pair = jnp.stack([scale_mid, keep_mid.astype(F32)])
    gain_beside = core_swap(gain_pair)
    pre_mine = mine(pre_act)
    pre_beside = core_swap(theirs(pre_act))

    def chip_order(a, b):
        return jnp.concatenate(
            [jnp.where(core == 0, a, b), jnp.where(core == 0, b, a)], axis=1
        )

    pre_chip = chip_order(pre_mine, pre_beside).astype(F32)
    gain_chip = chip_order(gain_pair, gain_beside)
    mid_gain = gain_chip[0] * gain_chip[1]
    hidden = jnp.maximum(pre_chip * mid_gain, 0.0).astype(BF16)
    hid = gather_x(hidden, y_hi, core)

    out_beside = core_swap(out_full)

    def partial(step):
        at = ((x + step) % 4) * 512
        a = lax.dynamic_slice_in_dim(out_full, at, 512, 0)
        b = lax.dynamic_slice_in_dim(out_beside, at, 512, 0)
        return dot(conv_mine, a, 1, 1) + dot(conv_beside, b, 1, 1)

    sends = {step: x_shift(partial(step).astype(BF16), step) for step in (2, 1, 3)}
    total = partial(0)
    for step in (1, 3, 2):
        total = total + sends[step].astype(F32)
    total = total.reshape(half, 2, 256)
    own = lax.dynamic_index_in_dim(total, y_hi, 1, keepdims=False)
    away = lax.dynamic_index_in_dim(total, 1 - y_hi, 1, keepdims=False)
    grad_hid = own + y_hi_swap(away.astype(BF16)).astype(F32)
    alive = (pre_chip > 0) & (gain_chip[1] > 0)[None, :]
    grad_pre = jnp.where(alive, grad_hid, 0.0)
    mid_part = jnp.sum(grad_pre * pre_chip, axis=0).reshape(2, 128)
    grad_act = (grad_pre * mid_gain).astype(BF16)
    act = gather_x(grad_act, y_hi, core)

    mid_own = lax.dynamic_index_in_dim(mid_part, core, 0, keepdims=False)
    mid_away = lax.dynamic_index_in_dim(mid_part, 1 - core, 0, keepdims=False)
    mid_own = mid_own + core_swap(mid_away)
    sums = jnp.concatenate([mid_own, wide_part]).reshape(5, 128)
    sums = sums + z_flip(sums, 1)
    sums = sums + z_flip(sums, 2)
    sums = sums + y_lo_swap(sums)
    grad_smid = keep_mid.astype(F32) * scaling * sums[0]
    grad_swide = keep_wide.astype(F32) * scaling * sums[1:].reshape(512)

    def weight_partial(blocks, a_mine, a_theirs):
        whole = jnp.zeros((2048, 512), BF16)
        for step, block in blocks.items():
            product = dot(block, a_mine, 0, 0) + dot(core_swap(block), a_theirs, 0, 0)
            whole = lax.dynamic_update_slice_in_dim(
                whole, product.astype(BF16), ((x + step) % 4) * 512, 0
            )
        return whole

    wout = weight_partial(hid, conv_mine, conv_theirs)
    grad_wout = (
        lax.psum_scatter(wout, "row", scatter_dimension=0, tiled=True).astype(F32) * scaling
    )

    act_beside = {step: core_swap(block) for step, block in act.items()}
    win = jnp.zeros((2048, 512), BF16)
    in_mine, in_theirs = mine(inputs), theirs(inputs)
    grad_mine, grad_theirs = mine(cotangent).astype(F32), theirs(cotangent).astype(F32)
    for step, block in act.items():
        at = ((x + step) % 4) * 512
        product = dot(block, in_mine, 0, 0) + dot(act_beside[step], in_theirs, 0, 0)
        win = lax.dynamic_update_slice_in_dim(win, product.astype(BF16), at, 0)
        weights = lax.dynamic_slice_in_dim(in_full, at, 512, 1)
        grad_mine = grad_mine + dot(block, weights, 1, 1)
        grad_theirs = grad_theirs + dot(act_beside[step], weights, 1, 1)
    grad_win = (reduce_z(win, z, y_lo) * scaling).T
    grad_x = jnp.zeros((rows, width), BF16)
    grad_x = lax.dynamic_update_slice_in_dim(grad_x, grad_mine.astype(BF16), core * half, 0)
    grad_x = lax.dynamic_update_slice_in_dim(
        grad_x, grad_theirs.astype(BF16), (1 - core) * half, 0
    )
    return (grad_x, grad_win, grad_wout, grad_smid, grad_swide)


def solution(mesh):
    return jax.shard_map(
        local,
        mesh=mesh,
        in_specs=(
            P("row", "col"),
            P("row", "col"),
            P("row", "col"),
            P("row", "col"),
            P("col", "row"),
            P("row", "col"),
            P("col"),
            P("col"),
            P("col"),
            P("col"),
        ),
        out_specs=(P("row", "col"), P("col", "row"), P("row", "col"), P("col"), P("col")),
        check_vma=False,
    )
```

```python
import math

import jax
import jax.numpy as jnp
from jax import lax
from jax.sharding import PartitionSpec as P

F32 = jnp.float32
BF16 = jnp.bfloat16
AXES = ("row", "col")


def flat_pairs(target):
    pairs = []
    for row in range(8):
        for col in range(16):
            where = target(row // 4, row % 4, col // 4, (col // 2) % 2, col % 2)
            y_lo, z, x, y_hi, core = where
            pairs.append(
                (row * 16 + col, (y_lo * 4 + z % 4) * 16 + (x % 4) * 4 + y_hi * 2 + core)
            )
    return pairs


def core_swap(v):
    return lax.ppermute(v, AXES, flat_pairs(lambda yl, z, x, yh, c: (yl, z, x, yh, 1 - c)))


def y_hi_swap(v):
    return lax.ppermute(v, AXES, flat_pairs(lambda yl, z, x, yh, c: (yl, z, x, 1 - yh, c)))


def y_lo_swap(v):
    return lax.ppermute(v, AXES, flat_pairs(lambda yl, z, x, yh, c: (1 - yl, z, x, yh, c)))


def x_shift(v, step):
    return lax.ppermute(v, AXES, flat_pairs(lambda yl, z, x, yh, c: (yl, z, x + step, yh, c)))


def x_split_shift(v):
    return lax.ppermute(
        v, AXES, flat_pairs(lambda yl, z, x, yh, c: (yl, z, x + 1 - 2 * c, yh, c))
    )


def z_shift(v, step):
    return lax.ppermute(v, AXES, flat_pairs(lambda yl, z, x, yh, c: (yl, z + step, x, yh, c)))


def z_flip(v, mask):
    return lax.ppermute(v, AXES, flat_pairs(lambda yl, z, x, yh, c: (yl, z ^ mask, x, yh, c)))


def dot(a, b, ca, cb):
    return lax.dot_general(a, b, (((ca,), (cb,)), ((), ())), preferred_element_type=F32)


def gather_x(block, core):
    here = jnp.concatenate([block, y_hi_swap(block)], axis=1)
    below = x_shift(here, 1)
    above = x_shift(here, -1)
    across = x_split_shift(jnp.where(core == 0, below, above))
    return {0: here, -1: below, 1: above, 2: across}


def z_split_shift(v):
    return lax.ppermute(
        v, AXES, flat_pairs(lambda yl, z, x, yh, c: (yl, z + 1 - 2 * c, x, yh, c))
    )


def gather_z(block, core):
    here = jnp.stack([block, y_lo_swap(block)])
    below = z_shift(here, 1)
    above = z_shift(here, -1)
    across = z_split_shift(jnp.where(core == 0, below, above))
    return {0: here, -1: below, 1: above, 2: across}


def reduce_z(whole, z, y_lo):
    parts = whole.reshape(2, 4, 256, 512)

    def take(step):
        return lax.dynamic_index_in_dim(parts, (z + step) % 4, 1, keepdims=False)

    total = take(0).astype(F32)
    for step in (1, 3, 2):
        total = total + z_shift(take(step), step).astype(F32)
    mine = lax.dynamic_index_in_dim(total, y_lo, 0, keepdims=False)
    other = lax.dynamic_index_in_dim(total, 1 - y_lo, 0, keepdims=False)
    return mine + y_lo_swap(other.astype(BF16)).astype(F32)


def local(
    inputs,
    cotangent,
    conv_out,
    pre_act,
    weight_in,
    weight_out,
    scale_mid,
    scale_wide,
    keep_mid,
    keep_wide,
):
    rows, width = inputs.shape
    half = rows // 2
    scaling = 1.0 / math.sqrt(rows * lax.axis_size("row"))
    row, col = lax.axis_index("row"), lax.axis_index("col")
    y_lo, z = row // 4, row % 4
    x, y_hi, core = col // 4, (col // 2) % 2, col % 2

    def mine(v):
        return lax.dynamic_slice_in_dim(v, core * half, half, 0)

    def theirs(v):
        return lax.dynamic_slice_in_dim(v, (1 - core) * half, half, 0)

    out_blocks = gather_z(weight_out, core)

    wide_gain = scale_wide * keep_wide.astype(F32)
    cot_float = cotangent.astype(F32)
    grad_conv = (cot_float * wide_gain).astype(BF16)
    wide_part = jnp.sum(cot_float * conv_out.astype(F32), axis=0)
    conv_mine, conv_theirs = mine(grad_conv), theirs(grad_conv)
    conv_beside = core_swap(conv_theirs)

    gain_pair = jnp.stack([scale_mid, keep_mid.astype(F32)])
    gain_beside = core_swap(gain_pair)
    pre_mine = mine(pre_act)
    pre_beside = core_swap(theirs(pre_act))

    def chip_order(a, b):
        return jnp.concatenate(
            [jnp.where(core == 0, a, b), jnp.where(core == 0, b, a)], axis=1
        )

    pre_chip = chip_order(pre_mine, pre_beside).astype(F32)
    gain_chip = chip_order(gain_pair, gain_beside)
    mid_gain = gain_chip[0] * gain_chip[1]
    hidden = jnp.maximum(pre_chip * mid_gain, 0.0).astype(BF16)
    hid = gather_x(hidden, core)

    out_full = jnp.zeros((2, 4, 256, 1024), BF16)
    for step, block in out_blocks.items():
        wide = jnp.concatenate([block, core_swap(block)], axis=2)
        for i, at in ((0, y_lo), (1, 1 - y_lo)):
            out_full = lax.dynamic_update_slice(
                out_full, wide[i][None, None], (at, (z + step) % 4, 0, 0)
            )
    out_full = out_full.reshape(2048, 1024)
    conv_both = jnp.concatenate([conv_mine, conv_beside], axis=1)
    weight_in, out_full = lax.optimization_barrier((weight_in, out_full))
    in_full = lax.all_gather(weight_in, "row", axis=1, tiled=True)

    def partial(step):
        at = ((x + step) % 4) * 512
        return dot(conv_both, lax.dynamic_slice_in_dim(out_full, at, 512, 0), 1, 1)

    sends = {step: x_shift(partial(step).astype(BF16), step) for step in (2, 1, 3)}
    total = partial(0)
    for step in (1, 3, 2):
        total = total + sends[step].astype(F32)
    total = total.reshape(half, 2, 256)
    own = lax.dynamic_index_in_dim(total, y_hi, 1, keepdims=False)
    away = lax.dynamic_index_in_dim(total, 1 - y_hi, 1, keepdims=False)
    grad_hid = own + y_hi_swap(away.astype(BF16)).astype(F32)
    alive = (pre_chip > 0) & (gain_chip[1] > 0)[None, :]
    grad_pre = jnp.where(alive, grad_hid, 0.0)
    mid_part = jnp.sum(grad_pre * pre_chip, axis=0).reshape(2, 128)
    grad_act = (grad_pre * mid_gain).astype(BF16)

    def weight_partial(blocks, beside, a_mine, a_theirs):
        whole = jnp.zeros((2048, 512), BF16)
        for step, block in blocks.items():
            product = dot(block, a_mine, 0, 0) + dot(beside[step], a_theirs, 0, 0)
            product = product.astype(BF16)
            for i, y in ((0, y_hi), (1, 1 - y_hi)):
                whole = lax.dynamic_update_slice_in_dim(
                    whole,
                    product[i * 256 : i * 256 + 256],
                    ((x + step) % 4) * 512 + y * 256,
                    0,
                )
        return whole

    hid_beside = {step: core_swap(block) for step, block in hid.items()}
    wout = weight_partial(hid, hid_beside, conv_mine, conv_theirs)
    grad_act, wout = lax.optimization_barrier((grad_act, wout))
    grad_wout = (
        lax.psum_scatter(wout, "row", scatter_dimension=0, tiled=True).astype(F32) * scaling
    )
    act = gather_x(grad_act, core)

    mid_own = lax.dynamic_index_in_dim(mid_part, core, 0, keepdims=False)
    mid_away = lax.dynamic_index_in_dim(mid_part, 1 - core, 0, keepdims=False)
    mid_own = mid_own + core_swap(mid_away)
    sums = jnp.concatenate([mid_own, wide_part]).reshape(5, 128)
    sums = sums + z_flip(sums, 1)
    sums = sums + z_flip(sums, 2)
    sums = sums + y_lo_swap(sums)
    grad_smid = keep_mid.astype(F32) * scaling * sums[0]
    grad_swide = keep_wide.astype(F32) * scaling * sums[1:].reshape(512)

    act_beside = {step: core_swap(block) for step, block in act.items()}
    win = weight_partial(act, act_beside, mine(inputs), theirs(inputs))
    grad_win = (reduce_z(win, z, y_lo) * scaling).T
    act, act_beside, win = lax.optimization_barrier((act, act_beside, win))
    grad_mine, grad_theirs = mine(cotangent).astype(F32), theirs(cotangent).astype(F32)
    for step, block in act.items():
        at = ((x + step) % 4) * 512
        weights = jnp.concatenate(
            [
                lax.dynamic_slice_in_dim(in_full, at + y * 256, 256, 1)
                for y in (y_hi, 1 - y_hi)
            ],
            axis=1,
        )
        grad_mine = grad_mine + dot(block, weights, 1, 1)
        grad_theirs = grad_theirs + dot(act_beside[step], weights, 1, 1)
    grad_x = jnp.zeros((rows, width), BF16)
    grad_x = lax.dynamic_update_slice_in_dim(grad_x, grad_mine.astype(BF16), core * half, 0)
    grad_x = lax.dynamic_update_slice_in_dim(
        grad_x, grad_theirs.astype(BF16), (1 - core) * half, 0
    )
    return (grad_x, grad_win, grad_wout, grad_smid, grad_swide)


def solution(mesh):
    return jax.shard_map(
        local,
        mesh=mesh,
        in_specs=(
            P("row", "col"),
            P("row", "col"),
            P("row", "col"),
            P("row", "col"),
            P("col", "row"),
            P("row", "col"),
            P("col"),
            P("col"),
            P("col"),
            P("col"),
        ),
        out_specs=(P("row", "col"), P("col", "row"), P("row", "col"), P("col"), P("col")),
        check_vma=False,
    )
```

```python
import math

import jax
import jax.numpy as jnp
from jax import lax
from jax.experimental import pallas as pl
from jax.experimental.pallas import tpu as pltpu
from jax.sharding import PartitionSpec as P

F32 = jnp.float32
BF16 = jnp.bfloat16
AXES = ("row", "col")
STEPS = (0, 1, 3, 2)


def permute(v, target):
    pairs = []
    for row in range(8):
        for col in range(16):
            y_lo, z, x, y_hi, core = target(
                row // 4, row % 4, col // 4, (col // 2) % 2, col % 2
            )
            pairs.append(
                (row * 16 + col, (y_lo * 4 + z % 4) * 16 + (x % 4) * 4 + y_hi * 2 + core)
            )
    return lax.ppermute(v, AXES, pairs)


def core_swap(v):
    return permute(v, lambda yl, z, x, yh, c: (yl, z, x, yh, 1 - c))


def y_hi_swap(v):
    return permute(v, lambda yl, z, x, yh, c: (yl, z, x, 1 - yh, c))


def y_lo_swap(v):
    return permute(v, lambda yl, z, x, yh, c: (1 - yl, z, x, yh, c))


def z_flip(v, mask):
    return permute(v, lambda yl, z, x, yh, c: (yl, z ^ mask, x, yh, c))


def x_shift(v, step):
    return permute(v, lambda yl, z, x, yh, c: (yl, z, x + step, yh, c))


def z_shift(v, step):
    return permute(v, lambda yl, z, x, yh, c: (yl, z + step, x, yh, c))


def x_split(v, way):
    return permute(v, lambda yl, z, x, yh, c: (yl, z, x + way * (1 - 2 * c), yh, c))


def z_split(v, way):
    return permute(v, lambda yl, z, x, yh, c: (yl, z + way * (1 - 2 * c), x, yh, c))


def dot(a, b, ca, cb):
    return lax.dot_general(a, b, (((ca,), (cb,)), ((), ())), preferred_element_type=F32)


def gather(block, core, swap, shift, split):
    here = jnp.stack([block, swap(block)])
    below = shift(here, 1)
    above = shift(here, -1)
    return [here, above, below, split(jnp.where(core == 0, below, above), 1)]


def load_blocks(refs, held, sems):
    half = held.shape[2] // 2
    copies = []
    for k, ref in enumerate(refs):
        copies.append(
            pltpu.make_async_copy(
                ref, held.at[k % 4, :, pl.ds((k // 4) * half, half), :], sems.at[k]
            )
        )
    for copy in copies:
        copy.start()
    for copy in copies:
        copy.wait()


def weight_kernel(place, left, *refs):
    blocks, outs, (held, sems) = refs[:8], refs[8:12], refs[12:]
    load_blocks(blocks, held, sems)
    for o, out in enumerate(outs):
        for i in range(2):
            at = o * 2 + i
            block = held[place[at, 0], place[at, 1]]
            out[i] = jnp.dot(left[...], block, preferred_element_type=F32).astype(BF16)


def weight_partial(place, left, mine, beside):
    any_space = pl.BlockSpec(memory_space=pl.ANY)
    vmem = pl.BlockSpec(memory_space=pltpu.VMEM)
    return pl.pallas_call(
        weight_kernel,
        out_shape=[jax.ShapeDtypeStruct((2, 512, 256), BF16)] * 4,
        in_specs=[pl.BlockSpec(memory_space=pltpu.SMEM), vmem] + [any_space] * 8,
        out_specs=[vmem] * 4,
        scratch_shapes=[pltpu.VMEM((4, 2, 1536, 256), BF16), pltpu.SemaphoreType.DMA((8,))],
        compiler_params=pltpu.CompilerParams(vmem_limit_bytes=32 * 1024 * 1024),
        cost_estimate=pl.CostEstimate(
            flops=2 * 1536 * 512 * 2048, bytes_accessed=10 * 1024 * 1024, transcendentals=0
        ),
    )(place, left, *mine, *beside)


def out_kernel(place, weights, cot, *refs):
    blocks, out, (held, sems) = refs[:8], refs[8], refs[9:]
    load_blocks(blocks, held, sems)
    tile = 256
    for part in range(2):
        start = place[8 + part, 0] * 768
        for t in range(3):
            at = pl.multiple_of(start + t * tile, tile)
            total = cot[pl.ds(at, tile), :].astype(F32)
            for k in range(8):
                columns = pl.ds(pl.multiple_of(place[k, 0] * 256, 256), 256)
                total = total + lax.dot_general(
                    held[k // 2, k % 2, pl.ds(part * 768 + t * tile, tile), :],
                    weights[:, columns],
                    (((1,), (1,)), ((), ())),
                    preferred_element_type=F32,
                )
            out[pl.ds(at, tile), :] = total.astype(BF16)


def out_gradient(place, weights, cot, mine, beside):
    any_space = pl.BlockSpec(memory_space=pl.ANY)
    vmem = pl.BlockSpec(memory_space=pltpu.VMEM)
    return pl.pallas_call(
        out_kernel,
        out_shape=jax.ShapeDtypeStruct((1536, 512), BF16),
        in_specs=[pl.BlockSpec(memory_space=pltpu.SMEM), vmem, vmem] + [any_space] * 8,
        out_specs=vmem,
        scratch_shapes=[pltpu.VMEM((4, 2, 1536, 256), BF16), pltpu.SemaphoreType.DMA((8,))],
        compiler_params=pltpu.CompilerParams(vmem_limit_bytes=32 * 1024 * 1024),
        cost_estimate=pl.CostEstimate(
            flops=2 * 1536 * 512 * 2048, bytes_accessed=12 * 1024 * 1024, transcendentals=0
        ),
    )(place, weights, cot, *mine, *beside)


def reduce(away, there, onward, here, split):
    passed = split(away, 1)
    back = split(there, -1)
    onward = (onward + passed.astype(F32)).astype(BF16)
    return here + back.astype(F32) + split(onward, 1).astype(F32)


def local(
    inputs,
    cotangent,
    conv_out,
    pre_act,
    weight_in,
    weight_out,
    scale_mid,
    scale_wide,
    keep_mid,
    keep_wide,
):
    rows = inputs.shape[0]
    half = rows // 2
    scaling = 1.0 / math.sqrt(rows * lax.axis_size("row"))
    row, col = lax.axis_index("row"), lax.axis_index("col")
    y_lo, z = row // 4, row % 4
    x, y_hi, core = col // 4, (col // 2) % 2, col % 2
    ahead = 1 - 2 * core

    def mine(v):
        return lax.dynamic_slice_in_dim(v, core * half, half, 0)

    def theirs(v):
        return lax.dynamic_slice_in_dim(v, (1 - core) * half, half, 0)

    def halves(v):
        return jnp.concatenate([mine(v), theirs(v)], axis=0)

    out_blocks = gather(weight_out, core, y_lo_swap, z_shift, z_split)

    gain_pair = jnp.stack([scale_mid, keep_mid.astype(F32)])
    gain_beside = core_swap(gain_pair)
    pre_mine = mine(pre_act)
    pre_beside = core_swap(theirs(pre_act))

    def chip_order(a, b):
        return jnp.concatenate(
            [jnp.where(core == 0, a, b), jnp.where(core == 0, b, a)], axis=1
        )

    pre_chip = chip_order(pre_mine, pre_beside).astype(F32)
    gain_chip = chip_order(gain_pair, gain_beside)
    mid_gain = gain_chip[0] * gain_chip[1]
    hidden = jnp.maximum(pre_chip * mid_gain, 0.0).astype(BF16)
    hid = gather(hidden, core, y_hi_swap, x_shift, x_split)

    wide_gain = scale_wide * keep_wide.astype(F32)
    cot_float = cotangent.astype(F32)
    grad_conv = (cot_float * wide_gain).astype(BF16)
    wide_part = jnp.sum(cot_float * conv_out.astype(F32), axis=0)
    conv_mine, conv_theirs = mine(grad_conv), theirs(grad_conv)
    conv_both = jnp.concatenate([conv_mine, core_swap(conv_theirs)], axis=1)

    out_full = jnp.zeros((2, 4, 256, 1024), BF16)
    for step, block in zip(STEPS, out_blocks):
        wide = jnp.concatenate([block, core_swap(block)], axis=2)
        for i, at in ((0, y_lo), (1, 1 - y_lo)):
            out_full = lax.dynamic_update_slice(
                out_full, wide[i][None, None], (at, (z + step) % 4, 0, 0)
            )
    out_full = out_full.reshape(2048, 1024)
    out_full, weight_in, hid[0], hid[1], hid[2] = lax.optimization_barrier(
        (out_full, weight_in, hid[0], hid[1], hid[2])
    )
    in_full = lax.all_gather(weight_in, "row", axis=1, tiled=True)

    def partial(step):
        at = ((x + step) % 4) * 512
        return dot(conv_both, lax.dynamic_slice_in_dim(out_full, at, 512, 0), 1, 1)

    hid_beside = [core_swap(block) for block in hid]

    def block_of(row_z, row_y):
        step = (row_y * 2 + row_z // 2 - x) % 4
        slot = jnp.array([0, 1, 3, 2], jnp.int32)[step]
        return jnp.stack([slot, (row_z % 2) ^ y_hi])

    send_place = jnp.stack(
        [
            block_of((z + step) % 4, y_lo ^ i)
            for step in (2, -ahead, ahead, 0)
            for i in range(2)
        ]
    ).astype(jnp.int32)
    natural = [((x + step) % 4) * 2 + (y_hi ^ i) for step in STEPS for i in range(2)]
    out_place = jnp.stack([jnp.stack(natural + [core, 1 - core]), jnp.zeros(10, jnp.int32)], 1)
    out_place = out_place.astype(jnp.int32)
    scatter_place = jnp.stack(
        [block_of(r % 4, jnp.int32(r // 4)) for r in range(8)]
    ).astype(jnp.int32)

    wout = weight_partial(
        scatter_place,
        jnp.concatenate([conv_mine, conv_theirs], axis=0).T,
        hid,
        hid_beside,
    )
    total = reduce(
        partial(2).astype(BF16), partial(-ahead).astype(BF16), partial(ahead), partial(0), x_split
    )
    total = total.reshape(half, 2, 256)
    own = lax.dynamic_index_in_dim(total, y_hi, 1, keepdims=False)
    away = lax.dynamic_index_in_dim(total, 1 - y_hi, 1, keepdims=False)
    grad_hid = own + y_hi_swap(away.astype(BF16)).astype(F32)
    alive = (pre_chip > 0) & (gain_chip[1] > 0)[None, :]
    grad_pre = jnp.where(alive, grad_hid, 0.0)
    mid_part = jnp.sum(grad_pre * pre_chip, axis=0).reshape(2, 128)
    grad_act = (grad_pre * mid_gain).astype(BF16)
    grad_act, wout, in_full = lax.optimization_barrier((grad_act, wout, in_full))
    wout = lax.psum_scatter(
        jnp.concatenate(wout, axis=0), "row", scatter_dimension=0, tiled=False
    )
    act = gather(grad_act, core, y_hi_swap, x_shift, x_split)

    mid_own = lax.dynamic_index_in_dim(mid_part, core, 0, keepdims=False)
    mid_away = lax.dynamic_index_in_dim(mid_part, 1 - core, 0, keepdims=False)
    mid_own = mid_own + core_swap(mid_away)
    sums = jnp.concatenate([mid_own, wide_part]).reshape(5, 128)
    sums = sums + z_flip(sums, 1)
    sums = sums + z_flip(sums, 2)
    sums = sums + y_lo_swap(sums)
    grad_smid = keep_mid.astype(F32) * scaling * sums[0]
    grad_swide = keep_wide.astype(F32) * scaling * sums[1:].reshape(512)

    act_beside = [core_swap(block) for block in act]
    win = weight_partial(send_place, halves(inputs).T, act, act_beside)
    total = reduce(win[0], win[1], win[2].astype(F32), win[3].astype(F32), z_split)
    act, act_beside, win, wout = lax.optimization_barrier((act, act_beside, win, wout))
    grad_win = (total[0] + y_lo_swap(total[1].astype(BF16)).astype(F32)) * scaling
    grad_wout = wout.astype(F32).T * scaling
    grad_x = out_gradient(out_place, in_full, cotangent, act, act_beside)
    return (grad_x, grad_win, grad_wout, grad_smid, grad_swide)


def solution(mesh):
    return jax.shard_map(
        local,
        mesh=mesh,
        in_specs=(
            P("row", "col"),
            P("row", "col"),
            P("row", "col"),
            P("row", "col"),
            P("col", "row"),
            P("row", "col"),
            P("col"),
            P("col"),
            P("col"),
            P("col"),
        ),
        out_specs=(P("row", "col"), P("col", "row"), P("row", "col"), P("col"), P("col")),
        check_vma=False,
    )
```

```python
import math

import jax
import jax.numpy as jnp
from jax import lax
from jax.experimental import pallas as pl
from jax.experimental.pallas import tpu as pltpu
from jax.sharding import PartitionSpec as P

F32 = jnp.float32
BF16 = jnp.bfloat16
AXES = ("row", "col")
STEPS = (0, 1, 3, 2)


def permute(v, target):
    pairs = []
    for row in range(8):
        for col in range(16):
            y_lo, z, x, y_hi, core = target(
                row // 4, row % 4, col // 4, (col // 2) % 2, col % 2
            )
            pairs.append(
                (row * 16 + col, (y_lo * 4 + z % 4) * 16 + (x % 4) * 4 + y_hi * 2 + core)
            )
    return lax.ppermute(v, AXES, pairs)


def core_swap(v):
    return permute(v, lambda yl, z, x, yh, c: (yl, z, x, yh, 1 - c))


def y_hi_swap(v):
    return permute(v, lambda yl, z, x, yh, c: (yl, z, x, 1 - yh, c))


def y_lo_swap(v):
    return permute(v, lambda yl, z, x, yh, c: (1 - yl, z, x, yh, c))


def z_flip(v, mask):
    return permute(v, lambda yl, z, x, yh, c: (yl, z ^ mask, x, yh, c))


def x_shift(v, step):
    return permute(v, lambda yl, z, x, yh, c: (yl, z, x + step, yh, c))


def z_shift(v, step):
    return permute(v, lambda yl, z, x, yh, c: (yl, z + step, x, yh, c))


def x_split(v, way):
    return permute(v, lambda yl, z, x, yh, c: (yl, z, x + way * (1 - 2 * c), yh, c))


def z_split(v, way):
    return permute(v, lambda yl, z, x, yh, c: (yl, z + way * (1 - 2 * c), x, yh, c))


def dot(a, b, ca, cb):
    return lax.dot_general(a, b, (((ca,), (cb,)), ((), ())), preferred_element_type=F32)


def gather(block, core, swap, shift, split):
    above, below = shift(block, -1), shift(block, 1)
    beside = swap(block)
    beside_above, beside_below = shift(beside, -1), shift(beside, 1)
    across = split(jnp.where(core == 0, below, above), 1)
    beside_across = split(jnp.where(core == 0, beside_below, beside_above), 1)
    return [block, beside, above, beside_above, below, beside_below, across, beside_across]


def place_of(v):
    row, col = v[0], v[1]
    return row, row >> 2, row & 3, col >> 2, (col >> 1) & 1, col & 1


def slot_of(step):
    step = step & 3
    return jnp.where(step >= 2, 5 - step, step)


def load(copies):
    for copy in copies:
        copy.start()
    for copy in copies:
        copy.wait()


def call(body, outs, scratch, loads, flops, here, vmem_args, any_args):
    vmem = pl.BlockSpec(memory_space=pltpu.VMEM)
    return pl.pallas_call(
        body,
        out_shape=outs,
        in_specs=[pl.BlockSpec(memory_space=pltpu.SMEM)]
        + [vmem] * len(vmem_args)
        + [pl.BlockSpec(memory_space=pl.ANY)] * len(any_args),
        out_specs=[vmem] * len(outs),
        scratch_shapes=[
            pltpu.VMEM(scratch, BF16),
            pltpu.SemaphoreType.DMA((len(any_args),)),
        ],
        compiler_params=pltpu.CompilerParams(vmem_limit_bytes=32 * 1024 * 1024),
        cost_estimate=pl.CostEstimate(flops=flops, bytes_accessed=loads, transcendentals=0),
    )(here, *vmem_args, *any_args)


def hid_kernel(here, conv_mine, conv_beside, *refs):
    blocks, outs, (held, sems) = refs[:16], refs[16:20], refs[20:]
    load(
        [
            pltpu.make_async_copy(
                ref, held.at[k % 8, :, pl.ds((k // 8) * 512, 512)], sems.at[k]
            )
            for k, ref in enumerate(blocks)
        ]
    )
    row, y_lo, z, x, y_hi, core = place_of(here)
    ahead = 1 - 2 * core
    for out, step in zip(outs, (2, -ahead, ahead, 0)):
        for i in range(2):
            block = ((x + step) & 3) * 2 + (y_hi ^ i)
            slot = slot_of((block & 3) - z) * 2 + ((block >> 2) ^ y_lo)
            total = lax.dot_general(
                conv_mine[...], held[slot, :, :512], (((1,), (1,)), ((), ())),
                preferred_element_type=F32,
            ) + lax.dot_general(
                conv_beside[...], held[slot, :, 512:], (((1,), (1,)), ((), ())),
                preferred_element_type=F32,
            )
            out[i] = total.astype(BF16)


def hid_partial(here, conv_mine, conv_beside, blocks, beside):
    return call(
        hid_kernel, [jax.ShapeDtypeStruct((2, 768, 256), BF16)] * 4, (8, 256, 1024),
        9 << 20, 2 * 1536 * 512 * 2048, here, [conv_mine, conv_beside], [*blocks, *beside],
    )


def hidden_slot(block, x, y_hi):
    return slot_of((block >> 1) - x) * 2 + ((block & 1) ^ y_hi)


def wout_kernel(here, left, *refs):
    blocks, out, (held, sems) = refs[:16], refs[16], refs[17:]
    row, y_lo, z, x, y_hi, core = place_of(here)
    copies = []
    for k, ref in enumerate(blocks):
        at = core if k < 8 else 1 - core
        columns = pl.ds(pl.multiple_of(at * 128, 128), 128)
        copies.append(pltpu.make_async_copy(ref, held.at[k % 8, :, columns], sems.at[k]))
    load(copies)
    for block in range(8):
        out[block] = jnp.dot(
            left[...], held[hidden_slot(block, x, y_hi)], preferred_element_type=F32
        ).astype(BF16)


def wout_partial(here, left, blocks, beside):
    return call(
        wout_kernel, [jax.ShapeDtypeStruct((8, 512, 256), BF16)], (8, 1536, 256),
        10 << 20, 2 * 1536 * 512 * 2048, here, [left], [*blocks, *beside],
    )[0]


def load_act(blocks, held, sems, core):
    copies = []
    for k, ref in enumerate(blocks):
        at = core if k < 8 else 1 - core
        rows = pl.ds(pl.multiple_of(at * 768, 768), 768)
        copies.append(pltpu.make_async_copy(ref, held.at[k % 8, rows, :], sems.at[k]))
    load(copies)


def win_kernel(here, left, *refs):
    blocks, outs, (held, sems) = refs[:16], refs[16:20], refs[20:]
    row, y_lo, z, x, y_hi, core = place_of(here)
    load_act(blocks, held, sems, core)
    ahead = 1 - 2 * core
    for out, step in zip(outs, (2, -ahead, ahead, 0)):
        for i in range(2):
            block = (y_lo ^ i) * 4 + ((z + step) & 3)
            out[i] = jnp.dot(
                left[...], held[hidden_slot(block, x, y_hi)], preferred_element_type=F32
            ).astype(BF16)


def win_partial(here, left, blocks, beside):
    return call(
        win_kernel, [jax.ShapeDtypeStruct((2, 512, 256), BF16)] * 4, (8, 1536, 256),
        10 << 20, 2 * 1536 * 512 * 2048, here, [left], [*blocks, *beside],
    )


def out_kernel(here, weights, cot, *refs):
    blocks, out, (held, sems) = refs[:16], refs[16], refs[17:]
    row, y_lo, z, x, y_hi, core = place_of(here)
    load_act(blocks, held, sems, core)
    for at in range(0, 1536, 256):
        total = cot[at : at + 256, :].astype(F32)
        for block in range(8):
            total = total + lax.dot_general(
                held[hidden_slot(block, x, y_hi), at : at + 256, :],
                weights[:, block * 256 : block * 256 + 256],
                (((1,), (1,)), ((), ())),
                preferred_element_type=F32,
            )
        out[at : at + 256, :] = total.astype(BF16)


def out_gradient(here, weights, cot, blocks, beside):
    return call(
        out_kernel, [jax.ShapeDtypeStruct((1536, 512), BF16)], (8, 1536, 256),
        12 << 20, 2 * 1536 * 512 * 2048, here, [weights, cot], [*blocks, *beside],
    )[0]


def reduce(away, there, onward, here, split):
    passed = split(away, 1)
    back = split(there, -1)
    onward = (onward.astype(F32) + passed.astype(F32)).astype(BF16)
    return here, back, split(onward, 1)


def add(terms):
    return sum(term.astype(F32) for term in terms)


def local(
    inputs,
    cotangent,
    conv_out,
    pre_act,
    weight_in,
    weight_out,
    scale_mid,
    scale_wide,
    keep_mid,
    keep_wide,
):
    rows = inputs.shape[0]
    half = rows // 2
    scaling = 1.0 / math.sqrt(rows * lax.axis_size("row"))
    row, col = lax.axis_index("row"), lax.axis_index("col")
    y_lo, z = row // 4, row % 4
    x, y_hi, core = col // 4, (col // 2) % 2, col % 2
    place = jnp.stack([row, col]).astype(jnp.int32)

    def mine(v):
        return lax.dynamic_slice_in_dim(v, core * half, half, 0)

    def theirs(v):
        return lax.dynamic_slice_in_dim(v, (1 - core) * half, half, 0)

    out_blocks = gather(weight_out, core, y_lo_swap, z_shift, z_split)
    mid_gain = scale_mid * keep_mid.astype(F32)
    hidden = jnp.maximum(pre_act.astype(F32) * mid_gain, 0.0).astype(BF16)
    hid = gather(hidden, core, y_hi_swap, x_shift, x_split)

    wide_gain = scale_wide * keep_wide.astype(F32)
    cot_float = cotangent.astype(F32)
    grad_conv = (cot_float * wide_gain).astype(BF16)
    wide_part = jnp.sum(cot_float * conv_out.astype(F32), axis=0)
    conv_mine = mine(grad_conv)
    conv_beside = core_swap(theirs(grad_conv))

    gain_pair = jnp.stack([scale_mid, keep_mid.astype(F32)])
    gain_beside = core_swap(gain_pair)
    pre_mine = mine(pre_act)
    pre_beside = core_swap(theirs(pre_act))

    def chip_order(a, b):
        return jnp.concatenate(
            [jnp.where(core == 0, a, b), jnp.where(core == 0, b, a)], axis=1
        )

    pre_chip = chip_order(pre_mine, pre_beside).astype(F32)
    gain_chip = chip_order(gain_pair, gain_beside)
    mid_gain = gain_chip[0] * gain_chip[1]

    out_beside = [core_swap(block) for block in out_blocks]
    input_turned, conv_turned = inputs.T, grad_conv.T
    out_beside[7], weight_in, hid[2:6], input_turned, conv_turned = lax.optimization_barrier(
        (out_beside[7], weight_in, hid[2:6], input_turned, conv_turned)
    )
    in_full = lax.all_gather(weight_in, "row", axis=1, tiled=True)
    hid_beside = [core_swap(block) for block in hid]
    wout = wout_partial(place, conv_turned, hid, hid_beside)
    partials = hid_partial(place, conv_mine, conv_beside, out_blocks, out_beside)
    terms = reduce(*partials, x_split)
    terms, wout = lax.optimization_barrier((terms, wout))
    wout = lax.psum_scatter(wout, "row", scatter_dimension=0, tiled=False)
    total = add(terms)
    grad_hid = total[0] + y_hi_swap(total[1].astype(BF16)).astype(F32)
    alive = (pre_chip > 0) & (gain_chip[1] > 0)[None, :]
    grad_pre = jnp.where(alive, grad_hid, 0.0)
    mid_part = jnp.sum(grad_pre * pre_chip, axis=0).reshape(2, 128)
    grad_act = (grad_pre * mid_gain).astype(BF16)
    act = gather(grad_act, core, y_hi_swap, x_shift, x_split)

    mid_own = lax.dynamic_index_in_dim(mid_part, core, 0, keepdims=False)
    mid_away = lax.dynamic_index_in_dim(mid_part, 1 - core, 0, keepdims=False)
    mid_own = mid_own + core_swap(mid_away)
    sums = jnp.concatenate([mid_own, wide_part]).reshape(5, 128)
    sums = sums + z_flip(sums, 1)
    sums = sums + z_flip(sums, 2)
    sums = sums + y_lo_swap(sums)
    grad_smid = keep_mid.astype(F32) * scaling * sums[0]
    grad_swide = keep_wide.astype(F32) * scaling * sums[1:].reshape(512)

    act_beside = [core_swap(block) for block in act]
    win = win_partial(place, input_turned, act, act_beside)
    act[7], win = lax.optimization_barrier((act[7], win))
    total = add(reduce(*win, z_split))
    grad_win = (total[0] + y_lo_swap(total[1].astype(BF16)).astype(F32)) * scaling
    grad_wout = wout.astype(F32).T * scaling
    grad_x = out_gradient(place, in_full, cotangent, act, act_beside)
    return (grad_x, grad_win, grad_wout, grad_smid, grad_swide)


def solution(mesh):
    return jax.shard_map(
        local,
        mesh=mesh,
        in_specs=(
            P("row", "col"),
            P("row", "col"),
            P("row", "col"),
            P("row", "col"),
            P("col", "row"),
            P("row", "col"),
            P("col"),
            P("col"),
            P("col"),
            P("col"),
        ),
        out_specs=(P("row", "col"), P("col", "row"), P("row", "col"), P("col"), P("col")),
        check_vma=False,
    )
```

```python
import math

import jax
import jax.numpy as jnp
from jax import lax
from jax.experimental import pallas as pl
from jax.experimental.pallas import tpu as pltpu
from jax.sharding import PartitionSpec as P

F32 = jnp.float32
BF16 = jnp.bfloat16
AXES = ("row", "col")
STEPS = (0, 1, 3, 2)


def permute(v, target):
    pairs = []
    for row in range(8):
        for col in range(16):
            y_lo, z, x, y_hi, core = target(
                row // 4, row % 4, col // 4, (col // 2) % 2, col % 2
            )
            pairs.append(
                (row * 16 + col, (y_lo * 4 + z % 4) * 16 + (x % 4) * 4 + y_hi * 2 + core)
            )
    return lax.ppermute(v, AXES, pairs)


def core_swap(v):
    return permute(v, lambda yl, z, x, yh, c: (yl, z, x, yh, 1 - c))


def y_hi_swap(v):
    return permute(v, lambda yl, z, x, yh, c: (yl, z, x, 1 - yh, c))


def y_lo_swap(v):
    return permute(v, lambda yl, z, x, yh, c: (1 - yl, z, x, yh, c))


def z_flip(v, mask):
    return permute(v, lambda yl, z, x, yh, c: (yl, z ^ mask, x, yh, c))


def x_shift(v, step):
    return permute(v, lambda yl, z, x, yh, c: (yl, z, x + step, yh, c))


def z_shift(v, step):
    return permute(v, lambda yl, z, x, yh, c: (yl, z + step, x, yh, c))


def x_split(v, way):
    return permute(v, lambda yl, z, x, yh, c: (yl, z, x + way * (1 - 2 * c), yh, c))


def z_split(v, way):
    return permute(v, lambda yl, z, x, yh, c: (yl, z + way * (1 - 2 * c), x, yh, c))


def dot(a, b, ca, cb):
    return lax.dot_general(a, b, (((ca,), (cb,)), ((), ())), preferred_element_type=F32)


def gather(block, core, swap, shift, split):
    above, below = shift(block, -1), shift(block, 1)
    beside = swap(block)
    beside_above, beside_below = shift(beside, -1), shift(beside, 1)
    across = split(jnp.where(core == 0, below, above), 1)
    beside_across = split(jnp.where(core == 0, beside_below, beside_above), 1)
    return [block, beside, above, beside_above, below, beside_below, across, beside_across]


def gather_pairs(block, beside, core, shift, split):
    here = jnp.stack([block, beside])
    above, below = shift(here, -1), shift(here, 1)
    return [here, above, below, split(jnp.where(core == 0, below, above), 1)]


def place_of(v):
    row, col = v[0], v[1]
    return row, row >> 2, row & 3, col >> 2, (col >> 1) & 1, col & 1


def slot_of(step):
    step = step & 3
    return jnp.where(step >= 2, 5 - step, step)


def load(copies):
    for copy in copies:
        copy.start()
    for copy in copies:
        copy.wait()


def call(body, outs, scratch, loads, flops, here, vmem_args, any_args):
    vmem = pl.BlockSpec(memory_space=pltpu.VMEM)
    return pl.pallas_call(
        body,
        out_shape=outs,
        in_specs=[pl.BlockSpec(memory_space=pltpu.SMEM)]
        + [vmem] * len(vmem_args)
        + [pl.BlockSpec(memory_space=pl.ANY)] * len(any_args),
        out_specs=[vmem] * len(outs),
        scratch_shapes=[
            pltpu.VMEM(scratch, BF16),
            pltpu.SemaphoreType.DMA((len(any_args),)),
        ],
        compiler_params=pltpu.CompilerParams(vmem_limit_bytes=60 * 1024 * 1024),
        cost_estimate=pl.CostEstimate(flops=flops, bytes_accessed=loads, transcendentals=0),
    )(here, *vmem_args, *any_args)


def hid_kernel(here, conv_mine, conv_beside, *refs):
    blocks, outs, (held, sems) = refs[:8], refs[8:12], refs[12:]
    load(
        [
            pltpu.make_async_copy(
                ref,
                held.at[pl.ds((k % 4) * 2, 2), :, pl.ds((k // 4) * 512, 512)],
                sems.at[k],
            )
            for k, ref in enumerate(blocks)
        ]
    )
    row, y_lo, z, x, y_hi, core = place_of(here)
    ahead = 1 - 2 * core
    for out, step in zip(outs, (2, -ahead, ahead, 0)):
        for i in range(2):
            block = ((x + step) & 3) * 2 + (y_hi ^ i)
            slot = slot_of((block & 3) - z) * 2 + ((block >> 2) ^ y_lo)
            total = lax.dot_general(
                conv_mine[...], held[slot, :, :512], (((1,), (1,)), ((), ())),
                preferred_element_type=F32,
            ) + lax.dot_general(
                conv_beside[...], held[slot, :, 512:], (((1,), (1,)), ((), ())),
                preferred_element_type=F32,
            )
            out[i] = total.astype(BF16)


def hid_partial(here, conv_mine, conv_beside, blocks, beside):
    return call(
        hid_kernel, [jax.ShapeDtypeStruct((2, 768, 256), BF16)] * 4, (8, 256, 1024),
        9 << 20, 2 * 1536 * 512 * 2048, here, [conv_mine, conv_beside], [*blocks, *beside],
    )


def hidden_slot(block, x, y_hi):
    return slot_of((block >> 1) - x) * 2 + ((block & 1) ^ y_hi)


def wout_kernel(here, left, *refs):
    blocks, out, (held, sems) = refs[:8], refs[8], refs[9:]
    row, y_lo, z, x, y_hi, core = place_of(here)
    copies = []
    for k, ref in enumerate(blocks):
        at = core if k < 4 else 1 - core
        columns = pl.ds(pl.multiple_of(at * 128, 128), 128)
        slots = pl.ds((k % 4) * 2, 2)
        copies.append(pltpu.make_async_copy(ref, held.at[slots, :, columns], sems.at[k]))
    load(copies)
    for block in range(8):
        out[block] = jnp.dot(
            left[...], held[hidden_slot(block, x, y_hi)], preferred_element_type=F32
        ).astype(BF16)


def wout_partial(here, left, blocks, beside):
    return call(
        wout_kernel, [jax.ShapeDtypeStruct((8, 512, 256), BF16)], (8, 1536, 256),
        10 << 20, 2 * 1536 * 512 * 2048, here, [left], [*blocks, *beside],
    )[0]


def load_act(blocks, held, sems, core):
    copies = []
    for k, ref in enumerate(blocks):
        at = core if k < 8 else 1 - core
        rows = pl.ds(pl.multiple_of(at * 768, 768), 768)
        copies.append(pltpu.make_async_copy(ref, held.at[k % 8, rows, :], sems.at[k]))
    load(copies)


def win_kernel(here, left, *refs):
    blocks, outs, (held, sems) = refs[:16], refs[16:20], refs[20:]
    row, y_lo, z, x, y_hi, core = place_of(here)
    load_act(blocks, held, sems, core)
    ahead = 1 - 2 * core
    for out, step in zip(outs, (2, -ahead, ahead, 0)):
        for i in range(2):
            block = (y_lo ^ i) * 4 + ((z + step) & 3)
            out[i] = jnp.dot(
                left[...], held[hidden_slot(block, x, y_hi)], preferred_element_type=F32
            ).astype(BF16)


def win_partial(here, left, blocks, beside):
    return call(
        win_kernel, [jax.ShapeDtypeStruct((2, 512, 256), BF16)] * 4, (8, 1536, 256),
        10 << 20, 2 * 1536 * 512 * 2048, here, [left], [*blocks, *beside],
    )


def out_kernel(here, weights, cot, *refs):
    blocks, out, (held, sems) = refs[:16], refs[16], refs[17:]
    row, y_lo, z, x, y_hi, core = place_of(here)
    load_act(blocks, held, sems, core)
    for at in range(0, 1536, 256):
        total = cot[at : at + 256, :].astype(F32)
        for block in range(8):
            total = total + lax.dot_general(
                held[hidden_slot(block, x, y_hi), at : at + 256, :],
                weights[:, block * 256 : block * 256 + 256],
                (((1,), (1,)), ((), ())),
                preferred_element_type=F32,
            )
        out[at : at + 256, :] = total.astype(BF16)


def out_gradient(here, weights, cot, blocks, beside):
    return call(
        out_kernel, [jax.ShapeDtypeStruct((1536, 512), BF16)], (8, 1536, 256),
        12 << 20, 2 * 1536 * 512 * 2048, here, [weights, cot], [*blocks, *beside],
    )[0]


def reduce(away, there, onward, here, split):
    passed = split(away, 1)
    back = split(there, -1)
    onward = (onward.astype(F32) + passed.astype(F32)).astype(BF16)
    return here, back, split(onward, 1)


def add(terms):
    return sum(term.astype(F32) for term in terms)


def local(
    inputs,
    cotangent,
    conv_out,
    pre_act,
    weight_in,
    weight_out,
    scale_mid,
    scale_wide,
    keep_mid,
    keep_wide,
):
    rows = inputs.shape[0]
    half = rows // 2
    scaling = 1.0 / math.sqrt(rows * lax.axis_size("row"))
    row, col = lax.axis_index("row"), lax.axis_index("col")
    y_lo, z = row // 4, row % 4
    x, y_hi, core = col // 4, (col // 2) % 2, col % 2
    place = jnp.stack([row, col]).astype(jnp.int32)

    def mine(v):
        return lax.dynamic_slice_in_dim(v, core * half, half, 0)

    def theirs(v):
        return lax.dynamic_slice_in_dim(v, (1 - core) * half, half, 0)

    mid_gain = scale_mid * keep_mid.astype(F32)
    hidden = jnp.maximum(pre_act.astype(F32) * mid_gain, 0.0).astype(BF16)
    out_beside = y_lo_swap(weight_out)
    hid_beside = y_hi_swap(hidden)
    out_beside, cotangent, pre_act, inputs, conv_out = lax.optimization_barrier(
        (out_beside, cotangent, pre_act, inputs, conv_out)
    )
    out_blocks = gather_pairs(weight_out, out_beside, core, z_shift, z_split)
    hid = gather_pairs(hidden, hid_beside, core, x_shift, x_split)

    wide_gain = scale_wide * keep_wide.astype(F32)
    cot_float = cotangent.astype(F32)
    grad_conv = (cot_float * wide_gain).astype(BF16)
    wide_part = jnp.sum(cot_float * conv_out.astype(F32), axis=0)
    conv_mine = mine(grad_conv)
    conv_beside = core_swap(theirs(grad_conv))

    gain_pair = jnp.stack([scale_mid, keep_mid.astype(F32)])
    gain_beside = core_swap(gain_pair)
    pre_mine = mine(pre_act)
    pre_beside = core_swap(theirs(pre_act))

    def chip_order(a, b):
        return jnp.concatenate(
            [jnp.where(core == 0, a, b), jnp.where(core == 0, b, a)], axis=1
        )

    pre_chip = chip_order(pre_mine, pre_beside).astype(F32)
    gain_chip = chip_order(gain_pair, gain_beside)
    mid_gain = gain_chip[0] * gain_chip[1]

    out_beside = [core_swap(block) for block in out_blocks]
    input_turned, conv_turned = inputs.T, grad_conv.T
    out_beside[3], weight_in, hid[:3], input_turned, conv_turned = lax.optimization_barrier(
        (out_beside[3], weight_in, hid[:3], input_turned, conv_turned)
    )
    in_full = lax.all_gather(weight_in, "row", axis=1, tiled=True)
    hid_beside = [core_swap(block) for block in hid]
    wout = wout_partial(place, conv_turned, hid, hid_beside)
    partials = hid_partial(place, conv_mine, conv_beside, out_blocks, out_beside)
    terms = reduce(*partials, x_split)
    terms, wout, in_full = lax.optimization_barrier((terms, wout, in_full))
    wout = lax.psum_scatter(wout, "row", scatter_dimension=0, tiled=False)
    total = add(terms)
    grad_hid = total[0] + y_hi_swap(total[1].astype(BF16)).astype(F32)
    alive = (pre_chip > 0) & (gain_chip[1] > 0)[None, :]
    grad_pre = jnp.where(alive, grad_hid, 0.0)
    mid_part = jnp.sum(grad_pre * pre_chip, axis=0).reshape(2, 128)
    grad_act = (grad_pre * mid_gain).astype(BF16)
    act = gather(grad_act, core, y_hi_swap, x_shift, x_split)

    mid_own = lax.dynamic_index_in_dim(mid_part, core, 0, keepdims=False)
    mid_away = lax.dynamic_index_in_dim(mid_part, 1 - core, 0, keepdims=False)
    mid_own = mid_own + core_swap(mid_away)
    sums = jnp.concatenate([mid_own, wide_part]).reshape(5, 128)
    sums = sums + z_flip(sums, 1)
    sums = sums + z_flip(sums, 2)
    sums = sums + y_lo_swap(sums)
    grad_smid = keep_mid.astype(F32) * scaling * sums[0]
    grad_swide = keep_wide.astype(F32) * scaling * sums[1:].reshape(512)

    act_beside = [core_swap(block) for block in act]
    act[7], wout = lax.optimization_barrier((act[7], wout))
    win = win_partial(place, input_turned, act, act_beside)
    act[7], win = lax.optimization_barrier((act[7], win))
    terms = reduce(*win, z_split)
    grad_x = out_gradient(place, in_full, cotangent, act, act_beside)
    terms, grad_x = lax.optimization_barrier((terms, grad_x))
    total = add(terms)
    grad_win = (total[0] + y_lo_swap(total[1].astype(BF16)).astype(F32)) * scaling
    grad_wout = wout.astype(F32).T * scaling
    return (grad_x, grad_win, grad_wout, grad_smid, grad_swide)


def solution(mesh):
    return jax.shard_map(
        local,
        mesh=mesh,
        in_specs=(
            P("row", "col"),
            P("row", "col"),
            P("row", "col"),
            P("row", "col"),
            P("col", "row"),
            P("row", "col"),
            P("col"),
            P("col"),
            P("col"),
            P("col"),
        ),
        out_specs=(P("row", "col"), P("col", "row"), P("row", "col"), P("col"), P("col")),
        check_vma=False,
    )
```

```python
import functools
import math

import jax
import jax.numpy as jnp
from jax import lax
from jax.experimental import pallas as pl
from jax.experimental.pallas import tpu as pltpu
from jax.sharding import PartitionSpec as P

F32 = jnp.float32
BF16 = jnp.bfloat16
AXES = ("row", "col")
STEPS = (0, 1, 3, 2)


def permute(v, target):
    pairs = []
    for row in range(8):
        for col in range(16):
            y_lo, z, x, y_hi, core = target(
                row // 4, row % 4, col // 4, (col // 2) % 2, col % 2
            )
            pairs.append(
                (row * 16 + col, (y_lo * 4 + z % 4) * 16 + (x % 4) * 4 + y_hi * 2 + core)
            )
    return lax.ppermute(v, AXES, pairs)


def core_swap(v):
    return permute(v, lambda yl, z, x, yh, c: (yl, z, x, yh, 1 - c))


def y_hi_swap(v):
    return permute(v, lambda yl, z, x, yh, c: (yl, z, x, 1 - yh, c))


def y_lo_swap(v):
    return permute(v, lambda yl, z, x, yh, c: (1 - yl, z, x, yh, c))


def z_flip(v, mask):
    return permute(v, lambda yl, z, x, yh, c: (yl, z ^ mask, x, yh, c))


def x_shift(v, step):
    return permute(v, lambda yl, z, x, yh, c: (yl, z, x + step, yh, c))


def z_shift(v, step):
    return permute(v, lambda yl, z, x, yh, c: (yl, z + step, x, yh, c))


def x_split(v, way):
    return permute(v, lambda yl, z, x, yh, c: (yl, z, x + way * (1 - 2 * c), yh, c))


def z_split(v, way):
    return permute(v, lambda yl, z, x, yh, c: (yl, z + way * (1 - 2 * c), x, yh, c))


def dot(a, b, ca, cb):
    return lax.dot_general(a, b, (((ca,), (cb,)), ((), ())), preferred_element_type=F32)


def gather(block, core, swap, shift, split):
    above, below = shift(block, -1), shift(block, 1)
    beside = swap(block)
    beside_above, beside_below = shift(beside, -1), shift(beside, 1)
    across = onward(above, below, core, split)
    beside_across = onward(beside_above, beside_below, core, split)
    return [block, beside, above, beside_above, below, beside_below, across, beside_across]


def onward(above, below, core, split):
    return split(jnp.where(core == 0, below, above), 1)


def place_of(v):
    row, col = v[0], v[1]
    return row, row >> 2, row & 3, col >> 2, (col >> 1) & 1, col & 1


def slot_of(step):
    step = step & 3
    return jnp.where(step >= 2, 5 - step, step)


def load(copies):
    for copy in copies:
        copy.start()
    for copy in copies:
        copy.wait()


def call(body, outs, scratch, loads, flops, here, vmem_args, any_args):
    vmem = pl.BlockSpec(memory_space=pltpu.VMEM)
    return pl.pallas_call(
        body,
        out_shape=outs,
        in_specs=[pl.BlockSpec(memory_space=pltpu.SMEM)]
        + [vmem] * len(vmem_args)
        + [pl.BlockSpec(memory_space=pl.ANY)] * len(any_args),
        out_specs=[vmem] * len(outs),
        scratch_shapes=[
            pltpu.VMEM(scratch, BF16),
            pltpu.SemaphoreType.DMA((len(any_args),)),
        ],
        compiler_params=pltpu.CompilerParams(vmem_limit_bytes=60 * 1024 * 1024),
        cost_estimate=pl.CostEstimate(flops=flops, bytes_accessed=loads, transcendentals=0),
    )(here, *vmem_args, *any_args)


def hid_kernel(ways, here, conv_mine, conv_beside, *refs):
    blocks, outs, (held, sems) = refs[:8], refs[8:10], refs[10:]
    load(
        [
            pltpu.make_async_copy(
                ref,
                held.at[pl.ds((k % 4) * 2, 2), :, pl.ds((k // 4) * 512, 512)],
                sems.at[k],
            )
            for k, ref in enumerate(blocks)
        ]
    )
    row, y_lo, z, x, y_hi, core = place_of(here)
    ahead = 1 - 2 * core
    for out, (fixed, way) in zip(outs, ways):
        step = fixed + way * ahead
        for i in range(2):
            block = ((x + step) & 3) * 2 + (y_hi ^ i)
            slot = slot_of((block & 3) - z) * 2 + ((block >> 2) ^ y_lo)
            total = lax.dot_general(
                conv_mine[...], held[slot, :, :512], (((1,), (1,)), ((), ())),
                preferred_element_type=F32,
            ) + lax.dot_general(
                conv_beside[...], held[slot, :, 512:], (((1,), (1,)), ((), ())),
                preferred_element_type=F32,
            )
            out[i] = total.astype(BF16)


def hid_partial(here, conv_mine, conv_beside, blocks, beside, ways):
    return call(
        functools.partial(hid_kernel, ways), [jax.ShapeDtypeStruct((2, 768, 256), BF16)] * 2,
        (8, 256, 1024), 7 << 20, 1536 * 512 * 2048, here, [conv_mine, conv_beside],
        [*blocks, *beside],
    )


def hidden_slot(block, x, y_hi):
    return slot_of((block >> 1) - x) * 2 + ((block & 1) ^ y_hi)


def load_hid(blocks, held, sems, core):
    copies = []
    for k, ref in enumerate(blocks):
        at = core if k < 8 else 1 - core
        columns = pl.ds(pl.multiple_of(at * 128, 128), 128)
        copies.append(pltpu.make_async_copy(ref, held.at[k % 8, :, columns], sems.at[k]))
    load(copies)


def load_act(blocks, held, sems, core):
    copies = []
    for k, ref in enumerate(blocks):
        at = core if k < 8 else 1 - core
        rows = pl.ds(pl.multiple_of(at * 768, 768), 768)
        copies.append(pltpu.make_async_copy(ref, held.at[k % 8, rows, :], sems.at[k]))
    load(copies)


def weight_kernel(load_blocks, here, left, *refs):
    blocks, outs, (held, sems) = refs[:16], refs[16:20], refs[20:]
    row, y_lo, z, x, y_hi, core = place_of(here)
    load_blocks(blocks, held, sems, core)
    ahead = 1 - 2 * core
    for out, step in zip(outs, (2, -ahead, ahead, 0)):
        for i in range(2):
            block = (y_lo ^ i) * 4 + ((z + step) & 3)
            out[i] = jnp.dot(
                left[...], held[hidden_slot(block, x, y_hi)], preferred_element_type=F32
            ).astype(BF16)


def weight_partial(load_blocks, here, left, blocks, beside):
    return call(
        functools.partial(weight_kernel, load_blocks), [jax.ShapeDtypeStruct((2, 512, 256), BF16)] * 4, (8, 1536, 256),
        10 << 20, 2 * 1536 * 512 * 2048, here, [left], [*blocks, *beside],
    )


def out_kernel(here, weights, cot, *refs):
    blocks, out, (held, sems) = refs[:16], refs[16], refs[17:]
    row, y_lo, z, x, y_hi, core = place_of(here)
    load_act(blocks, held, sems, core)
    for at in range(0, 1536, 256):
        total = cot[at : at + 256, :].astype(F32)
        for block in range(8):
            total = total + lax.dot_general(
                held[hidden_slot(block, x, y_hi), at : at + 256, :],
                weights[:, block * 256 : block * 256 + 256],
                (((1,), (1,)), ((), ())),
                preferred_element_type=F32,
            )
        out[at : at + 256, :] = total.astype(BF16)


def out_gradient(here, weights, cot, blocks, beside):
    return call(
        out_kernel, [jax.ShapeDtypeStruct((1536, 512), BF16)], (8, 1536, 256),
        12 << 20, 2 * 1536 * 512 * 2048, here, [weights, cot], [*blocks, *beside],
    )[0]


def tie(*values):
    return lax.optimization_barrier(values)


def add(terms):
    return sum(term.astype(F32) for term in terms)


def local(
    inputs,
    cotangent,
    conv_out,
    pre_act,
    weight_in,
    weight_out,
    scale_mid,
    scale_wide,
    keep_mid,
    keep_wide,
):
    rows = inputs.shape[0]
    half = rows // 2
    scaling = 1.0 / math.sqrt(rows * lax.axis_size("row"))
    row, col = lax.axis_index("row"), lax.axis_index("col")
    y_lo, z = row // 4, row % 4
    x, y_hi, core = col // 4, (col // 2) % 2, col % 2
    place = jnp.stack([row, col]).astype(jnp.int32)

    def mine(v):
        return lax.dynamic_slice_in_dim(v, core * half, half, 0)

    def theirs(v):
        return lax.dynamic_slice_in_dim(v, (1 - core) * half, half, 0)

    mid_gain = scale_mid * keep_mid.astype(F32)
    hidden = jnp.maximum(pre_act.astype(F32) * mid_gain, 0.0).astype(BF16)
    out_beside = y_lo_swap(weight_out)
    hid_above, hid_below = x_shift(hidden, -1), x_shift(hidden, 1)
    out_beside, hidden, cotangent, pre_act, inputs, conv_out = tie(
        out_beside, hidden, cotangent, pre_act, inputs, conv_out
    )
    hid_near = y_hi_swap(hidden)
    out_here = jnp.stack([weight_out, out_beside])
    out_above, out_below = z_shift(out_here, -1), z_shift(out_here, 1)
    out_above, hid_above, hid_below = tie(out_above, hid_above, hid_below)
    out_across = onward(out_above, out_below, core, z_split)
    out_blocks = [out_here, out_above, out_below, out_across]
    hid_across = onward(hid_above, hid_below, core, x_split)
    hid = [hidden, hid_near, hid_above, y_hi_swap(hid_above)]
    hid += [hid_below, y_hi_swap(hid_below), hid_across, y_hi_swap(hid_across)]

    wide_gain = scale_wide * keep_wide.astype(F32)
    cot_float = cotangent.astype(F32)
    grad_conv = (cot_float * wide_gain).astype(BF16)
    wide_part = jnp.sum(cot_float * conv_out.astype(F32), axis=0)
    conv_mine = mine(grad_conv)
    conv_beside = core_swap(theirs(grad_conv))

    gain_pair = jnp.stack([scale_mid, keep_mid.astype(F32)])
    gain_beside = core_swap(gain_pair)
    pre_mine = mine(pre_act)
    pre_beside = core_swap(theirs(pre_act))

    def chip_order(a, b):
        return jnp.concatenate(
            [jnp.where(core == 0, a, b), jnp.where(core == 0, b, a)], axis=1
        )

    pre_chip = chip_order(pre_mine, pre_beside).astype(F32)
    gain_chip = chip_order(gain_pair, gain_beside)
    mid_gain = gain_chip[0] * gain_chip[1]

    out_beside = [core_swap(block) for block in out_blocks]
    input_turned, conv_turned = inputs.T, grad_conv.T
    out_beside[3], weight_in, hid[1], hid[6], input_turned, conv_turned = tie(
        out_beside[3], weight_in, hid[1], hid[6], input_turned, conv_turned
    )
    in_full = lax.all_gather(weight_in, "row", axis=1, tiled=True)
    hid_beside = [core_swap(block) for block in hid]
    away, there = hid_partial(
        place, conv_mine, conv_beside, out_blocks, out_beside, ((2, 0), (0, -1))
    )
    passed, back = x_split(away, 1), x_split(there, -1)
    further, own = hid_partial(
        place, conv_mine, conv_beside, out_blocks, out_beside, ((0, 1), (0, 0))
    )
    passed, own = tie(passed, own)
    further = x_split(add([further, passed]).astype(BF16), 1)
    wout = weight_partial(load_hid, place, conv_turned, hid, hid_beside)
    further, wout, in_full = tie(further, wout, in_full)
    terms = [own, back, further]
    wout_back, wout_passed = z_split(wout[1], -1), z_split(wout[0], 1)
    total = add(terms)
    grad_hid = total[0] + y_hi_swap(total[1].astype(BF16)).astype(F32)
    alive = (pre_chip > 0) & (gain_chip[1] > 0)[None, :]
    grad_pre = jnp.where(alive, grad_hid, 0.0)
    mid_part = jnp.sum(grad_pre * pre_chip, axis=0).reshape(2, 128)
    grad_act = (grad_pre * mid_gain).astype(BF16)
    act = gather(grad_act, core, y_hi_swap, x_shift, x_split)

    mid_own = lax.dynamic_index_in_dim(mid_part, core, 0, keepdims=False)
    mid_away = lax.dynamic_index_in_dim(mid_part, 1 - core, 0, keepdims=False)
    mid_own = mid_own + core_swap(mid_away)
    sums = jnp.concatenate([mid_own, wide_part]).reshape(5, 128)
    sums = sums + z_flip(sums, 1)
    sums = sums + z_flip(sums, 2)
    sums = sums + y_lo_swap(sums)
    act_beside = [core_swap(block) for block in act]
    wout_onward = z_split(add([wout[2], wout_passed]).astype(BF16), 1)
    wout_total = add([wout[3], wout_back, wout_onward])
    wout_away = y_lo_swap(wout_total[1].astype(BF16))
    act[7], wout_total, sums = tie(act[7], wout_total, sums)
    win = weight_partial(load_act, place, input_turned, act, act_beside)
    passed, back = z_split(win[0], 1), z_split(win[1], -1)
    grad_x = out_gradient(place, in_full, cotangent, act, act_beside)
    passed, grad_x = tie(passed, grad_x)
    total = add([win[3], back, z_split(add([win[2], passed]).astype(BF16), 1)])
    grad_win = add([total[0], y_lo_swap(total[1].astype(BF16))]) * scaling
    grad_wout = add([wout_total[0], wout_away]).T * scaling
    grad_smid = keep_mid.astype(F32) * scaling * sums[0]
    grad_swide = keep_wide.astype(F32) * scaling * sums[1:].reshape(512)
    return (grad_x, grad_win, grad_wout, grad_smid, grad_swide)


def solution(mesh):
    return jax.shard_map(
        local,
        mesh=mesh,
        in_specs=(
            P("row", "col"),
            P("row", "col"),
            P("row", "col"),
            P("row", "col"),
            P("col", "row"),
            P("row", "col"),
            P("col"),
            P("col"),
            P("col"),
            P("col"),
        ),
        out_specs=(P("row", "col"), P("col", "row"), P("row", "col"), P("col"), P("col")),
        check_vma=False,
    )
```

```python
import functools
import math

import jax
import jax.numpy as jnp
from jax import lax
from jax.experimental import pallas as pl
from jax.experimental.pallas import tpu as pltpu
from jax.sharding import PartitionSpec as P

F32 = jnp.float32
BF16 = jnp.bfloat16
AXES = ("row", "col")
STEPS = (0, 1, 3, 2)


def permute(v, target):
    pairs = []
    for row in range(8):
        for col in range(16):
            y_lo, z, x, y_hi, core = target(
                row // 4, row % 4, col // 4, (col // 2) % 2, col % 2
            )
            pairs.append(
                (row * 16 + col, (y_lo * 4 + z % 4) * 16 + (x % 4) * 4 + y_hi * 2 + core)
            )
    return lax.ppermute(v, AXES, pairs)


def core_swap(v):
    return permute(v, lambda yl, z, x, yh, c: (yl, z, x, yh, 1 - c))


def y_hi_swap(v):
    return permute(v, lambda yl, z, x, yh, c: (yl, z, x, 1 - yh, c))


def y_lo_swap(v):
    return permute(v, lambda yl, z, x, yh, c: (1 - yl, z, x, yh, c))


def z_flip(v, mask):
    return permute(v, lambda yl, z, x, yh, c: (yl, z ^ mask, x, yh, c))


def x_shift(v, step):
    return permute(v, lambda yl, z, x, yh, c: (yl, z, x + step, yh, c))


def z_shift(v, step):
    return permute(v, lambda yl, z, x, yh, c: (yl, z + step, x, yh, c))


def x_split(v, way):
    return permute(v, lambda yl, z, x, yh, c: (yl, z, x + way * (1 - 2 * c), yh, c))


def z_split(v, way):
    return permute(v, lambda yl, z, x, yh, c: (yl, z + way * (1 - 2 * c), x, yh, c))


def dot(a, b, ca, cb):
    return lax.dot_general(a, b, (((ca,), (cb,)), ((), ())), preferred_element_type=F32)


def onward(above, below, core, split):
    return split(jnp.where(core == 0, below, above), 1)


def place_of(v):
    row, col = v[0], v[1]
    return row, row >> 2, row & 3, col >> 2, (col >> 1) & 1, col & 1


def slot_of(step):
    step = step & 3
    return jnp.where(step >= 2, 5 - step, step)


def load(copies):
    for copy in copies:
        copy.start()
    for copy in copies:
        copy.wait()


def call(body, outs, scratch, loads, flops, here, vmem_args, any_args):
    vmem = pl.BlockSpec(memory_space=pltpu.VMEM)
    return pl.pallas_call(
        body,
        out_shape=outs,
        in_specs=[pl.BlockSpec(memory_space=pltpu.SMEM)]
        + [vmem] * len(vmem_args)
        + [pl.BlockSpec(memory_space=pl.ANY)] * len(any_args),
        out_specs=[vmem] * len(outs),
        scratch_shapes=[*scratch, pltpu.SemaphoreType.DMA((len(any_args),))],
        compiler_params=pltpu.CompilerParams(vmem_limit_bytes=60 * 1024 * 1024),
        cost_estimate=pl.CostEstimate(flops=flops, bytes_accessed=loads, transcendentals=0),
    )(here, *vmem_args, *any_args)


def hid_kernel(ways, here, conv_mine, conv_beside, *refs):
    blocks, outs, (held, sems) = refs[:8], refs[8:10], refs[10:]
    load(
        [
            pltpu.make_async_copy(
                ref,
                held.at[pl.ds((k % 4) * 2, 2), :, pl.ds((k // 4) * 512, 512)],
                sems.at[k],
            )
            for k, ref in enumerate(blocks)
        ]
    )
    row, y_lo, z, x, y_hi, core = place_of(here)
    ahead = 1 - 2 * core
    for out, (fixed, way) in zip(outs, ways):
        step = fixed + way * ahead
        for i in range(2):
            block = ((x + step) & 3) * 2 + (y_hi ^ i)
            slot = row_slot(block, y_lo, z)
            total = lax.dot_general(
                conv_mine[...], held[slot, :, :512], (((1,), (1,)), ((), ())),
                preferred_element_type=F32,
            ) + lax.dot_general(
                conv_beside[...], held[slot, :, 512:], (((1,), (1,)), ((), ())),
                preferred_element_type=F32,
            )
            out[i] = total.astype(BF16)


def hid_partial(here, conv_mine, conv_beside, blocks, beside, ways):
    return call(
        functools.partial(hid_kernel, ways), [jax.ShapeDtypeStruct((2, 768, 256), BF16)] * 2,
        [pltpu.VMEM((8, 256, 1024), BF16)], 7 << 20, 1536 * 512 * 2048, here, [conv_mine, conv_beside],
        [*blocks, *beside],
    )


def row_slot(block, y_lo, z):
    return slot_of((block & 3) - z) * 2 + ((block >> 2) ^ y_lo)


def hidden_slot(block, x, y_hi):
    return slot_of((block >> 1) - x) * 2 + ((block & 1) ^ y_hi)


def load_act(blocks, held, sems, core):
    copies = []
    for k, ref in enumerate(blocks):
        at = core if k < 8 else 1 - core
        rows = pl.ds(pl.multiple_of(at * 768, 768), 768)
        copies.append(pltpu.make_async_copy(ref, held.at[k % 8, rows, :], sems.at[k]))
    load(copies)


def win_kernel(here, left, *refs):
    blocks, outs, (held, sems) = refs[:16], refs[16:20], refs[20:]
    row, y_lo, z, x, y_hi, core = place_of(here)
    load_act(blocks, held, sems, core)
    ahead = 1 - 2 * core
    for out, step in zip(outs, (2, -ahead, ahead, 0)):
        for i in range(2):
            block = (y_lo ^ i) * 4 + ((z + step) & 3)
            out[i] = jnp.dot(
                left[...], held[hidden_slot(block, x, y_hi)], preferred_element_type=F32
            ).astype(BF16)


def win_partial(here, left, blocks, beside):
    return call(
        win_kernel, [jax.ShapeDtypeStruct((2, 512, 256), BF16)] * 4,
        [pltpu.VMEM((8, 1536, 256), BF16)], 10 << 20, 2 * 1536 * 512 * 2048, here, [left],
        [*blocks, *beside],
    )


def out_kernel(here, cot, *refs):
    blocks, parts, out = refs[:16], refs[16:20], refs[20]
    held, weights, sems = refs[21:]
    row, y_lo, z, x, y_hi, core = place_of(here)
    load(
        [
            pltpu.make_async_copy(ref, weights.at[pl.ds(k * 2, 2)], sems.at[16 + k])
            for k, ref in enumerate(parts)
        ]
    )
    load_act(blocks, held, sems, core)
    for at in range(0, 1536, 512):
        total = cot[at : at + 512, :].astype(F32)
        for block in range(8):
            total = total + lax.dot_general(
                held[hidden_slot(block, x, y_hi), at : at + 512, :],
                weights[row_slot(block, y_lo, z)],
                (((1,), (1,)), ((), ())),
                preferred_element_type=F32,
            )
        out[at : at + 512, :] = total.astype(BF16)


def out_gradient(here, cot, blocks, beside, weights):
    return call(
        out_kernel, [jax.ShapeDtypeStruct((1536, 512), BF16)],
        [pltpu.VMEM((8, 1536, 256), BF16), pltpu.VMEM((8, 512, 256), BF16)], 12 << 20,
        2 * 1536 * 512 * 2048, here, [cot], [*blocks, *beside, *weights],
    )[0]


def tie(*values):
    return lax.optimization_barrier(values)


def add(terms):
    return sum(term.astype(F32) for term in terms)


def local(
    inputs,
    cotangent,
    conv_out,
    pre_act,
    weight_in,
    weight_out,
    scale_mid,
    scale_wide,
    keep_mid,
    keep_wide,
):
    rows = inputs.shape[0]
    half = rows // 2
    scaling = 1.0 / math.sqrt(rows * lax.axis_size("row"))
    row, col = lax.axis_index("row"), lax.axis_index("col")
    y_lo, z = row // 4, row % 4
    x, y_hi, core = col // 4, (col // 2) % 2, col % 2
    place = jnp.stack([row, col]).astype(jnp.int32)

    def mine(v):
        return lax.dynamic_slice_in_dim(v, core * half, half, 0)

    def theirs(v):
        return lax.dynamic_slice_in_dim(v, (1 - core) * half, half, 0)

    mid_gain = scale_mid * keep_mid.astype(F32)
    hidden = jnp.maximum(pre_act.astype(F32) * mid_gain, 0.0).astype(BF16)
    hidden_full = lax.all_gather(hidden, "col", axis=1, tiled=True)
    out_near = y_lo_swap(weight_out)
    out_near, cotangent, pre_act, inputs, conv_out = tie(
        out_near, cotangent, pre_act, inputs, conv_out
    )
    out_here = jnp.stack([weight_out, out_near])
    out_above, out_below = z_shift(out_here, -1), z_shift(out_here, 1)
    out_blocks = [out_here, out_above, out_below, onward(out_above, out_below, core, z_split)]

    wide_gain = scale_wide * keep_wide.astype(F32)
    cot_float = cotangent.astype(F32)
    grad_conv = (cot_float * wide_gain).astype(BF16)
    wide_part = jnp.sum(cot_float * conv_out.astype(F32), axis=0)
    conv_mine = mine(grad_conv)
    conv_beside = core_swap(theirs(grad_conv))

    gain_pair = jnp.stack([scale_mid, keep_mid.astype(F32)])
    gain_beside = core_swap(gain_pair)
    pre_mine = mine(pre_act)
    pre_beside = core_swap(theirs(pre_act))

    def chip_order(a, b):
        return jnp.concatenate(
            [jnp.where(core == 0, a, b), jnp.where(core == 0, b, a)], axis=1
        )

    pre_chip = chip_order(pre_mine, pre_beside).astype(F32)
    gain_chip = chip_order(gain_pair, gain_beside)
    mid_gain = gain_chip[0] * gain_chip[1]

    out_beside = [core_swap(block) for block in out_blocks]
    input_turned = inputs.T
    out_beside[3], weight_in, input_turned = tie(out_beside[3], weight_in, input_turned)
    in_near = y_lo_swap(weight_in)
    away, there = hid_partial(
        place, conv_mine, conv_beside, out_blocks, out_beside, ((2, 0), (0, -1))
    )
    passed, back = x_split(away, 1), x_split(there, -1)
    further, own = hid_partial(
        place, conv_mine, conv_beside, out_blocks, out_beside, ((0, 1), (0, 0))
    )
    passed, own, in_near = tie(passed, own, in_near)
    in_here = jnp.stack([weight_in, in_near])
    in_above, in_below = z_shift(in_here, -1), z_shift(in_here, 1)
    further = x_split(add([further, passed]).astype(BF16), 1)
    terms = [own, back, further]
    total = add(terms)
    grad_hid = total[0] + y_hi_swap(total[1].astype(BF16)).astype(F32)
    alive = (pre_chip > 0) & (gain_chip[1] > 0)[None, :]
    grad_pre = jnp.where(alive, grad_hid, 0.0)
    mid_part = jnp.sum(grad_pre * pre_chip, axis=0).reshape(2, 128)
    grad_act = (grad_pre * mid_gain).astype(BF16)
    grad_act, in_above, in_below = tie(grad_act, in_above, in_below)
    act_near = y_hi_swap(grad_act)
    act_above, act_below = x_shift(grad_act, -1), x_shift(grad_act, 1)
    in_blocks = [in_here, in_above, in_below, onward(in_above, in_below, core, z_split)]
    wout = dot(hidden_full, grad_conv, 0, 0).astype(BF16)
    act_above, wout = tie(act_above, wout)
    wout = lax.psum_scatter(wout, "row", scatter_dimension=0, tiled=True)
    near_above, near_below = x_shift(act_near, -1), x_shift(act_near, 1)
    act_across = onward(act_above, act_below, core, x_split)
    near_across = onward(near_above, near_below, core, x_split)
    act = [
        grad_act, act_near, act_above, near_above, act_below, near_below, act_across, near_across
    ]

    mid_own = lax.dynamic_index_in_dim(mid_part, core, 0, keepdims=False)
    mid_away = lax.dynamic_index_in_dim(mid_part, 1 - core, 0, keepdims=False)
    mid_own = mid_own + core_swap(mid_away)
    sums = jnp.concatenate([mid_own, wide_part]).reshape(5, 128)
    sums = jnp.sum(lax.all_gather(sums, "row", axis=0), axis=0)

    act_beside = [core_swap(block) for block in act]
    act[7], sums = tie(act[7], sums)
    win = win_partial(place, input_turned, act, act_beside)
    passed, back = z_split(win[0], 1), z_split(win[1], -1)
    grad_x = out_gradient(place, cotangent, act, act_beside, in_blocks)
    passed, grad_x = tie(passed, grad_x)
    total = add([win[3], back, z_split(add([win[2], passed]).astype(BF16), 1)])
    grad_win = add([total[0], y_lo_swap(total[1].astype(BF16))]) * scaling
    grad_wout = wout.astype(F32) * scaling
    grad_smid = keep_mid.astype(F32) * scaling * sums[0]
    grad_swide = keep_wide.astype(F32) * scaling * sums[1:].reshape(512)
    return (grad_x, grad_win, grad_wout, grad_smid, grad_swide)


def solution(mesh):
    return jax.shard_map(
        local,
        mesh=mesh,
        in_specs=(
            P("row", "col"),
            P("row", "col"),
            P("row", "col"),
            P("row", "col"),
            P("col", "row"),
            P("row", "col"),
            P("col"),
            P("col"),
            P("col"),
            P("col"),
        ),
        out_specs=(P("row", "col"), P("col", "row"), P("row", "col"), P("col"), P("col")),
        check_vma=False,
    )
```

```python
import functools
import math

import jax
import jax.numpy as jnp
from jax import lax
from jax.experimental import pallas as pl
from jax.experimental.pallas import tpu as pltpu
from jax.sharding import PartitionSpec as P

F32 = jnp.float32
BF16 = jnp.bfloat16
AXES = ("row", "col")
STEPS = (0, 1, 3, 2)


def permute(v, target):
    pairs = []
    for row in range(8):
        for col in range(16):
            y_lo, z, x, y_hi, core = target(
                row // 4, row % 4, col // 4, (col // 2) % 2, col % 2
            )
            pairs.append(
                (row * 16 + col, (y_lo * 4 + z % 4) * 16 + (x % 4) * 4 + y_hi * 2 + core)
            )
    return lax.ppermute(v, AXES, pairs)


def core_swap(v):
    return permute(v, lambda yl, z, x, yh, c: (yl, z, x, yh, 1 - c))


def y_hi_swap(v):
    return permute(v, lambda yl, z, x, yh, c: (yl, z, x, 1 - yh, c))


def y_lo_swap(v):
    return permute(v, lambda yl, z, x, yh, c: (1 - yl, z, x, yh, c))


def z_flip(v, mask):
    return permute(v, lambda yl, z, x, yh, c: (yl, z ^ mask, x, yh, c))


def x_shift(v, step):
    return permute(v, lambda yl, z, x, yh, c: (yl, z, x + step, yh, c))


def z_shift(v, step):
    return permute(v, lambda yl, z, x, yh, c: (yl, z + step, x, yh, c))


def x_split(v, way):
    return permute(v, lambda yl, z, x, yh, c: (yl, z, x + way * (1 - 2 * c), yh, c))


def z_split(v, way):
    return permute(v, lambda yl, z, x, yh, c: (yl, z + way * (1 - 2 * c), x, yh, c))


def dot(a, b, ca, cb):
    return lax.dot_general(a, b, (((ca,), (cb,)), ((), ())), preferred_element_type=F32)


def onward(above, below, core, split):
    return split(jnp.where(core == 0, below, above), 1)


def place_of(v):
    row, col = v[0], v[1]
    return row, row >> 2, row & 3, col >> 2, (col >> 1) & 1, col & 1


def slot_of(step):
    step = step & 3
    return jnp.where(step >= 2, 5 - step, step)


def load(copies):
    for copy in copies:
        copy.start()
    for copy in copies:
        copy.wait()


def call(body, outs, scratch, loads, flops, here, vmem_args, any_args):
    vmem = pl.BlockSpec(memory_space=pltpu.VMEM)
    return pl.pallas_call(
        body,
        out_shape=outs,
        in_specs=[pl.BlockSpec(memory_space=pltpu.SMEM)]
        + [vmem] * len(vmem_args)
        + [pl.BlockSpec(memory_space=pl.ANY)] * len(any_args),
        out_specs=[vmem] * len(outs),
        scratch_shapes=[*scratch, pltpu.SemaphoreType.DMA((len(any_args),))],
        compiler_params=pltpu.CompilerParams(vmem_limit_bytes=60 * 1024 * 1024),
        cost_estimate=pl.CostEstimate(flops=flops, bytes_accessed=loads, transcendentals=0),
    )(here, *vmem_args, *any_args)


def hid_kernel(ways, here, conv_mine, conv_beside, *refs):
    blocks, outs, (held, sems) = refs[:8], refs[8:10], refs[10:]
    load(
        [
            pltpu.make_async_copy(
                ref,
                held.at[pl.ds((k % 4) * 2, 2), :, pl.ds((k // 4) * 512, 512)],
                sems.at[k],
            )
            for k, ref in enumerate(blocks)
        ]
    )
    row, y_lo, z, x, y_hi, core = place_of(here)
    ahead = 1 - 2 * core
    for out, (fixed, way) in zip(outs, ways):
        step = fixed + way * ahead
        for i in range(2):
            block = ((x + step) & 3) * 2 + (y_hi ^ i)
            slot = row_slot(block, y_lo, z)
            total = lax.dot_general(
                conv_mine[...], held[slot, :, :512], (((1,), (1,)), ((), ())),
                preferred_element_type=F32,
            ) + lax.dot_general(
                conv_beside[...], held[slot, :, 512:], (((1,), (1,)), ((), ())),
                preferred_element_type=F32,
            )
            out[i] = total.astype(BF16)


def hid_partial(here, conv_mine, conv_beside, blocks, beside, ways):
    return call(
        functools.partial(hid_kernel, ways), [jax.ShapeDtypeStruct((2, 768, 256), BF16)] * 2,
        [pltpu.VMEM((8, 256, 1024), BF16)], 7 << 20, 1536 * 512 * 2048, here, [conv_mine, conv_beside],
        [*blocks, *beside],
    )


def row_slot(block, y_lo, z):
    return slot_of((block & 3) - z) * 2 + ((block >> 2) ^ y_lo)


def hidden_slot(block, x, y_hi):
    return slot_of((block >> 1) - x) * 2 + ((block & 1) ^ y_hi)


def load_act(blocks, held, sems, core):
    copies = []
    for k, ref in enumerate(blocks):
        at = core if k < 8 else 1 - core
        rows = pl.ds(pl.multiple_of(at * 768, 768), 768)
        copies.append(pltpu.make_async_copy(ref, held.at[k % 8, rows, :], sems.at[k]))
    load(copies)


def win_kernel(here, left, *refs):
    blocks, outs, (held, sems) = refs[:16], refs[16:20], refs[20:]
    row, y_lo, z, x, y_hi, core = place_of(here)
    load_act(blocks, held, sems, core)
    ahead = 1 - 2 * core
    for out, step in zip(outs, (2, -ahead, ahead, 0)):
        for i in range(2):
            block = (y_lo ^ i) * 4 + ((z + step) & 3)
            out[i] = jnp.dot(
                left[...], held[hidden_slot(block, x, y_hi)], preferred_element_type=F32
            ).astype(BF16)


def win_partial(here, left, blocks, beside):
    return call(
        win_kernel, [jax.ShapeDtypeStruct((2, 512, 256), BF16)] * 4,
        [pltpu.VMEM((8, 1536, 256), BF16)], 10 << 20, 2 * 1536 * 512 * 2048, here, [left],
        [*blocks, *beside],
    )


def out_kernel(here, cot, *refs):
    blocks, parts, out = refs[:16], refs[16:20], refs[20]
    held, weights, sems = refs[21:]
    row, y_lo, z, x, y_hi, core = place_of(here)
    load(
        [
            pltpu.make_async_copy(ref, weights.at[pl.ds(k * 2, 2)], sems.at[16 + k])
            for k, ref in enumerate(parts)
        ]
    )
    load_act(blocks, held, sems, core)
    for at in range(0, 1536, 512):
        total = cot[at : at + 512, :].astype(F32)
        for block in range(8):
            total = total + lax.dot_general(
                held[hidden_slot(block, x, y_hi), at : at + 512, :],
                weights[row_slot(block, y_lo, z)],
                (((1,), (1,)), ((), ())),
                preferred_element_type=F32,
            )
        out[at : at + 512, :] = total.astype(BF16)


def out_gradient(here, cot, blocks, beside, weights):
    return call(
        out_kernel, [jax.ShapeDtypeStruct((1536, 512), BF16)],
        [pltpu.VMEM((8, 1536, 256), BF16), pltpu.VMEM((8, 512, 256), BF16)], 12 << 20,
        2 * 1536 * 512 * 2048, here, [cot], [*blocks, *beside, *weights],
    )[0]


def tie(*values):
    return lax.optimization_barrier(values)


def add(terms):
    return sum(term.astype(F32) for term in terms)


def local(
    inputs,
    cotangent,
    conv_out,
    pre_act,
    weight_in,
    weight_out,
    scale_mid,
    scale_wide,
    keep_mid,
    keep_wide,
):
    rows = inputs.shape[0]
    half = rows // 2
    scaling = 1.0 / math.sqrt(rows * lax.axis_size("row"))
    row, col = lax.axis_index("row"), lax.axis_index("col")
    y_lo, z = row // 4, row % 4
    x, y_hi, core = col // 4, (col // 2) % 2, col % 2
    place = jnp.stack([row, col]).astype(jnp.int32)

    def mine(v):
        return lax.dynamic_slice_in_dim(v, core * half, half, 0)

    def theirs(v):
        return lax.dynamic_slice_in_dim(v, (1 - core) * half, half, 0)

    mid_gain = scale_mid * keep_mid.astype(F32)
    hidden = jnp.maximum(pre_act.astype(F32) * mid_gain, 0.0).astype(BF16)
    hidden_full = lax.all_gather(hidden, "col", axis=1, tiled=True)
    out_near = y_lo_swap(weight_out)
    out_near, cotangent, pre_act, inputs, conv_out = tie(
        out_near, cotangent, pre_act, inputs, conv_out
    )
    out_here = jnp.stack([weight_out, out_near])
    out_above, out_below = z_shift(out_here, -1), z_shift(out_here, 1)
    out_blocks = [out_here, out_above, out_below, onward(out_above, out_below, core, z_split)]

    wide_gain = scale_wide * keep_wide.astype(F32)
    cot_float = cotangent.astype(F32)
    grad_conv = (cot_float * wide_gain).astype(BF16)
    wide_part = jnp.sum(cot_float * conv_out.astype(F32), axis=0)
    conv_mine = mine(grad_conv)
    conv_beside = core_swap(theirs(grad_conv))

    gain_pair = jnp.stack([scale_mid, keep_mid.astype(F32)])
    gain_beside = core_swap(gain_pair)
    pre_mine = mine(pre_act)
    pre_beside = core_swap(theirs(pre_act))

    def chip_order(a, b):
        return jnp.concatenate(
            [jnp.where(core == 0, a, b), jnp.where(core == 0, b, a)], axis=1
        )

    pre_chip = chip_order(pre_mine, pre_beside).astype(F32)
    gain_chip = chip_order(gain_pair, gain_beside)
    mid_gain = gain_chip[0] * gain_chip[1]

    out_beside = [core_swap(block) for block in out_blocks]
    input_turned = inputs.T
    out_beside[3], weight_in, input_turned = tie(out_beside[3], weight_in, input_turned)
    in_near = y_lo_swap(weight_in)
    away, there = hid_partial(
        place, conv_mine, conv_beside, out_blocks, out_beside, ((2, 0), (0, -1))
    )
    passed, back = x_split(away, 1), x_split(there, -1)
    further, own = hid_partial(
        place, conv_mine, conv_beside, out_blocks, out_beside, ((0, 1), (0, 0))
    )
    passed, own, in_near = tie(passed, own, in_near)
    in_here = jnp.stack([weight_in, in_near])
    in_above, in_below = z_shift(in_here, -1), z_shift(in_here, 1)
    further = x_split(add([further, passed]).astype(BF16), 1)
    further, hidden_full = tie(further, hidden_full)
    terms = [own, back, further]
    total = add(terms)
    grad_hid = total[0] + y_hi_swap(total[1].astype(BF16)).astype(F32)
    alive = (pre_chip > 0) & (gain_chip[1] > 0)[None, :]
    grad_pre = jnp.where(alive, grad_hid, 0.0)
    mid_part = jnp.sum(grad_pre * pre_chip, axis=0).reshape(2, 128)
    grad_act = (grad_pre * mid_gain).astype(BF16)
    grad_act, in_above, in_below = tie(grad_act, in_above, in_below)
    act_near = y_hi_swap(grad_act)
    act_above, act_below = x_shift(grad_act, -1), x_shift(grad_act, 1)
    in_blocks = [in_here, in_above, in_below, onward(in_above, in_below, core, z_split)]
    wout = dot(hidden_full, grad_conv, 0, 0).astype(BF16)
    act_above, wout = tie(act_above, wout)
    wout = lax.psum_scatter(wout, "row", scatter_dimension=0, tiled=True)
    near_above, near_below = x_shift(act_near, -1), x_shift(act_near, 1)
    act_across = onward(act_above, act_below, core, x_split)
    near_across = onward(near_above, near_below, core, x_split)
    act = [
        grad_act, act_near, act_above, near_above, act_below, near_below, act_across, near_across
    ]

    mid_own = lax.dynamic_index_in_dim(mid_part, core, 0, keepdims=False)
    mid_away = lax.dynamic_index_in_dim(mid_part, 1 - core, 0, keepdims=False)
    mid_own = mid_own + core_swap(mid_away)
    sums = jnp.concatenate([mid_own, wide_part]).reshape(5, 128)
    sums = sums + z_flip(sums, 1)
    sums = sums + z_flip(sums, 2)
    sums = sums + y_lo_swap(sums)

    act_beside = [core_swap(block) for block in act]
    act[7], sums = tie(act[7], sums)
    win = win_partial(place, input_turned, act, act_beside)
    passed, back = z_split(win[0], 1), z_split(win[1], -1)
    grad_x = out_gradient(place, cotangent, act, act_beside, in_blocks)
    passed, grad_x = tie(passed, grad_x)
    total = add([win[3], back, z_split(add([win[2], passed]).astype(BF16), 1)])
    grad_win = add([total[0], y_lo_swap(total[1].astype(BF16))]) * scaling
    grad_wout = wout.astype(F32) * scaling
    grad_smid = keep_mid.astype(F32) * scaling * sums[0]
    grad_swide = keep_wide.astype(F32) * scaling * sums[1:].reshape(512)
    return (grad_x, grad_win, grad_wout, grad_smid, grad_swide)


def solution(mesh):
    return jax.shard_map(
        local,
        mesh=mesh,
        in_specs=(
            P("row", "col"),
            P("row", "col"),
            P("row", "col"),
            P("row", "col"),
            P("col", "row"),
            P("row", "col"),
            P("col"),
            P("col"),
            P("col"),
            P("col"),
        ),
        out_specs=(P("row", "col"), P("col", "row"), P("row", "col"), P("col"), P("col")),
        check_vma=False,
    )
```

```python
import functools
import math

import jax
import jax.numpy as jnp
from jax import lax
from jax.experimental import pallas as pl
from jax.experimental.pallas import tpu as pltpu
from jax.sharding import PartitionSpec as P

F32 = jnp.float32
BF16 = jnp.bfloat16
AXES = ("row", "col")
STEPS = (0, 1, 3, 2)


def permute(v, target):
    pairs = []
    for row in range(8):
        for col in range(16):
            y_lo, z, x, y_hi, core = target(
                row // 4, row % 4, col // 4, (col // 2) % 2, col % 2
            )
            pairs.append(
                (row * 16 + col, (y_lo * 4 + z % 4) * 16 + (x % 4) * 4 + y_hi * 2 + core)
            )
    return lax.ppermute(v, AXES, pairs)


def core_swap(v):
    return permute(v, lambda yl, z, x, yh, c: (yl, z, x, yh, 1 - c))


def y_hi_swap(v):
    return permute(v, lambda yl, z, x, yh, c: (yl, z, x, 1 - yh, c))


def y_lo_swap(v):
    return permute(v, lambda yl, z, x, yh, c: (1 - yl, z, x, yh, c))


def z_flip(v, mask):
    return permute(v, lambda yl, z, x, yh, c: (yl, z ^ mask, x, yh, c))


def x_shift(v, step):
    return permute(v, lambda yl, z, x, yh, c: (yl, z, x + step, yh, c))


def z_shift(v, step):
    return permute(v, lambda yl, z, x, yh, c: (yl, z + step, x, yh, c))


def x_split(v, way):
    return permute(v, lambda yl, z, x, yh, c: (yl, z, x + way * (1 - 2 * c), yh, c))


def z_split(v, way):
    return permute(v, lambda yl, z, x, yh, c: (yl, z + way * (1 - 2 * c), x, yh, c))


def dot(a, b, ca, cb):
    return lax.dot_general(a, b, (((ca,), (cb,)), ((), ())), preferred_element_type=F32)


def onward(above, below, core, split):
    return split(jnp.where(core == 0, below, above), 1)


def place_of(v):
    row, col = v[0], v[1]
    return row, row >> 2, row & 3, col >> 2, (col >> 1) & 1, col & 1


def slot_of(step):
    step = step & 3
    return jnp.where(step >= 2, 5 - step, step)


def call(body, outs, scratch, loads, flops, here, vmem_args, any_args):
    vmem = pl.BlockSpec(memory_space=pltpu.VMEM)
    return pl.pallas_call(
        body,
        out_shape=outs,
        in_specs=[pl.BlockSpec(memory_space=pltpu.SMEM)]
        + [vmem] * len(vmem_args)
        + [pl.BlockSpec(memory_space=pl.ANY)] * len(any_args),
        out_specs=[vmem] * len(outs),
        scratch_shapes=[*scratch, pltpu.SemaphoreType.DMA((len(any_args),))],
        compiler_params=pltpu.CompilerParams(vmem_limit_bytes=60 * 1024 * 1024),
        cost_estimate=pl.CostEstimate(flops=flops, bytes_accessed=loads, transcendentals=0),
    )(here, *vmem_args, *any_args)


def row_slot(block, y_lo, z):
    return slot_of((block & 3) - z) * 2 + ((block >> 2) ^ y_lo)


def hidden_slot(block, x, y_hi):
    return slot_of((block >> 1) - x) * 2 + ((block & 1) ^ y_hi)


def fetch(copy_of, slots):
    if len(slots) == 2:
        for j, slot in enumerate(slots):
            for k in range(8):

                @pl.when(slot == k)
                def _(j=j, k=k):
                    copy_of(k, 0, j).start()
                    copy_of(k, 1, j).start()

        def ready(j):
            copy_of(0, 0, j).wait()
            copy_of(0, 1, j).wait()
            return j
    else:
        for k in range(8):
            copy_of(k, 0, k).start()
            copy_of(k, 1, k).start()

        def ready(j):
            copy_of(0, 0, slots[j]).wait()
            copy_of(0, 1, slots[j]).wait()
            return slots[j]
    return ready


def hid_kernel(ways, here, conv_mine, conv_beside, *refs):
    count = len(ways)
    blocks, outs, (held, sems) = refs[:16], refs[16 : 16 + count], refs[16 + count :]
    row, y_lo, z, x, y_hi, core = place_of(here)
    ahead = 1 - 2 * core
    steps = [fixed + way * ahead for fixed, way in ways] + [2] * (count - 1)
    slots = [
        row_slot(((x + step) & 3) * 2 + (y_hi ^ i), y_lo, z)
        for step in steps[: 4 if count > 1 else 1]
        for i in range(2)
    ]

    def copy_of(k, part, at):
        return pltpu.make_async_copy(
            blocks[part * 8 + k], held.at[at, :, pl.ds(part * 512, 512)], sems.at[at * 2 + part]
        )

    ready = fetch(copy_of, slots)
    for j in range(len(slots)):
        at = ready(j)
        if j < 2 * count:
            total = lax.dot_general(
                conv_mine[...], held[at, :, :512], (((1,), (1,)), ((), ())),
                preferred_element_type=F32,
            ) + lax.dot_general(
                conv_beside[...], held[at, :, 512:], (((1,), (1,)), ((), ())),
                preferred_element_type=F32,
            )
            outs[j // 2][j % 2] = total.astype(BF16)


def hid_partial(here, conv_mine, conv_beside, blocks, beside, ways):
    return call(
        functools.partial(hid_kernel, ways),
        [jax.ShapeDtypeStruct((2, 768, 256), BF16)] * len(ways),
        [pltpu.VMEM((8, 256, 1024), BF16)], len(ways) * 2 << 20, len(ways) * 768 * 512 * 2048,
        here, [conv_mine, conv_beside], [*blocks, *beside],
    )


def act_copy(blocks, held, sems, core):
    def copy_of(k, part, at):
        rows = pl.ds(pl.multiple_of((core ^ part) * 768, 768), 768)
        return pltpu.make_async_copy(
            blocks[part * 8 + k], held.at[at, rows, :], sems.at[at * 2 + part]
        )

    return copy_of


def win_kernel(ways, here, left, *refs):
    count = len(ways)
    blocks, outs, (held, sems) = refs[:16], refs[16 : 16 + count], refs[16 + count :]
    row, y_lo, z, x, y_hi, core = place_of(here)
    ahead = 1 - 2 * core
    steps = [fixed + way * ahead for fixed, way in ways] + [2] * (count - 1)
    slots = [
        hidden_slot((y_lo ^ i) * 4 + ((z + step) & 3), x, y_hi)
        for step in steps[: 4 if count > 1 else 1]
        for i in range(2)
    ]
    ready = fetch(act_copy(blocks, held, sems, core), slots)
    for j in range(len(slots)):
        at = ready(j)
        if j < 2 * count:
            outs[j // 2][j % 2] = jnp.dot(
                left[...], held[at], preferred_element_type=F32
            ).astype(BF16)


def win_partial(here, left, blocks, beside, ways):
    return call(
        functools.partial(win_kernel, ways),
        [jax.ShapeDtypeStruct((2, 512, 256), BF16)] * len(ways),
        [pltpu.VMEM((8, 1536, 256), BF16)], len(ways) * 3 << 20, len(ways) * 768 * 512 * 2048,
        here, [left], [*blocks, *beside],
    )


def out_kernel(here, cot, *refs):
    blocks, parts, out = refs[:16], refs[16:20], refs[20]
    held, weights, sems = refs[21:]
    row, y_lo, z, x, y_hi, core = place_of(here)
    copy_of = act_copy(blocks, held, sems, core)
    copies = [
        pltpu.make_async_copy(ref, weights.at[pl.ds(k * 2, 2)], sems.at[16 + k])
        for k, ref in enumerate(parts)
    ]
    copies += [copy_of(k, part, k) for k in range(8) for part in range(2)]
    for copy in copies:
        copy.start()
    for copy in copies:
        copy.wait()
    for at in range(0, 1536, 256):
        total = cot[at : at + 256, :].astype(F32)
        for block in range(8):
            total = total + lax.dot_general(
                held[hidden_slot(block, x, y_hi), at : at + 256, :],
                weights[row_slot(block, y_lo, z)],
                (((1,), (1,)), ((), ())),
                preferred_element_type=F32,
            )
        out[at : at + 256, :] = total.astype(BF16)


def out_gradient(here, cot, blocks, beside, weights):
    return call(
        out_kernel, [jax.ShapeDtypeStruct((1536, 512), BF16)],
        [pltpu.VMEM((8, 1536, 256), BF16), pltpu.VMEM((8, 512, 256), BF16)], 12 << 20,
        2 * 1536 * 512 * 2048, here, [cot], [*blocks, *beside, *weights],
    )[0]


def tie(*values):
    return lax.optimization_barrier(values)


def add(terms):
    return sum(term.astype(F32) for term in terms)


def local(
    inputs,
    cotangent,
    conv_out,
    pre_act,
    weight_in,
    weight_out,
    scale_mid,
    scale_wide,
    keep_mid,
    keep_wide,
):
    rows = inputs.shape[0]
    half = rows // 2
    scaling = 1.0 / math.sqrt(rows * lax.axis_size("row"))
    row, col = lax.axis_index("row"), lax.axis_index("col")
    y_lo, z = row // 4, row % 4
    x, y_hi, core = col // 4, (col // 2) % 2, col % 2
    place = jnp.stack([row, col]).astype(jnp.int32)

    def mine(v):
        return lax.dynamic_slice_in_dim(v, core * half, half, 0)

    def theirs(v):
        return lax.dynamic_slice_in_dim(v, (1 - core) * half, half, 0)

    mid_gain = scale_mid * keep_mid.astype(F32)
    hidden = jnp.maximum(pre_act.astype(F32) * mid_gain, 0.0).astype(BF16)
    hidden_full = lax.all_gather(hidden, "col", axis=1, tiled=True)
    out_above, out_below = z_shift(weight_out, -1), z_shift(weight_out, 1)
    out_near = y_lo_swap(weight_out)
    out_near, cotangent, pre_act, inputs, conv_out = tie(
        out_near, cotangent, pre_act, inputs, conv_out
    )
    near_above, near_below = z_shift(out_near, -1), z_shift(out_near, 1)
    out_across = onward(out_above, out_below, core, z_split)

    wide_gain = scale_wide * keep_wide.astype(F32)
    cot_float = cotangent.astype(F32)
    grad_conv = (cot_float * wide_gain).astype(BF16)
    wide_part = jnp.sum(cot_float * conv_out.astype(F32), axis=0)
    conv_mine = mine(grad_conv)
    conv_beside = core_swap(theirs(grad_conv))

    input_turned = inputs.T
    near_above, conv_beside, input_turned, wide_part = tie(
        near_above, conv_beside, input_turned, wide_part
    )
    near_across = onward(near_above, near_below, core, z_split)
    out_blocks = [
        weight_out, out_near, out_above, near_above, out_below, near_below, out_across, near_across
    ]

    gain_pair = jnp.stack([scale_mid, keep_mid.astype(F32)])
    gain_beside = core_swap(gain_pair)
    pre_mine = mine(pre_act)
    pre_beside = core_swap(theirs(pre_act))

    def chip_order(a, b):
        return jnp.concatenate(
            [jnp.where(core == 0, a, b), jnp.where(core == 0, b, a)], axis=1
        )

    pre_chip = chip_order(pre_mine, pre_beside).astype(F32)
    gain_chip = chip_order(gain_pair, gain_beside)
    mid_gain = gain_chip[0] * gain_chip[1]

    out_beside = [core_swap(block) for block in out_blocks]
    near_across, weight_in = tie(near_across, weight_in)
    out_blocks[7] = near_across
    in_near = y_lo_swap(weight_in)
    (away,) = hid_partial(place, conv_mine, conv_beside, out_blocks, out_beside, ((2, 0),))
    passed = x_split(away, 1)
    there, further, own = hid_partial(
        place, conv_mine, conv_beside, out_blocks, out_beside, ((0, -1), (0, 1), (0, 0))
    )
    back = x_split(there, -1)
    passed, own, in_near = tie(passed, own, in_near)
    in_here = jnp.stack([weight_in, in_near])
    in_above, in_below = z_shift(in_here, -1), z_shift(in_here, 1)
    further = x_split(add([further, passed]).astype(BF16), 1)
    further, hidden_full = tie(further, hidden_full)
    terms = [own, back, further]
    total = add(terms)
    wout = dot(hidden_full, grad_conv, 0, 0).astype(BF16)
    crossed, wout = tie(y_hi_swap(total[1].astype(BF16)), wout)
    wout = lax.psum_scatter(wout, "row", scatter_dimension=0, tiled=True)
    grad_hid = add([total[0], crossed])
    alive = (pre_chip > 0) & (gain_chip[1] > 0)[None, :]
    grad_pre = jnp.where(alive, grad_hid, 0.0)
    mid_part = jnp.sum(grad_pre * pre_chip, axis=0).reshape(2, 128)
    grad_act = (grad_pre * mid_gain).astype(BF16)
    grad_act, in_above, in_below = tie(grad_act, in_above, in_below)
    act_near = y_hi_swap(grad_act)
    act_above, act_below = x_shift(grad_act, -1), x_shift(grad_act, 1)
    in_blocks = [in_here, in_above, in_below, onward(in_above, in_below, core, z_split)]
    near_above, near_below = x_shift(act_near, -1), x_shift(act_near, 1)
    act_across = onward(act_above, act_below, core, x_split)
    near_across = onward(near_above, near_below, core, x_split)
    act = [
        grad_act, act_near, act_above, near_above, act_below, near_below, act_across, near_across
    ]

    mid_own = lax.dynamic_index_in_dim(mid_part, core, 0, keepdims=False)
    mid_away = lax.dynamic_index_in_dim(mid_part, 1 - core, 0, keepdims=False)
    mid_own = mid_own + core_swap(mid_away)
    sums = jnp.concatenate([mid_own, wide_part]).reshape(5, 128)
    sums = sums + z_flip(sums, 1)
    sums = sums + z_flip(sums, 2)
    sums = sums + y_lo_swap(sums)

    act_beside = [core_swap(block) for block in act]
    act[7], sums = tie(act[7], sums)
    (away,) = win_partial(place, input_turned, act, act_beside, ((2, 0),))
    passed = z_split(away, 1)
    there, further, own = win_partial(
        place, input_turned, act, act_beside, ((0, -1), (0, 1), (0, 0))
    )
    back = z_split(there, -1)
    passed, own = tie(passed, own)
    further = z_split(add([further, passed]).astype(BF16), 1)
    grad_x = out_gradient(place, cotangent, act, act_beside, in_blocks)
    back, grad_x, wout = tie(back, grad_x, wout)
    total = add([own, back, further])
    grad_win = add([total[0], y_lo_swap(total[1].astype(BF16))]) * scaling
    grad_wout = wout.astype(F32) * scaling
    grad_smid = keep_mid.astype(F32) * scaling * sums[0]
    grad_swide = keep_wide.astype(F32) * scaling * sums[1:].reshape(512)
    return (grad_x, grad_win, grad_wout, grad_smid, grad_swide)


def solution(mesh):
    return jax.shard_map(
        local,
        mesh=mesh,
        in_specs=(
            P("row", "col"),
            P("row", "col"),
            P("row", "col"),
            P("row", "col"),
            P("col", "row"),
            P("row", "col"),
            P("col"),
            P("col"),
            P("col"),
            P("col"),
        ),
        out_specs=(P("row", "col"), P("col", "row"), P("row", "col"), P("col"), P("col")),
        check_vma=False,
    )
```

```python
import functools
import math

import jax
import jax.numpy as jnp
from jax import lax
from jax.experimental import pallas as pl
from jax.experimental.pallas import tpu as pltpu
from jax.sharding import PartitionSpec as P

F32 = jnp.float32
BF16 = jnp.bfloat16
AXES = ("row", "col")
STEPS = (0, 1, 3, 2)


def permute(v, target):
    pairs = []
    for row in range(8):
        for col in range(16):
            y_lo, z, x, y_hi, core = target(
                row // 4, row % 4, col // 4, (col // 2) % 2, col % 2
            )
            pairs.append(
                (row * 16 + col, (y_lo * 4 + z % 4) * 16 + (x % 4) * 4 + y_hi * 2 + core)
            )
    return lax.ppermute(v, AXES, pairs)


def core_swap(v):
    return permute(v, lambda yl, z, x, yh, c: (yl, z, x, yh, 1 - c))


def y_hi_swap(v):
    return permute(v, lambda yl, z, x, yh, c: (yl, z, x, 1 - yh, c))


def y_lo_swap(v):
    return permute(v, lambda yl, z, x, yh, c: (1 - yl, z, x, yh, c))


def z_flip(v, mask):
    return permute(v, lambda yl, z, x, yh, c: (yl, z ^ mask, x, yh, c))


def x_shift(v, step):
    return permute(v, lambda yl, z, x, yh, c: (yl, z, x + step, yh, c))


def z_shift(v, step):
    return permute(v, lambda yl, z, x, yh, c: (yl, z + step, x, yh, c))


def x_split(v, way):
    return permute(v, lambda yl, z, x, yh, c: (yl, z, x + way * (1 - 2 * c), yh, c))


def z_split(v, way):
    return permute(v, lambda yl, z, x, yh, c: (yl, z + way * (1 - 2 * c), x, yh, c))


def dot(a, b, ca, cb):
    return lax.dot_general(a, b, (((ca,), (cb,)), ((), ())), preferred_element_type=F32)


def onward(above, below, core, split):
    return split(jnp.where(core == 0, below, above), 1)


def place_of(v):
    row, col = v[0], v[1]
    return row, row >> 2, row & 3, col >> 2, (col >> 1) & 1, col & 1


def slot_of(step):
    step = step & 3
    return jnp.where(step >= 2, 5 - step, step)


def load(copies):
    for copy in copies:
        copy.start()
    for copy in copies:
        copy.wait()


def call(body, outs, scratch, loads, flops, here, vmem_args, any_args):
    vmem = pl.BlockSpec(memory_space=pltpu.VMEM)
    return pl.pallas_call(
        body,
        out_shape=outs,
        in_specs=[pl.BlockSpec(memory_space=pltpu.SMEM)]
        + [vmem] * len(vmem_args)
        + [pl.BlockSpec(memory_space=pl.ANY)] * len(any_args),
        out_specs=[vmem] * len(outs),
        scratch_shapes=[*scratch, pltpu.SemaphoreType.DMA((len(any_args),))],
        compiler_params=pltpu.CompilerParams(vmem_limit_bytes=60 * 1024 * 1024),
        cost_estimate=pl.CostEstimate(flops=flops, bytes_accessed=loads, transcendentals=0),
    )(here, *vmem_args, *any_args)


def hid_kernel(ways, here, conv_mine, conv_beside, *refs):
    blocks, outs, (held, sems) = refs[:8], refs[8:10], refs[10:]
    load(
        [
            pltpu.make_async_copy(
                ref,
                held.at[pl.ds((k % 4) * 2, 2), :, pl.ds((k // 4) * 512, 512)],
                sems.at[k],
            )
            for k, ref in enumerate(blocks)
        ]
    )
    row, y_lo, z, x, y_hi, core = place_of(here)
    ahead = 1 - 2 * core
    for out, (fixed, way) in zip(outs, ways):
        step = fixed + way * ahead
        for i in range(2):
            block = ((x + step) & 3) * 2 + (y_hi ^ i)
            slot = row_slot(block, y_lo, z)
            total = lax.dot_general(
                conv_mine[...], held[slot, :, :512], (((1,), (1,)), ((), ())),
                preferred_element_type=F32,
            ) + lax.dot_general(
                conv_beside[...], held[slot, :, 512:], (((1,), (1,)), ((), ())),
                preferred_element_type=F32,
            )
            out[i] = total.astype(BF16)


def hid_partial(here, conv_mine, conv_beside, blocks, beside, ways):
    return call(
        functools.partial(hid_kernel, ways), [jax.ShapeDtypeStruct((2, 768, 256), BF16)] * 2,
        [pltpu.VMEM((8, 256, 1024), BF16)], 7 << 20, 1536 * 512 * 2048, here, [conv_mine, conv_beside],
        [*blocks, *beside],
    )


def row_slot(block, y_lo, z):
    return slot_of((block & 3) - z) * 2 + ((block >> 2) ^ y_lo)


def hidden_slot(block, x, y_hi):
    return slot_of((block >> 1) - x) * 2 + ((block & 1) ^ y_hi)


def load_act(blocks, held, sems, core):
    copies = []
    for k, ref in enumerate(blocks):
        at = core if k < 8 else 1 - core
        rows = pl.ds(pl.multiple_of(at * 768, 768), 768)
        copies.append(pltpu.make_async_copy(ref, held.at[k % 8, rows, :], sems.at[k]))
    load(copies)


def win_kernel(ways, here, left, *refs):
    blocks, outs, (held, sems) = refs[:16], refs[16:18], refs[18:]
    row, y_lo, z, x, y_hi, core = place_of(here)
    load_act(blocks, held, sems, core)
    ahead = 1 - 2 * core
    for out, (fixed, way) in zip(outs, ways):
        step = fixed + way * ahead
        for i in range(2):
            block = (y_lo ^ i) * 4 + ((z + step) & 3)
            out[i] = jnp.dot(
                left[...], held[hidden_slot(block, x, y_hi)], preferred_element_type=F32
            ).astype(BF16)


def win_partial(here, left, blocks, beside, ways):
    return call(
        functools.partial(win_kernel, ways), [jax.ShapeDtypeStruct((2, 512, 256), BF16)] * 2,
        [pltpu.VMEM((8, 1536, 256), BF16)], 9 << 20, 1536 * 512 * 2048, here, [left],
        [*blocks, *beside],
    )


def out_kernel(here, cot, *refs):
    blocks, parts, out = refs[:16], refs[16:20], refs[20]
    held, weights, sems = refs[21:]
    row, y_lo, z, x, y_hi, core = place_of(here)
    load(
        [
            pltpu.make_async_copy(ref, weights.at[pl.ds(k * 2, 2)], sems.at[16 + k])
            for k, ref in enumerate(parts)
        ]
    )
    load_act(blocks, held, sems, core)
    for at in range(0, 1536, 256):
        total = cot[at : at + 256, :].astype(F32)
        for block in range(8):
            total = total + lax.dot_general(
                held[hidden_slot(block, x, y_hi), at : at + 256, :],
                weights[row_slot(block, y_lo, z)],
                (((1,), (1,)), ((), ())),
                preferred_element_type=F32,
            )
        out[at : at + 256, :] = total.astype(BF16)


def out_gradient(here, cot, blocks, beside, weights):
    return call(
        out_kernel, [jax.ShapeDtypeStruct((1536, 512), BF16)],
        [pltpu.VMEM((8, 1536, 256), BF16), pltpu.VMEM((8, 512, 256), BF16)], 12 << 20,
        2 * 1536 * 512 * 2048, here, [cot], [*blocks, *beside, *weights],
    )[0]


def tie(*values):
    return lax.optimization_barrier(values)


def add(terms):
    return sum(term.astype(F32) for term in terms)


def local(
    inputs,
    cotangent,
    conv_out,
    pre_act,
    weight_in,
    weight_out,
    scale_mid,
    scale_wide,
    keep_mid,
    keep_wide,
):
    rows = inputs.shape[0]
    half = rows // 2
    scaling = 1.0 / math.sqrt(rows * lax.axis_size("row"))
    row, col = lax.axis_index("row"), lax.axis_index("col")
    y_lo, z = row // 4, row % 4
    x, y_hi, core = col // 4, (col // 2) % 2, col % 2
    place = jnp.stack([row, col]).astype(jnp.int32)

    def mine(v):
        return lax.dynamic_slice_in_dim(v, core * half, half, 0)

    def theirs(v):
        return lax.dynamic_slice_in_dim(v, (1 - core) * half, half, 0)

    mid_gain = scale_mid * keep_mid.astype(F32)
    hidden = jnp.maximum(pre_act.astype(F32) * mid_gain, 0.0).astype(BF16)
    hidden_full = lax.all_gather(hidden, "col", axis=1, tiled=True)
    out_near = y_lo_swap(weight_out)
    out_near, cotangent, pre_act, inputs, conv_out = tie(
        out_near, cotangent, pre_act, inputs, conv_out
    )
    out_here = jnp.stack([weight_out, out_near])
    out_above, out_below = z_shift(out_here, -1), z_shift(out_here, 1)

    wide_gain = scale_wide * keep_wide.astype(F32)
    cot_float = cotangent.astype(F32)
    grad_conv = (cot_float * wide_gain).astype(BF16)
    wide_part = jnp.sum(cot_float * conv_out.astype(F32), axis=0)
    conv_mine = mine(grad_conv)
    conv_beside = core_swap(theirs(grad_conv))

    input_turned = inputs.T
    out_above, conv_beside, input_turned, wide_part = tie(
        out_above, conv_beside, input_turned, wide_part
    )
    out_blocks = [out_here, out_above, out_below, onward(out_above, out_below, core, z_split)]

    gain_pair = jnp.stack([scale_mid, keep_mid.astype(F32)])
    gain_beside = core_swap(gain_pair)
    pre_mine = mine(pre_act)
    pre_beside = core_swap(theirs(pre_act))

    def chip_order(a, b):
        return jnp.concatenate(
            [jnp.where(core == 0, a, b), jnp.where(core == 0, b, a)], axis=1
        )

    pre_chip = chip_order(pre_mine, pre_beside).astype(F32)
    gain_chip = chip_order(gain_pair, gain_beside)
    mid_gain = gain_chip[0] * gain_chip[1]

    out_beside = [core_swap(block) for block in out_blocks]
    out_beside[3], weight_in = tie(out_beside[3], weight_in)
    in_near = y_lo_swap(weight_in)
    away, there = hid_partial(
        place, conv_mine, conv_beside, out_blocks, out_beside, ((2, 0), (0, -1))
    )
    passed, back = x_split(away, 1), x_split(there, -1)
    away, in_near = tie(away, in_near)
    in_here = jnp.stack([weight_in, in_near])
    in_above, in_below = z_shift(in_here, -1), z_shift(in_here, 1)
    further, own = hid_partial(
        place, conv_mine, conv_beside, out_blocks, out_beside, ((0, 1), (0, 0))
    )
    passed, own, in_above, in_below = tie(passed, own, in_above, in_below)
    further = x_split(add([further, passed]).astype(BF16), 1)
    in_across = onward(in_above, in_below, core, z_split)
    further, hidden_full, in_across = tie(further, hidden_full, in_across)
    in_blocks = [in_here, in_above, in_below, in_across]
    terms = [own, back, further]
    total = add(terms)
    wout = dot(hidden_full, grad_conv, 0, 0).astype(BF16)
    crossed, wout = tie(y_hi_swap(total[1].astype(BF16)), wout)
    wout = lax.psum_scatter(wout, "row", scatter_dimension=0, tiled=True)
    grad_hid = add([total[0], crossed])
    alive = (pre_chip > 0) & (gain_chip[1] > 0)[None, :]
    grad_pre = jnp.where(alive, grad_hid, 0.0)
    mid_part = jnp.sum(grad_pre * pre_chip, axis=0).reshape(2, 128)
    grad_act = (grad_pre * mid_gain).astype(BF16)
    act_near = y_hi_swap(grad_act)
    act_above, act_below = x_shift(grad_act, -1), x_shift(grad_act, 1)
    near_above, near_below = x_shift(act_near, -1), x_shift(act_near, 1)
    act_across = onward(act_above, act_below, core, x_split)
    near_across = onward(near_above, near_below, core, x_split)
    act = [
        grad_act, act_near, act_above, near_above, act_below, near_below, act_across, near_across
    ]

    mid_own = lax.dynamic_index_in_dim(mid_part, core, 0, keepdims=False)
    mid_away = lax.dynamic_index_in_dim(mid_part, 1 - core, 0, keepdims=False)
    mid_own = mid_own + core_swap(mid_away)
    sums = jnp.concatenate([mid_own, wide_part]).reshape(5, 128)
    sums = sums + z_flip(sums, 1)
    sums = sums + z_flip(sums, 2)
    sums = sums + y_lo_swap(sums)

    act_beside = [core_swap(block) for block in act]
    act[7], sums = tie(act[7], sums)
    away, there = win_partial(place, input_turned, act, act_beside, ((2, 0), (0, -1)))
    passed, back = z_split(away, 1), z_split(there, -1)
    further, own = win_partial(place, input_turned, act, act_beside, ((0, 1), (0, 0)))
    passed, own = tie(passed, own)
    further = z_split(add([further, passed]).astype(BF16), 1)
    grad_x = out_gradient(place, cotangent, act, act_beside, in_blocks)
    further, grad_x = tie(further, grad_x)
    total = add([own, back, further])
    grad_win = add([total[0], y_lo_swap(total[1].astype(BF16))]) * scaling
    grad_wout = wout.astype(F32) * scaling
    grad_smid = keep_mid.astype(F32) * scaling * sums[0]
    grad_swide = keep_wide.astype(F32) * scaling * sums[1:].reshape(512)
    return (grad_x, grad_win, grad_wout, grad_smid, grad_swide)


def solution(mesh):
    return jax.shard_map(
        local,
        mesh=mesh,
        in_specs=(
            P("row", "col"),
            P("row", "col"),
            P("row", "col"),
            P("row", "col"),
            P("col", "row"),
            P("row", "col"),
            P("col"),
            P("col"),
            P("col"),
            P("col"),
        ),
        out_specs=(P("row", "col"), P("col", "row"), P("row", "col"), P("col"), P("col")),
        check_vma=False,
    )
```

```python
import functools
import math

import jax
import jax.numpy as jnp
from jax import lax
from jax.experimental import pallas as pl
from jax.experimental.pallas import tpu as pltpu
from jax.sharding import PartitionSpec as P

F32 = jnp.float32
BF16 = jnp.bfloat16
AXES = ("row", "col")
STEPS = (0, 1, 3, 2)


def permute(v, target):
    pairs = []
    for row in range(8):
        for col in range(16):
            y_lo, z, x, y_hi, core = target(
                row // 4, row % 4, col // 4, (col // 2) % 2, col % 2
            )
            pairs.append(
                (row * 16 + col, (y_lo * 4 + z % 4) * 16 + (x % 4) * 4 + y_hi * 2 + core)
            )
    return lax.ppermute(v, AXES, pairs)


def core_swap(v):
    return permute(v, lambda yl, z, x, yh, c: (yl, z, x, yh, 1 - c))


def y_hi_swap(v):
    return permute(v, lambda yl, z, x, yh, c: (yl, z, x, 1 - yh, c))


def y_lo_swap(v):
    return permute(v, lambda yl, z, x, yh, c: (1 - yl, z, x, yh, c))


def z_flip(v, mask):
    return permute(v, lambda yl, z, x, yh, c: (yl, z ^ mask, x, yh, c))


def x_shift(v, step):
    return permute(v, lambda yl, z, x, yh, c: (yl, z, x + step, yh, c))


def z_shift(v, step):
    return permute(v, lambda yl, z, x, yh, c: (yl, z + step, x, yh, c))


def x_split(v, way):
    return permute(v, lambda yl, z, x, yh, c: (yl, z, x + way * (1 - 2 * c), yh, c))


def z_split(v, way):
    return permute(v, lambda yl, z, x, yh, c: (yl, z + way * (1 - 2 * c), x, yh, c))


def dot(a, b, ca, cb):
    return lax.dot_general(a, b, (((ca,), (cb,)), ((), ())), preferred_element_type=F32)


def onward(above, below, core, split):
    return split(jnp.where(core == 0, below, above), 1)


def place_of(v):
    row, col = v[0], v[1]
    return row, row >> 2, row & 3, col >> 2, (col >> 1) & 1, col & 1


def slot_of(step):
    step = step & 3
    return jnp.where(step >= 2, 5 - step, step)


def row_slot(block, y_lo, z):
    return slot_of((block & 3) - z) * 2 + ((block >> 2) ^ y_lo)


def hidden_slot(block, x, y_hi):
    return slot_of((block >> 1) - x) * 2 + ((block & 1) ^ y_hi)


def call(body, outs, out_space, scratch, sems, loads, flops, here, vmem_args, any_args):
    vmem = pl.BlockSpec(memory_space=pltpu.VMEM)
    return pl.pallas_call(
        body,
        out_shape=outs,
        in_specs=[pl.BlockSpec(memory_space=pltpu.SMEM)]
        + [vmem] * len(vmem_args)
        + [pl.BlockSpec(memory_space=pl.ANY)] * len(any_args),
        out_specs=[pl.BlockSpec(memory_space=out_space)] * len(outs),
        scratch_shapes=[*scratch, pltpu.SemaphoreType.DMA((sems,))],
        compiler_params=pltpu.CompilerParams(vmem_limit_bytes=60 * 1024 * 1024),
        cost_estimate=pl.CostEstimate(flops=flops, bytes_accessed=loads, transcendentals=0),
    )(here, *vmem_args, *any_args)


def send_out(whole, slots, outs, sems, first):
    copies = [
        pltpu.make_async_copy(whole.at[slot], out, sems.at[first + j])
        for j, (slot, out) in enumerate(zip(slots, outs))
    ]
    for copy in copies:
        copy.start()
    for copy in copies:
        copy.wait()


def hid_copies(own, beside, held, k, sems):
    return [
        pltpu.make_async_copy(own, held.at[k, :, pl.ds(0, 512)], sems.at[2 * k]),
        pltpu.make_async_copy(beside, held.at[k, :, pl.ds(512, 512)], sems.at[2 * k + 1]),
    ]


def hid_dot(conv, weights):
    return lax.dot_general(
        conv, weights, (((1,), (1,)), ((), ())), preferred_element_type=F32
    ).astype(BF16)


def hid_kernel(here, conv, *refs):
    blocks, out, (held, sems) = refs[:14], refs[14], refs[15:]
    copies = [hid_copies(blocks[k], blocks[7 + k], held, k, sems) for k in range(7)]
    for pair in copies:
        for copy in pair:
            copy.start()
    for k, pair in enumerate(copies):
        for copy in pair:
            copy.wait()
        out[k] = hid_dot(conv[...], held[k])


def hid_last_kernel(here, conv, done, own, beside, *refs):
    outs, (held, whole, sems) = refs[:8], refs[8:]
    copies = hid_copies(own, beside, held, 0, sems)
    copies.append(pltpu.make_async_copy(done, whole.at[pl.ds(0, 7)], sems.at[2]))
    for copy in copies:
        copy.start()
    row, y_lo, z, x, y_hi, core = place_of(here)
    ahead = 1 - 2 * core
    copies[0].wait()
    copies[1].wait()
    whole[7] = hid_dot(conv[...], held[0])
    copies[2].wait()
    slots = [
        row_slot(((x + step) & 3) * 2 + (y_hi ^ i), y_lo, z)
        for step in (2, -ahead, ahead, 0)
        for i in range(2)
    ]
    send_out(whole, slots, outs, sems, 3)


def hid_partial(here, conv, blocks, beside):
    part = jax.ShapeDtypeStruct((768, 256), BF16)
    flops = 2 * 768 * 1024 * 256
    (done,) = call(
        hid_kernel, [jax.ShapeDtypeStruct((7, 768, 256), BF16)], pltpu.VMEM,
        [pltpu.VMEM((7, 256, 1024), BF16)], 14, 8 << 20, 7 * flops, here, [conv],
        [*blocks[:7], *beside[:7]],
    )
    return call(
        hid_last_kernel, [part] * 8, pl.ANY,
        [pltpu.VMEM((1, 256, 1024), BF16), pltpu.VMEM((8, 768, 256), BF16)], 11, 6 << 20, flops,
        here, [conv], [done, blocks[7], beside[7]],
    )


def act_copies(own, beside, at, sems, first, core):
    copies = []
    for part, ref in enumerate((own, beside)):
        rows = pl.ds(pl.multiple_of((core ^ part) * 768, 768), 768)
        copies.append(pltpu.make_async_copy(ref, at(rows), sems.at[first + part]))
    return copies


def win_kernel(here, left, *refs):
    blocks, out, (held, sems) = refs[:14], refs[14], refs[15:]
    core = here[1] & 1
    copies = [
        act_copies(
            blocks[k], blocks[7 + k], lambda rows, k=k: held.at[k, rows, :], sems, 2 * k, core
        )
        for k in range(7)
    ]
    for pair in copies:
        for copy in pair:
            copy.start()
    for k, pair in enumerate(copies):
        for copy in pair:
            copy.wait()
        out[k] = jnp.dot(left[...], held[k], preferred_element_type=F32).astype(BF16)


def win_last_kernel(here, left, done, own, beside, *refs):
    outs, (held, whole, sems) = refs[:8], refs[8:]
    row, y_lo, z, x, y_hi, core = place_of(here)
    ahead = 1 - 2 * core
    copies = act_copies(own, beside, lambda rows: held.at[rows, :], sems, 0, core)
    copies.append(pltpu.make_async_copy(done, whole.at[pl.ds(0, 7)], sems.at[2]))
    for copy in copies:
        copy.start()
    copies[0].wait()
    copies[1].wait()
    whole[7] = jnp.dot(left[...], held[...], preferred_element_type=F32).astype(BF16)
    copies[2].wait()
    slots = [
        hidden_slot((y_lo ^ i) * 4 + ((z + step) & 3), x, y_hi)
        for step in (2, -ahead, ahead, 0)
        for i in range(2)
    ]
    send_out(whole, slots, outs, sems, 3)


def win_partial(here, left, blocks, beside):
    part = jax.ShapeDtypeStruct((512, 256), BF16)
    flops = 2 * 512 * 1536 * 256
    (done,) = call(
        win_kernel, [jax.ShapeDtypeStruct((7, 512, 256), BF16)], pltpu.VMEM,
        [pltpu.VMEM((7, 1536, 256), BF16)], 14, 8 << 20, 7 * flops, here, [left],
        [*blocks[:7], *beside[:7]],
    )
    return call(
        win_last_kernel, [part] * 8, pl.ANY,
        [pltpu.VMEM((1536, 256), BF16), pltpu.VMEM((8, 512, 256), BF16)], 11, 6 << 20, flops,
        here, [left], [done, blocks[7], beside[7]],
    )


def out_kernel(held_slots, here, start, *refs):
    blocks, parts, out = refs[:8], refs[8:12], refs[12]
    held, loaded, weights, sems = refs[13:]
    row, y_lo, z, x, y_hi, core = place_of(here)
    copies = [
        pltpu.make_async_copy(ref, loaded.at[pl.ds(k * 2, 2)], sems.at[8 + k])
        for k, ref in enumerate(parts)
    ]
    for k in range(4):
        copies += act_copies(
            blocks[k], blocks[4 + k],
            lambda rows, k=k: held.at[rows, pl.ds(k * 256, 256)], sems, 2 * k, core,
        )
    for copy in copies:
        copy.start()
    for copy in copies:
        copy.wait()
    for k, slot in enumerate(held_slots):
        block = ((x + STEPS[slot // 2]) & 3) * 2 + (y_hi ^ (slot & 1))
        weights[:, k * 256 : k * 256 + 256] = loaded[row_slot(block, y_lo, z)]
    for at in range(0, 1536, 256):
        total = start[at : at + 256, :].astype(F32) + lax.dot_general(
            held[at : at + 256, :], weights[...], (((1,), (1,)), ((), ())),
            preferred_element_type=F32,
        )
        out[at : at + 256, :] = total.astype(out.dtype)


def out_partial(here, start, blocks, beside, weights, slots, kind):
    return call(
        functools.partial(out_kernel, slots), [jax.ShapeDtypeStruct((1536, 512), kind)],
        pltpu.VMEM,
        [
            pltpu.VMEM((1536, 1024), BF16),
            pltpu.VMEM((8, 512, 256), BF16),
            pltpu.VMEM((512, 1024), BF16),
        ],
        12, 10 << 20, 1536 * 512 * 2048, here, [start],
        [*(blocks[k] for k in slots), *(beside[k] for k in slots), *weights],
    )[0]


def tie(*values):
    return lax.optimization_barrier(values)


def add(terms):
    return sum(term.astype(F32) for term in terms)


def local(
    inputs,
    cotangent,
    conv_out,
    pre_act,
    weight_in,
    weight_out,
    scale_mid,
    scale_wide,
    keep_mid,
    keep_wide,
):
    rows = inputs.shape[0]
    half = rows // 2
    scaling = 1.0 / math.sqrt(rows * lax.axis_size("row"))
    row, col = lax.axis_index("row"), lax.axis_index("col")
    y_lo, z = row // 4, row % 4
    x, y_hi, core = col // 4, (col // 2) % 2, col % 2
    place = jnp.stack([row, col]).astype(jnp.int32)

    def mine(v):
        return lax.dynamic_slice_in_dim(v, core * half, half, 0)

    def theirs(v):
        return lax.dynamic_slice_in_dim(v, (1 - core) * half, half, 0)

    mid_gain = scale_mid * keep_mid.astype(F32)
    hidden = jnp.maximum(pre_act.astype(F32) * mid_gain, 0.0).astype(BF16)
    hidden_full = lax.all_gather(hidden, "col", axis=1, tiled=True)
    out_above, out_below = z_shift(weight_out, -1), z_shift(weight_out, 1)
    out_near = y_lo_swap(weight_out)

    wide_gain = scale_wide * keep_wide.astype(F32)
    cot_float = cotangent.astype(F32)
    grad_conv = (cot_float * wide_gain).astype(BF16)
    wide_part = jnp.sum(cot_float * conv_out.astype(F32), axis=0)
    conv_mine = mine(grad_conv)
    conv_sent, input_turned = theirs(grad_conv), inputs.T
    out_near, conv_sent, input_turned, wide_part, pre_act = tie(
        out_near, conv_sent, input_turned, wide_part, pre_act
    )
    near_above, near_below = z_shift(out_near, -1), z_shift(out_near, 1)
    out_across = onward(out_above, out_below, core, z_split)
    conv_both = jnp.concatenate([conv_mine, core_swap(conv_sent)], axis=1)
    near_above, conv_both = tie(near_above, conv_both)
    near_across = onward(near_above, near_below, core, z_split)
    out_blocks = [
        weight_out, out_near, out_above, near_above, out_below, near_below, out_across, near_across
    ]

    gain_pair = jnp.stack([scale_mid, keep_mid.astype(F32)])
    gain_beside = core_swap(gain_pair)
    pre_mine = mine(pre_act)
    pre_beside = core_swap(theirs(pre_act))

    def chip_order(a, b):
        return jnp.concatenate(
            [jnp.where(core == 0, a, b), jnp.where(core == 0, b, a)], axis=1
        )

    pre_chip = chip_order(pre_mine, pre_beside).astype(F32)
    gain_chip = chip_order(gain_pair, gain_beside)
    mid_gain = gain_chip[0] * gain_chip[1]

    out_beside = [core_swap(block) for block in out_blocks]
    out_beside[7], weight_in = tie(out_beside[7], weight_in)
    in_near = y_lo_swap(weight_in)
    sends = hid_partial(place, conv_both, out_blocks, out_beside)
    passed = [x_split(sends[i], 1) for i in (1, 0)]
    back = [x_split(sends[2 + i], -1) for i in (1, 0)]
    passed[0], in_near = tie(passed[0], in_near)
    in_here = jnp.stack([weight_in, in_near])
    in_above, in_below = z_shift(in_here, -1), z_shift(in_here, 1)
    far = x_split(add([sends[5], passed[0]]).astype(BF16), 1)
    near = x_split(add([sends[4], passed[1]]).astype(BF16), 1)
    far, in_above, in_below = tie(far, in_above, in_below)
    in_across = onward(in_above, in_below, core, z_split)
    crossed = y_hi_swap(add([sends[7], back[0], far]).astype(BF16))
    near, hidden_full = tie(near, hidden_full)
    total = add([sends[6], back[1], near])
    wout = dot(hidden_full, grad_conv, 0, 0).astype(BF16)
    crossed, wout, in_across = tie(crossed, wout, in_across)
    in_blocks = [in_here, in_above, in_below, in_across]
    wout = lax.psum_scatter(wout, "row", scatter_dimension=0, tiled=True)
    grad_hid = add([total, crossed])
    alive = (pre_chip > 0) & (gain_chip[1] > 0)[None, :]
    grad_pre = jnp.where(alive, grad_hid, 0.0)
    mid_part = jnp.sum(grad_pre * pre_chip, axis=0).reshape(2, 128)
    grad_act = (grad_pre * mid_gain).astype(BF16)
    act_near = y_hi_swap(grad_act)
    act_above, act_below = x_shift(grad_act, -1), x_shift(grad_act, 1)
    near_above, near_below = x_shift(act_near, -1), x_shift(act_near, 1)
    act_across = onward(act_above, act_below, core, x_split)
    act = [grad_act, act_near, act_above, near_above, act_below, near_below, act_across]
    act_beside = [core_swap(block) for block in act]
    grad_x = out_partial(place, cotangent, act, act_beside, in_blocks, (0, 1, 2, 4), F32)
    near_above, grad_x = tie(near_above, grad_x)
    act.append(onward(near_above, near_below, core, x_split))
    act_beside.append(core_swap(act[7]))

    mid_own = lax.dynamic_index_in_dim(mid_part, core, 0, keepdims=False)
    mid_away = lax.dynamic_index_in_dim(mid_part, 1 - core, 0, keepdims=False)
    mid_own = mid_own + core_swap(mid_away)
    sums = jnp.concatenate([mid_own, wide_part]).reshape(5, 128)
    sums = sums + z_flip(sums, 1)
    sums = sums + z_flip(sums, 2)
    sums = sums + y_lo_swap(sums)

    act[7], sums = tie(act[7], sums)
    sends = win_partial(place, input_turned, act, act_beside)
    passed = [z_split(sends[i], 1) for i in (1, 0)]
    back = [z_split(sends[2 + i], -1) for i in (1, 0)]
    far = z_split(add([sends[5], passed[0]]).astype(BF16), 1)
    near = z_split(add([sends[4], passed[1]]).astype(BF16), 1)
    grad_x = out_partial(place, grad_x, act, act_beside, in_blocks, (3, 5, 6, 7), BF16)
    far, grad_x, wout = tie(far, grad_x, wout)
    crossed = y_lo_swap(add([sends[7], back[0], far]).astype(BF16))
    grad_win = add([sends[6], back[1], near, crossed]) * scaling
    grad_wout = wout.astype(F32) * scaling
    grad_smid = keep_mid.astype(F32) * scaling * sums[0]
    grad_swide = keep_wide.astype(F32) * scaling * sums[1:].reshape(512)
    return (grad_x, grad_win, grad_wout, grad_smid, grad_swide)


def solution(mesh):
    return jax.shard_map(
        local,
        mesh=mesh,
        in_specs=(
            P("row", "col"),
            P("row", "col"),
            P("row", "col"),
            P("row", "col"),
            P("col", "row"),
            P("row", "col"),
            P("col"),
            P("col"),
            P("col"),
            P("col"),
        ),
        out_specs=(P("row", "col"), P("col", "row"), P("row", "col"), P("col"), P("col")),
        check_vma=False,
    )
```

```python
import functools
import math

import jax
import jax.numpy as jnp
from jax import lax
from jax.experimental import pallas as pl
from jax.experimental.pallas import tpu as pltpu
from jax.sharding import PartitionSpec as P

F32 = jnp.float32
BF16 = jnp.bfloat16
AXES = ("row", "col")
STEPS = (0, 1, 3, 2)


def permute(v, target):
    pairs = []
    for row in range(8):
        for col in range(16):
            y_lo, z, x, y_hi, core = target(
                row // 4, row % 4, col // 4, (col // 2) % 2, col % 2
            )
            pairs.append(
                (row * 16 + col, (y_lo * 4 + z % 4) * 16 + (x % 4) * 4 + y_hi * 2 + core)
            )
    return lax.ppermute(v, AXES, pairs)


def core_swap(v):
    return permute(v, lambda yl, z, x, yh, c: (yl, z, x, yh, 1 - c))


def y_hi_swap(v):
    return permute(v, lambda yl, z, x, yh, c: (yl, z, x, 1 - yh, c))


def y_lo_swap(v):
    return permute(v, lambda yl, z, x, yh, c: (1 - yl, z, x, yh, c))


def z_flip(v, mask):
    return permute(v, lambda yl, z, x, yh, c: (yl, z ^ mask, x, yh, c))


def x_shift(v, step):
    return permute(v, lambda yl, z, x, yh, c: (yl, z, x + step, yh, c))


def z_shift(v, step):
    return permute(v, lambda yl, z, x, yh, c: (yl, z + step, x, yh, c))


def x_split(v, way):
    return permute(v, lambda yl, z, x, yh, c: (yl, z, x + way * (1 - 2 * c), yh, c))


def z_split(v, way):
    return permute(v, lambda yl, z, x, yh, c: (yl, z + way * (1 - 2 * c), x, yh, c))


def dot(a, b, ca, cb):
    return lax.dot_general(a, b, (((ca,), (cb,)), ((), ())), preferred_element_type=F32)


def onward(above, below, core, split):
    return split(jnp.where(core == 0, below, above), 1)


def place_of(v):
    row, col = v[0], v[1]
    return row, row >> 2, row & 3, col >> 2, (col >> 1) & 1, col & 1


def slot_of(step):
    step = step & 3
    return jnp.where(step >= 2, 5 - step, step)


def row_slot(block, y_lo, z):
    return slot_of((block & 3) - z) * 2 + ((block >> 2) ^ y_lo)


def hidden_slot(block, x, y_hi):
    return slot_of((block >> 1) - x) * 2 + ((block & 1) ^ y_hi)


def call(body, outs, out_space, scratch, sems, loads, flops, here, vmem_args, any_args):
    vmem = pl.BlockSpec(memory_space=pltpu.VMEM)
    return pl.pallas_call(
        body,
        out_shape=outs,
        in_specs=[pl.BlockSpec(memory_space=pltpu.SMEM)]
        + [vmem] * len(vmem_args)
        + [pl.BlockSpec(memory_space=pl.ANY)] * len(any_args),
        out_specs=[pl.BlockSpec(memory_space=out_space)] * len(outs),
        scratch_shapes=[*scratch, pltpu.SemaphoreType.DMA((sems,))],
        compiler_params=pltpu.CompilerParams(vmem_limit_bytes=60 * 1024 * 1024),
        cost_estimate=pl.CostEstimate(flops=flops, bytes_accessed=loads, transcendentals=0),
    )(here, *vmem_args, *any_args)


def hid_kernel(ways, here, conv, *refs):
    blocks, outs, (held, sems) = refs[:16], refs[16:20], refs[20:]
    copies = [
        pltpu.make_async_copy(
            ref, held.at[k % 8, :, pl.ds((k // 8) * 512, 512)], sems.at[k]
        )
        for k, ref in enumerate(blocks)
    ]
    for copy in copies:
        copy.start()
    row, y_lo, z, x, y_hi, core = place_of(here)
    ahead = 1 - 2 * core
    for copy in copies:
        copy.wait()
    for j, out in enumerate(outs):
        fixed, way = ways[j // 2]
        block = ((x + fixed + way * ahead) & 3) * 2 + (y_hi ^ (j % 2))
        out[...] = lax.dot_general(
            conv[...], held[row_slot(block, y_lo, z)], (((1,), (1,)), ((), ())),
            preferred_element_type=F32,
        ).astype(BF16)


def hid_partial(here, conv, blocks, beside, ways):
    return call(
        functools.partial(hid_kernel, ways), [jax.ShapeDtypeStruct((768, 256), BF16)] * 4,
        pltpu.VMEM, [pltpu.VMEM((8, 256, 1024), BF16)], 16, 8 << 20, 768 * 1024 * 2048, here,
        [conv], [*blocks, *beside],
    )


def act_copies(own, beside, at, sems, first, core):
    copies = []
    for part, ref in enumerate((own, beside)):
        rows = pl.ds(pl.multiple_of((core ^ part) * 768, 768), 768)
        copies.append(pltpu.make_async_copy(ref, at(rows), sems.at[first + part]))
    return copies


def win_kernel(here, left, *refs):
    blocks, outs, (held, sems) = refs[:16], refs[16:24], refs[24:]
    row, y_lo, z, x, y_hi, core = place_of(here)
    copies = []
    for k in range(8):
        copies += act_copies(
            blocks[k], blocks[8 + k], lambda rows, k=k: held.at[k, rows, :], sems, 2 * k, core
        )
    for copy in copies:
        copy.start()
    for copy in copies:
        copy.wait()
    ahead = 1 - 2 * core
    for j, out in enumerate(outs):
        step = (2, -ahead, ahead, 0)[j // 2]
        block = (y_lo ^ (j % 2)) * 4 + ((z + step) & 3)
        out[...] = jnp.dot(
            left[...], held[hidden_slot(block, x, y_hi)], preferred_element_type=F32
        ).astype(BF16)


def win_partial(here, left, blocks, beside):
    return call(
        win_kernel, [jax.ShapeDtypeStruct((512, 256), BF16)] * 8, pltpu.VMEM,
        [pltpu.VMEM((8, 1536, 256), BF16)], 16, 10 << 20, 2 * 512 * 1536 * 2048, here, [left],
        [*blocks, *beside],
    )


def out_kernel(held_slots, here, start, *refs):
    blocks, parts, out = refs[:8], refs[8:12], refs[12]
    held, loaded, weights, sems = refs[13:]
    row, y_lo, z, x, y_hi, core = place_of(here)
    copies = [
        pltpu.make_async_copy(ref, loaded.at[pl.ds(k * 2, 2)], sems.at[8 + k])
        for k, ref in enumerate(parts)
    ]
    for k in range(4):
        copies += act_copies(
            blocks[k], blocks[4 + k],
            lambda rows, k=k: held.at[rows, pl.ds(k * 256, 256)], sems, 2 * k, core,
        )
    for copy in copies:
        copy.start()
    for copy in copies:
        copy.wait()
    for k, slot in enumerate(held_slots):
        block = ((x + STEPS[slot // 2]) & 3) * 2 + (y_hi ^ (slot & 1))
        weights[:, k * 256 : k * 256 + 256] = loaded[row_slot(block, y_lo, z)]
    for at in range(0, 1536, 256):
        total = start[at : at + 256, :].astype(F32) + lax.dot_general(
            held[at : at + 256, :], weights[...], (((1,), (1,)), ((), ())),
            preferred_element_type=F32,
        )
        out[at : at + 256, :] = total.astype(out.dtype)


def out_partial(here, start, blocks, beside, weights, slots, kind):
    return call(
        functools.partial(out_kernel, slots), [jax.ShapeDtypeStruct((1536, 512), kind)],
        pltpu.VMEM,
        [
            pltpu.VMEM((1536, 1024), BF16),
            pltpu.VMEM((8, 512, 256), BF16),
            pltpu.VMEM((512, 1024), BF16),
        ],
        12, 10 << 20, 1536 * 512 * 2048, here, [start],
        [*(blocks[k] for k in slots), *(beside[k] for k in slots), *weights],
    )[0]


def tie(*values):
    return lax.optimization_barrier(values)


def add(terms):
    return sum(term.astype(F32) for term in terms)


def local(
    inputs,
    cotangent,
    conv_out,
    pre_act,
    weight_in,
    weight_out,
    scale_mid,
    scale_wide,
    keep_mid,
    keep_wide,
):
    rows = inputs.shape[0]
    half = rows // 2
    scaling = 1.0 / math.sqrt(rows * lax.axis_size("row"))
    row, col = lax.axis_index("row"), lax.axis_index("col")
    y_lo, z = row // 4, row % 4
    x, y_hi, core = col // 4, (col // 2) % 2, col % 2
    place = jnp.stack([row, col]).astype(jnp.int32)

    def mine(v):
        return lax.dynamic_slice_in_dim(v, core * half, half, 0)

    def theirs(v):
        return lax.dynamic_slice_in_dim(v, (1 - core) * half, half, 0)

    mid_gain = scale_mid * keep_mid.astype(F32)
    hidden = jnp.maximum(pre_act.astype(F32) * mid_gain, 0.0).astype(BF16)
    hidden_full = lax.all_gather(hidden, "col", axis=1, tiled=True)
    out_above, out_below = z_shift(weight_out, -1), z_shift(weight_out, 1)
    out_near = y_lo_swap(weight_out)

    wide_gain = scale_wide * keep_wide.astype(F32)
    cot_float = cotangent.astype(F32)
    grad_conv = (cot_float * wide_gain).astype(BF16)
    wide_part = jnp.sum(cot_float * conv_out.astype(F32), axis=0)
    conv_mine = mine(grad_conv)
    conv_sent, input_turned = theirs(grad_conv), inputs.T
    out_near, conv_sent, input_turned, wide_part, pre_act = tie(
        out_near, conv_sent, input_turned, wide_part, pre_act
    )
    near_above, near_below = z_shift(out_near, -1), z_shift(out_near, 1)
    out_across = onward(out_above, out_below, core, z_split)
    conv_both = jnp.concatenate([conv_mine, core_swap(conv_sent)], axis=1)
    near_above, conv_both, weight_in = tie(near_above, conv_both, weight_in)
    in_near = y_lo_swap(weight_in)
    near_across = onward(near_above, near_below, core, z_split)
    out_blocks = [
        weight_out, out_near, out_above, near_above, out_below, near_below, out_across, near_across
    ]

    gain_pair = jnp.stack([scale_mid, keep_mid.astype(F32)])
    gain_beside = core_swap(gain_pair)
    pre_mine = mine(pre_act)
    pre_beside = core_swap(theirs(pre_act))

    def chip_order(a, b):
        return jnp.concatenate(
            [jnp.where(core == 0, a, b), jnp.where(core == 0, b, a)], axis=1
        )

    pre_chip = chip_order(pre_mine, pre_beside).astype(F32)
    gain_chip = chip_order(gain_pair, gain_beside)
    mid_gain = gain_chip[0] * gain_chip[1]

    out_beside = [core_swap(block) for block in out_blocks]
    ways = ((2, 0), (0, 1))
    first = list(hid_partial(place, conv_both, out_blocks, out_beside, ways))
    passed = [x_split(first[i], 1) for i in (1, 0)]
    first[3], in_near = tie(first[3], in_near)
    in_here = jnp.stack([weight_in, in_near])
    conv_both, in_here = tie(conv_both, in_here)
    in_above, in_below = z_shift(in_here, -1), z_shift(in_here, 1)
    second = hid_partial(place, conv_both, out_blocks, out_beside, ((0, -1), (0, 0)))
    passed[0], second = tie(passed[0], second)
    back = [x_split(second[i], -1) for i in (1, 0)]
    far = x_split(add([first[3], passed[0]]).astype(BF16), 1)
    near = x_split(add([first[2], passed[1]]).astype(BF16), 1)
    far, in_above, in_below = tie(far, in_above, in_below)
    in_across = onward(in_above, in_below, core, z_split)
    in_blocks = [in_here, in_above, in_below, in_across]
    crossed = y_hi_swap(add([second[3], back[0], far]).astype(BF16))
    near, hidden_full, in_blocks[3] = tie(near, hidden_full, in_across)
    total = add([second[2], back[1], near])
    wout = dot(hidden_full, grad_conv, 0, 0).astype(BF16)
    crossed, wout = tie(crossed, wout)
    grad_hid = add([total, crossed])
    alive = (pre_chip > 0) & (gain_chip[1] > 0)[None, :]
    grad_pre = jnp.where(alive, grad_hid, 0.0)
    mid_part = jnp.sum(grad_pre * pre_chip, axis=0).reshape(2, 128)
    grad_act = (grad_pre * mid_gain).astype(BF16)
    act_near = y_hi_swap(grad_act)
    act_above, act_below = x_shift(grad_act, -1), x_shift(grad_act, 1)
    act_near, wout = tie(act_near, wout)
    wout = lax.psum_scatter(wout, "row", scatter_dimension=0, tiled=True)
    near_above, near_below = x_shift(act_near, -1), x_shift(act_near, 1)
    act_across = onward(act_above, act_below, core, x_split)
    act = [grad_act, act_near, act_above, near_above, act_below, near_below, act_across]
    act_beside = [core_swap(block) for block in act]
    grad_x = out_partial(place, cotangent, act, act_beside, in_blocks, (0, 1, 2, 4), F32)
    near_above, grad_x = tie(near_above, grad_x)
    act.append(onward(near_above, near_below, core, x_split))
    act_beside.append(core_swap(act[7]))

    mid_own = lax.dynamic_index_in_dim(mid_part, core, 0, keepdims=False)
    mid_away = lax.dynamic_index_in_dim(mid_part, 1 - core, 0, keepdims=False)
    mid_own = mid_own + core_swap(mid_away)
    sums = jnp.concatenate([mid_own, wide_part]).reshape(5, 128)
    sums = sums + z_flip(sums, 1)
    sums = sums + z_flip(sums, 2)
    sums = sums + y_lo_swap(sums)

    act[7], sums = tie(act[7], sums)
    sends = win_partial(place, input_turned, act, act_beside)
    passed = [z_split(sends[i], 1) for i in (1, 0)]
    back = [z_split(sends[2 + i], -1) for i in (1, 0)]
    far = z_split(add([sends[5], passed[0]]).astype(BF16), 1)
    near = z_split(add([sends[4], passed[1]]).astype(BF16), 1)
    grad_x = out_partial(place, grad_x, act, act_beside, in_blocks, (3, 5, 6, 7), BF16)
    far, grad_x, wout = tie(far, grad_x, wout)
    crossed = y_lo_swap(add([sends[7], back[0], far]).astype(BF16))
    grad_win = add([sends[6], back[1], near, crossed]) * scaling
    grad_wout = wout.astype(F32) * scaling
    grad_smid = keep_mid.astype(F32) * scaling * sums[0]
    grad_swide = keep_wide.astype(F32) * scaling * sums[1:].reshape(512)
    return (grad_x, grad_win, grad_wout, grad_smid, grad_swide)


def solution(mesh):
    return jax.shard_map(
        local,
        mesh=mesh,
        in_specs=(
            P("row", "col"),
            P("row", "col"),
            P("row", "col"),
            P("row", "col"),
            P("col", "row"),
            P("row", "col"),
            P("col"),
            P("col"),
            P("col"),
            P("col"),
        ),
        out_specs=(P("row", "col"), P("col", "row"), P("row", "col"), P("col"), P("col")),
        check_vma=False,
    )
```

```python
import functools
import math

import jax
import jax.numpy as jnp
from jax import lax
from jax.experimental import pallas as pl
from jax.experimental.pallas import tpu as pltpu
from jax.sharding import PartitionSpec as P

F32 = jnp.float32
BF16 = jnp.bfloat16
AXES = ("row", "col")
STEPS = (0, 1, 3, 2)


def permute(v, target):
    pairs = []
    for row in range(8):
        for col in range(16):
            y_lo, z, x, y_hi, core = target(
                row // 4, row % 4, col // 4, (col // 2) % 2, col % 2
            )
            pairs.append(
                (row * 16 + col, (y_lo * 4 + z % 4) * 16 + (x % 4) * 4 + y_hi * 2 + core)
            )
    return lax.ppermute(v, AXES, pairs)


def core_swap(v):
    return permute(v, lambda yl, z, x, yh, c: (yl, z, x, yh, 1 - c))


def y_hi_swap(v):
    return permute(v, lambda yl, z, x, yh, c: (yl, z, x, 1 - yh, c))


def y_lo_swap(v):
    return permute(v, lambda yl, z, x, yh, c: (1 - yl, z, x, yh, c))


def z_flip(v, mask):
    return permute(v, lambda yl, z, x, yh, c: (yl, z ^ mask, x, yh, c))


def x_shift(v, step):
    return permute(v, lambda yl, z, x, yh, c: (yl, z, x + step, yh, c))


def z_shift(v, step):
    return permute(v, lambda yl, z, x, yh, c: (yl, z + step, x, yh, c))


def x_split(v, way):
    return permute(v, lambda yl, z, x, yh, c: (yl, z, x + way * (1 - 2 * c), yh, c))


def z_split(v, way):
    return permute(v, lambda yl, z, x, yh, c: (yl, z + way * (1 - 2 * c), x, yh, c))


def dot(a, b, ca, cb):
    return lax.dot_general(a, b, (((ca,), (cb,)), ((), ())), preferred_element_type=F32)


def onward(above, below, core, split):
    return split(jnp.where(core == 0, below, above), 1)


def place_of(v):
    row, col = v[0], v[1]
    return row, row >> 2, row & 3, col >> 2, (col >> 1) & 1, col & 1


def slot_of(step):
    step = step & 3
    return jnp.where(step >= 2, 5 - step, step)


def row_slot(block, y_lo, z):
    return slot_of((block & 3) - z) * 2 + ((block >> 2) ^ y_lo)


def hidden_slot(block, x, y_hi):
    return slot_of((block >> 1) - x) * 2 + ((block & 1) ^ y_hi)


def call(body, outs, out_space, scratch, sems, loads, flops, here, vmem_args, any_args):
    vmem = pl.BlockSpec(memory_space=pltpu.VMEM)
    return pl.pallas_call(
        body,
        out_shape=outs,
        in_specs=[pl.BlockSpec(memory_space=pltpu.SMEM)]
        + [vmem] * len(vmem_args)
        + [pl.BlockSpec(memory_space=pl.ANY)] * len(any_args),
        out_specs=[pl.BlockSpec(memory_space=out_space)] * len(outs),
        scratch_shapes=[*scratch, pltpu.SemaphoreType.DMA((sems,))],
        compiler_params=pltpu.CompilerParams(vmem_limit_bytes=60 * 1024 * 1024),
        cost_estimate=pl.CostEstimate(flops=flops, bytes_accessed=loads, transcendentals=0),
    )(here, *vmem_args, *any_args)


def hid_kernel(ways, here, conv, *refs):
    blocks, outs, (held, sems) = refs[:16], refs[16:18], refs[18:]
    copies = [
        pltpu.make_async_copy(
            ref, held.at[k % 8, :, pl.ds((k // 8) * 512, 512)], sems.at[k]
        )
        for k, ref in enumerate(blocks)
    ]
    for copy in copies:
        copy.start()
    row, y_lo, z, x, y_hi, core = place_of(here)
    ahead = 1 - 2 * core
    for copy in copies:
        copy.wait()
    for j in range(4):
        fixed, way = ways[j // 2]
        block = ((x + fixed + way * ahead) & 3) * 2 + (y_hi ^ (j % 2))
        outs[j // 2][j % 2] = lax.dot_general(
            conv[...], held[row_slot(block, y_lo, z)], (((1,), (1,)), ((), ())),
            preferred_element_type=F32,
        ).astype(BF16)


def hid_partial(here, conv, blocks, beside, ways):
    return call(
        functools.partial(hid_kernel, ways), [jax.ShapeDtypeStruct((2, 768, 256), BF16)] * 2,
        pltpu.VMEM, [pltpu.VMEM((8, 256, 1024), BF16)], 16, 8 << 20, 768 * 1024 * 2048, here,
        [conv], [*blocks, *beside],
    )


def act_copies(own, beside, at, sems, first, core):
    copies = []
    for part, ref in enumerate((own, beside)):
        rows = pl.ds(pl.multiple_of((core ^ part) * 768, 768), 768)
        copies.append(pltpu.make_async_copy(ref, at(rows), sems.at[first + part]))
    return copies


def win_kernel(here, left, *refs):
    blocks, outs, (held, sems) = refs[:16], refs[16:20], refs[20:]
    row, y_lo, z, x, y_hi, core = place_of(here)
    copies = []
    for k in range(8):
        copies += act_copies(
            blocks[k], blocks[8 + k], lambda rows, k=k: held.at[k, rows, :], sems, 2 * k, core
        )
    for copy in copies:
        copy.start()
    for copy in copies:
        copy.wait()
    ahead = 1 - 2 * core
    for j in range(8):
        step = (2, -ahead, ahead, 0)[j // 2]
        block = (y_lo ^ (j % 2)) * 4 + ((z + step) & 3)
        outs[j // 2][j % 2] = jnp.dot(
            left[...], held[hidden_slot(block, x, y_hi)], preferred_element_type=F32
        ).astype(BF16)


def win_partial(here, left, blocks, beside):
    return call(
        win_kernel, [jax.ShapeDtypeStruct((2, 512, 256), BF16)] * 4, pltpu.VMEM,
        [pltpu.VMEM((8, 1536, 256), BF16)], 16, 10 << 20, 2 * 512 * 1536 * 2048, here, [left],
        [*blocks, *beside],
    )


def out_kernel(here, cot, *refs):
    blocks, parts, out = refs[:16], refs[16:20], refs[20]
    held, weights, sems = refs[21:]
    row, y_lo, z, x, y_hi, core = place_of(here)
    copies = [
        pltpu.make_async_copy(ref, weights.at[pl.ds(k * 2, 2)], sems.at[16 + k])
        for k, ref in enumerate(parts)
    ]
    for k in range(8):
        copies += act_copies(
            blocks[k], blocks[8 + k], lambda rows, k=k: held.at[k, rows, :], sems, 2 * k, core
        )
    for copy in copies:
        copy.start()
    for copy in copies:
        copy.wait()
    for at in range(0, 1536, 256):
        total = cot[at : at + 256, :].astype(F32)
        for block in range(8):
            total = total + lax.dot_general(
                held[hidden_slot(block, x, y_hi), at : at + 256, :],
                weights[row_slot(block, y_lo, z)],
                (((1,), (1,)), ((), ())),
                preferred_element_type=F32,
            )
        out[at : at + 256, :] = total.astype(BF16)


def out_gradient(here, cot, blocks, beside, weights):
    return call(
        out_kernel, [jax.ShapeDtypeStruct((1536, 512), BF16)], pltpu.VMEM,
        [pltpu.VMEM((8, 1536, 256), BF16), pltpu.VMEM((8, 512, 256), BF16)], 20, 12 << 20,
        2 * 1536 * 512 * 2048, here, [cot], [*blocks, *beside, *weights],
    )[0]


def tie(*values):
    return lax.optimization_barrier(values)


def add(terms):
    return sum(term.astype(F32) for term in terms)


def local(
    inputs,
    cotangent,
    conv_out,
    pre_act,
    weight_in,
    weight_out,
    scale_mid,
    scale_wide,
    keep_mid,
    keep_wide,
):
    rows = inputs.shape[0]
    half = rows // 2
    scaling = 1.0 / math.sqrt(rows * lax.axis_size("row"))
    row, col = lax.axis_index("row"), lax.axis_index("col")
    y_lo, z = row // 4, row % 4
    x, y_hi, core = col // 4, (col // 2) % 2, col % 2
    place = jnp.stack([row, col]).astype(jnp.int32)

    def mine(v):
        return lax.dynamic_slice_in_dim(v, core * half, half, 0)

    def theirs(v):
        return lax.dynamic_slice_in_dim(v, (1 - core) * half, half, 0)

    mid_gain = scale_mid * keep_mid.astype(F32)
    hidden = jnp.maximum(pre_act.astype(F32) * mid_gain, 0.0).astype(BF16)
    hidden_full = lax.all_gather(hidden, "col", axis=1, tiled=True)
    out_above, out_below = z_shift(weight_out, -1), z_shift(weight_out, 1)
    out_near = y_lo_swap(weight_out)

    wide_gain = scale_wide * keep_wide.astype(F32)
    cot_float = cotangent.astype(F32)
    grad_conv = (cot_float * wide_gain).astype(BF16)
    wide_part = jnp.sum(cot_float * conv_out.astype(F32), axis=0)
    conv_mine = mine(grad_conv)
    conv_sent, input_turned = theirs(grad_conv), inputs.T
    out_near, conv_sent, input_turned, wide_part, pre_act = tie(
        out_near, conv_sent, input_turned, wide_part, pre_act
    )
    near_above, near_below = z_shift(out_near, -1), z_shift(out_near, 1)
    out_across = onward(out_above, out_below, core, z_split)
    conv_both = jnp.concatenate([conv_mine, core_swap(conv_sent)], axis=1)
    near_above, conv_both, weight_in = tie(near_above, conv_both, weight_in)
    in_near = y_lo_swap(weight_in)
    near_across = onward(near_above, near_below, core, z_split)
    out_blocks = [
        weight_out, out_near, out_above, near_above, out_below, near_below, out_across, near_across
    ]

    gain_pair = jnp.stack([scale_mid, keep_mid.astype(F32)])
    gain_beside = core_swap(gain_pair)
    pre_mine = mine(pre_act)
    pre_beside = core_swap(theirs(pre_act))

    def chip_order(a, b):
        return jnp.concatenate(
            [jnp.where(core == 0, a, b), jnp.where(core == 0, b, a)], axis=1
        )

    pre_chip = chip_order(pre_mine, pre_beside).astype(F32)
    gain_chip = chip_order(gain_pair, gain_beside)
    mid_gain = gain_chip[0] * gain_chip[1]

    out_beside = [core_swap(block) for block in out_blocks]
    away, there = hid_partial(place, conv_both, out_blocks, out_beside, ((2, 0), (0, -1)))
    passed, back = x_split(away, 1), x_split(there, -1)
    away, in_near = tie(away, in_near)
    in_here = jnp.stack([weight_in, in_near])
    conv_both, in_here = tie(conv_both, in_here)
    in_above, in_below = z_shift(in_here, -1), z_shift(in_here, 1)
    further, own = hid_partial(place, conv_both, out_blocks, out_beside, ((0, 1), (0, 0)))
    passed, own, in_above, in_below = tie(passed, own, in_above, in_below)
    further = x_split(add([further, passed]).astype(BF16), 1)
    in_across = onward(in_above, in_below, core, z_split)
    wout = dot(hidden_full, grad_conv, 0, 0).astype(BF16)
    further, wout = tie(further, wout)
    total = add([own, back, further])
    crossed, in_across = tie(y_hi_swap(total[1].astype(BF16)), in_across)
    in_blocks = [in_here, in_above, in_below, in_across]
    grad_hid = add([total[0], crossed])
    alive = (pre_chip > 0) & (gain_chip[1] > 0)[None, :]
    grad_pre = jnp.where(alive, grad_hid, 0.0)
    mid_part = jnp.sum(grad_pre * pre_chip, axis=0).reshape(2, 128)
    grad_act = (grad_pre * mid_gain).astype(BF16)
    act_near = y_hi_swap(grad_act)
    act_above, act_below = x_shift(grad_act, -1), x_shift(grad_act, 1)
    act_near, wout = tie(act_near, wout)
    wout = lax.psum_scatter(wout, "row", scatter_dimension=0, tiled=True)
    near_above, near_below = x_shift(act_near, -1), x_shift(act_near, 1)

    mid_own = lax.dynamic_index_in_dim(mid_part, core, 0, keepdims=False)
    mid_away = lax.dynamic_index_in_dim(mid_part, 1 - core, 0, keepdims=False)
    mid_own = mid_own + core_swap(mid_away)
    sums = jnp.concatenate([mid_own, wide_part]).reshape(5, 128)
    sums = sums + z_flip(sums, 1)
    near_above, sums = tie(near_above, sums)
    sums = sums + z_flip(sums, 2)
    sums = sums + y_lo_swap(sums)

    act_across = onward(act_above, act_below, core, x_split)
    near_across = onward(near_above, near_below, core, x_split)
    act = [
        grad_act, act_near, act_above, near_above, act_below, near_below, act_across, near_across
    ]
    act_beside = [core_swap(block) for block in act]

    away, there, further, own = win_partial(place, input_turned, act, act_beside)
    passed, back = z_split(away, 1), z_split(there, -1)
    grad_x = out_gradient(place, cotangent, act, act_beside, in_blocks)
    passed, grad_x = tie(passed, grad_x)
    further = z_split(add([further, passed]).astype(BF16), 1)
    grad_wout = wout.astype(F32) * scaling
    further, grad_wout, sums = tie(further, grad_wout, sums)
    total = add([own, back, further])
    grad_win = add([total[0], y_lo_swap(total[1].astype(BF16))]) * scaling
    grad_smid = keep_mid.astype(F32) * scaling * sums[0]
    grad_swide = keep_wide.astype(F32) * scaling * sums[1:].reshape(512)
    return (grad_x, grad_win, grad_wout, grad_smid, grad_swide)


def solution(mesh):
    return jax.shard_map(
        local,
        mesh=mesh,
        in_specs=(
            P("row", "col"),
            P("row", "col"),
            P("row", "col"),
            P("row", "col"),
            P("col", "row"),
            P("row", "col"),
            P("col"),
            P("col"),
            P("col"),
            P("col"),
        ),
        out_specs=(P("row", "col"), P("col", "row"), P("row", "col"), P("col"), P("col")),
        check_vma=False,
    )
```

```python
import functools
import math

import jax
import jax.numpy as jnp
from jax import lax
from jax.experimental import pallas as pl
from jax.experimental.pallas import tpu as pltpu
from jax.sharding import PartitionSpec as P

F32 = jnp.float32
BF16 = jnp.bfloat16
AXES = ("row", "col")
STEPS = (0, 1, 3, 2)


def permute(v, target):
    pairs = []
    for row in range(8):
        for col in range(16):
            y_lo, z, x, y_hi, core = target(
                row // 4, row % 4, col // 4, (col // 2) % 2, col % 2
            )
            pairs.append(
                (row * 16 + col, (y_lo * 4 + z % 4) * 16 + (x % 4) * 4 + y_hi * 2 + core)
            )
    return lax.ppermute(v, AXES, pairs)


def core_swap(v):
    return permute(v, lambda yl, z, x, yh, c: (yl, z, x, yh, 1 - c))


def y_hi_swap(v):
    return permute(v, lambda yl, z, x, yh, c: (yl, z, x, 1 - yh, c))


def y_lo_swap(v):
    return permute(v, lambda yl, z, x, yh, c: (1 - yl, z, x, yh, c))


def z_flip(v, mask):
    return permute(v, lambda yl, z, x, yh, c: (yl, z ^ mask, x, yh, c))


def x_shift(v, step):
    return permute(v, lambda yl, z, x, yh, c: (yl, z, x + step, yh, c))


def z_shift(v, step):
    return permute(v, lambda yl, z, x, yh, c: (yl, z + step, x, yh, c))


def x_split(v, way):
    return permute(v, lambda yl, z, x, yh, c: (yl, z, x + way * (1 - 2 * c), yh, c))


def z_split(v, way):
    return permute(v, lambda yl, z, x, yh, c: (yl, z + way * (1 - 2 * c), x, yh, c))


def dot(a, b, ca, cb):
    return lax.dot_general(a, b, (((ca,), (cb,)), ((), ())), preferred_element_type=F32)


def onward(above, below, core, split):
    return split(jnp.where(core == 0, below, above), 1)


def place_of(v):
    row, col = v[0], v[1]
    return row, row >> 2, row & 3, col >> 2, (col >> 1) & 1, col & 1


def slot_of(step):
    step = step & 3
    return jnp.where(step >= 2, 5 - step, step)


def row_slot(block, y_lo, z):
    return slot_of((block & 3) - z) * 2 + ((block >> 2) ^ y_lo)


def hidden_slot(block, x, y_hi):
    return slot_of((block >> 1) - x) * 2 + ((block & 1) ^ y_hi)


def call(body, outs, out_space, scratch, sems, loads, flops, here, vmem_args, any_args):
    vmem = pl.BlockSpec(memory_space=pltpu.VMEM)
    return pl.pallas_call(
        body,
        out_shape=outs,
        in_specs=[pl.BlockSpec(memory_space=pltpu.SMEM)]
        + [vmem] * len(vmem_args)
        + [pl.BlockSpec(memory_space=pl.ANY)] * len(any_args),
        out_specs=[pl.BlockSpec(memory_space=out_space)] * len(outs),
        scratch_shapes=[*scratch, pltpu.SemaphoreType.DMA((sems,))],
        compiler_params=pltpu.CompilerParams(vmem_limit_bytes=60 * 1024 * 1024),
        cost_estimate=pl.CostEstimate(flops=flops, bytes_accessed=loads, transcendentals=0),
    )(here, *vmem_args, *any_args)


def hid_kernel(ways, here, conv, *refs):
    blocks, outs, (held, sems) = refs[:16], refs[16:18], refs[18:]
    copies = [
        pltpu.make_async_copy(
            ref, held.at[k % 8, :, pl.ds((k // 8) * 512, 512)], sems.at[k]
        )
        for k, ref in enumerate(blocks)
    ]
    for copy in copies:
        copy.start()
    row, y_lo, z, x, y_hi, core = place_of(here)
    ahead = 1 - 2 * core
    for copy in copies:
        copy.wait()
    for j in range(4):
        fixed, way = ways[j // 2]
        block = ((x + fixed + way * ahead) & 3) * 2 + (y_hi ^ (j % 2))
        outs[j // 2][j % 2] = lax.dot_general(
            conv[...], held[row_slot(block, y_lo, z)], (((1,), (1,)), ((), ())),
            preferred_element_type=F32,
        ).astype(BF16)


def hid_partial(here, conv, blocks, beside, ways):
    return call(
        functools.partial(hid_kernel, ways), [jax.ShapeDtypeStruct((2, 768, 256), BF16)] * 2,
        pltpu.VMEM, [pltpu.VMEM((8, 256, 1024), BF16)], 16, 8 << 20, 768 * 1024 * 2048, here,
        [conv], [*blocks, *beside],
    )


def act_copies(own, beside, at, sems, first, core):
    copies = []
    for part, ref in enumerate((own, beside)):
        rows = pl.ds(pl.multiple_of((core ^ part) * 768, 768), 768)
        copies.append(pltpu.make_async_copy(ref, at(rows), sems.at[first + part]))
    return copies


def win_kernel(here, left, *refs):
    blocks, outs, (held, sems) = refs[:16], refs[16:20], refs[20:]
    row, y_lo, z, x, y_hi, core = place_of(here)
    copies = []
    for k in range(8):
        copies += act_copies(
            blocks[k], blocks[8 + k], lambda rows, k=k: held.at[k, rows, :], sems, 2 * k, core
        )
    for copy in copies:
        copy.start()
    for copy in copies:
        copy.wait()
    ahead = 1 - 2 * core
    for j in range(8):
        step = (2, -ahead, ahead, 0)[j // 2]
        block = (y_lo ^ (j % 2)) * 4 + ((z + step) & 3)
        outs[j // 2][j % 2] = jnp.dot(
            left[...], held[hidden_slot(block, x, y_hi)], preferred_element_type=F32
        ).astype(BF16)


def win_partial(here, left, blocks, beside):
    return call(
        win_kernel, [jax.ShapeDtypeStruct((2, 512, 256), BF16)] * 4, pltpu.VMEM,
        [pltpu.VMEM((8, 1536, 256), BF16)], 16, 10 << 20, 2 * 512 * 1536 * 2048, here, [left],
        [*blocks, *beside],
    )


def out_kernel(here, cot, *refs):
    blocks, parts, out = refs[:16], refs[16:20], refs[20]
    held, weights, sems = refs[21:]
    row, y_lo, z, x, y_hi, core = place_of(here)
    copies = [
        pltpu.make_async_copy(ref, weights.at[pl.ds(k * 2, 2)], sems.at[16 + k])
        for k, ref in enumerate(parts)
    ]
    for k in range(8):
        copies += act_copies(
            blocks[k], blocks[8 + k], lambda rows, k=k: held.at[k, rows, :], sems, 2 * k, core
        )
    for copy in copies:
        copy.start()
    for copy in copies:
        copy.wait()
    for at in range(0, 1536, 256):
        total = cot[at : at + 256, :].astype(F32)
        for block in range(8):
            total = total + lax.dot_general(
                held[hidden_slot(block, x, y_hi), at : at + 256, :],
                weights[row_slot(block, y_lo, z)],
                (((1,), (1,)), ((), ())),
                preferred_element_type=F32,
            )
        out[at : at + 256, :] = total.astype(BF16)


def out_gradient(here, cot, blocks, beside, weights):
    return call(
        out_kernel, [jax.ShapeDtypeStruct((1536, 512), BF16)], pltpu.VMEM,
        [pltpu.VMEM((8, 1536, 256), BF16), pltpu.VMEM((8, 512, 256), BF16)], 20, 12 << 20,
        2 * 1536 * 512 * 2048, here, [cot], [*blocks, *beside, *weights],
    )[0]


def tie(*values):
    return lax.optimization_barrier(values)


def add(terms):
    return sum(term.astype(F32) for term in terms)


def local(
    inputs,
    cotangent,
    conv_out,
    pre_act,
    weight_in,
    weight_out,
    scale_mid,
    scale_wide,
    keep_mid,
    keep_wide,
):
    rows = inputs.shape[0]
    half = rows // 2
    scaling = 1.0 / math.sqrt(rows * lax.axis_size("row"))
    row, col = lax.axis_index("row"), lax.axis_index("col")
    y_lo, z = row // 4, row % 4
    x, y_hi, core = col // 4, (col // 2) % 2, col % 2
    place = jnp.stack([row, col]).astype(jnp.int32)

    def mine(v):
        return lax.dynamic_slice_in_dim(v, core * half, half, 0)

    def theirs(v):
        return lax.dynamic_slice_in_dim(v, (1 - core) * half, half, 0)

    mid_gain = scale_mid * keep_mid.astype(F32)
    hidden = jnp.maximum(pre_act.astype(F32) * mid_gain, 0.0).astype(BF16)
    hidden_full = lax.all_gather(hidden, "col", axis=1, tiled=True)
    out_above, out_below = z_shift(weight_out, -1), z_shift(weight_out, 1)
    out_near = y_lo_swap(weight_out)

    wide_gain = scale_wide * keep_wide.astype(F32)
    cot_float = cotangent.astype(F32)
    grad_conv = (cot_float * wide_gain).astype(BF16)
    wide_part = jnp.sum(cot_float * conv_out.astype(F32), axis=0)
    conv_mine = mine(grad_conv)
    conv_sent, input_turned = theirs(grad_conv), inputs.T
    out_near, conv_sent, input_turned, wide_part, pre_act = tie(
        out_near, conv_sent, input_turned, wide_part, pre_act
    )
    near_above, near_below = z_shift(out_near, -1), z_shift(out_near, 1)
    out_across = onward(out_above, out_below, core, z_split)
    conv_both = jnp.concatenate([conv_mine, core_swap(conv_sent)], axis=1)
    near_above, conv_both, weight_in = tie(near_above, conv_both, weight_in)
    in_near = y_lo_swap(weight_in)
    near_across = onward(near_above, near_below, core, z_split)
    out_blocks = [
        weight_out, out_near, out_above, near_above, out_below, near_below, out_across, near_across
    ]

    gain_pair = jnp.stack([scale_mid, keep_mid.astype(F32)])
    gain_beside = core_swap(gain_pair)
    pre_mine = mine(pre_act)
    pre_beside = core_swap(theirs(pre_act))

    def chip_order(a, b):
        return jnp.concatenate(
            [jnp.where(core == 0, a, b), jnp.where(core == 0, b, a)], axis=1
        )

    pre_chip = chip_order(pre_mine, pre_beside).astype(F32)
    gain_chip = chip_order(gain_pair, gain_beside)
    mid_gain = gain_chip[0] * gain_chip[1]

    out_beside = [core_swap(block) for block in out_blocks]
    away, there = hid_partial(place, conv_both, out_blocks, out_beside, ((2, 0), (0, -1)))
    passed, back = x_split(away, 1), x_split(there, -1)
    away, in_near = tie(away, in_near)
    in_here = jnp.stack([weight_in, in_near])
    conv_both, in_here = tie(conv_both, in_here)
    in_above, in_below = z_shift(in_here, -1), z_shift(in_here, 1)
    further, own = hid_partial(place, conv_both, out_blocks, out_beside, ((0, 1), (0, 0)))
    passed, own, in_above, in_below = tie(passed, own, in_above, in_below)
    further = x_split(add([further, passed]).astype(BF16), 1)
    in_across = onward(in_above, in_below, core, z_split)
    total = add([own, back, further])
    wout = dot(hidden_full, grad_conv, 0, 0).astype(BF16)
    crossed, wout, in_across = tie(y_hi_swap(total[1].astype(BF16)), wout, in_across)
    in_blocks = [in_here, in_above, in_below, in_across]
    grad_hid = add([total[0], crossed])
    alive = (pre_chip > 0) & (gain_chip[1] > 0)[None, :]
    grad_pre = jnp.where(alive, grad_hid, 0.0)
    mid_part = jnp.sum(grad_pre * pre_chip, axis=0).reshape(2, 128)
    grad_act = (grad_pre * mid_gain).astype(BF16)
    act_near = y_hi_swap(grad_act)
    act_above, act_below = x_shift(grad_act, -1), x_shift(grad_act, 1)
    act_near, wout = tie(act_near, wout)
    wout = lax.psum_scatter(wout, "row", scatter_dimension=0, tiled=True)
    near_above, near_below = x_shift(act_near, -1), x_shift(act_near, 1)

    mid_own = lax.dynamic_index_in_dim(mid_part, core, 0, keepdims=False)
    mid_away = lax.dynamic_index_in_dim(mid_part, 1 - core, 0, keepdims=False)
    mid_own = mid_own + core_swap(mid_away)
    sums = jnp.concatenate([mid_own, wide_part]).reshape(5, 128)
    sums = sums + z_flip(sums, 1)
    sums = sums + z_flip(sums, 2)
    sums = sums + y_lo_swap(sums)

    act_across = onward(act_above, act_below, core, x_split)
    near_across = onward(near_above, near_below, core, x_split)
    act = [
        grad_act, act_near, act_above, near_above, act_below, near_below, act_across, near_across
    ]
    act_beside = [core_swap(block) for block in act]
    act[7], sums = tie(act[7], sums)

    away, there, further, own = win_partial(place, input_turned, act, act_beside)
    passed, back = z_split(away, 1), z_split(there, -1)
    grad_x = out_gradient(place, cotangent, act, act_beside, in_blocks)
    passed, grad_x = tie(passed, grad_x)
    further = z_split(add([further, passed]).astype(BF16), 1)
    grad_wout = wout.astype(F32) * scaling
    further, grad_wout = tie(further, grad_wout)
    total = add([own, back, further])
    grad_win = add([total[0], y_lo_swap(total[1].astype(BF16))]) * scaling
    grad_smid = keep_mid.astype(F32) * scaling * sums[0]
    grad_swide = keep_wide.astype(F32) * scaling * sums[1:].reshape(512)
    return (grad_x, grad_win, grad_wout, grad_smid, grad_swide)


def solution(mesh):
    return jax.shard_map(
        local,
        mesh=mesh,
        in_specs=(
            P("row", "col"),
            P("row", "col"),
            P("row", "col"),
            P("row", "col"),
            P("col", "row"),
            P("row", "col"),
            P("col"),
            P("col"),
            P("col"),
            P("col"),
        ),
        out_specs=(P("row", "col"), P("col", "row"), P("row", "col"), P("col"), P("col")),
        check_vma=False,
    )
```

```python
import functools
import math

import jax
import jax.numpy as jnp
from jax import lax
from jax.experimental import pallas as pl
from jax.experimental.pallas import tpu as pltpu
from jax.sharding import PartitionSpec as P

F32 = jnp.float32
BF16 = jnp.bfloat16
AXES = ("row", "col")
STEPS = (0, 1, 3, 2)


def permute(v, target):
    pairs = []
    for row in range(8):
        for col in range(16):
            y_lo, z, x, y_hi, core = target(
                row // 4, row % 4, col // 4, (col // 2) % 2, col % 2
            )
            pairs.append(
                (row * 16 + col, (y_lo * 4 + z % 4) * 16 + (x % 4) * 4 + y_hi * 2 + core)
            )
    return lax.ppermute(v, AXES, pairs)


def core_swap(v):
    return permute(v, lambda yl, z, x, yh, c: (yl, z, x, yh, 1 - c))


def y_hi_swap(v):
    return permute(v, lambda yl, z, x, yh, c: (yl, z, x, 1 - yh, c))


def y_lo_swap(v):
    return permute(v, lambda yl, z, x, yh, c: (1 - yl, z, x, yh, c))


def z_flip(v, mask):
    return permute(v, lambda yl, z, x, yh, c: (yl, z ^ mask, x, yh, c))


def x_shift(v, step):
    return permute(v, lambda yl, z, x, yh, c: (yl, z, x + step, yh, c))


def z_shift(v, step):
    return permute(v, lambda yl, z, x, yh, c: (yl, z + step, x, yh, c))


def x_split(v, way):
    return permute(v, lambda yl, z, x, yh, c: (yl, z, x + way * (1 - 2 * c), yh, c))


def z_split(v, way):
    return permute(v, lambda yl, z, x, yh, c: (yl, z + way * (1 - 2 * c), x, yh, c))


def dot(a, b, ca, cb):
    return lax.dot_general(a, b, (((ca,), (cb,)), ((), ())), preferred_element_type=F32)


def onward(above, below, core, split):
    return split(jnp.where(core == 0, below, above), 1)


def place_of(v):
    row, col = v[0], v[1]
    return row, row >> 2, row & 3, col >> 2, (col >> 1) & 1, col & 1


def slot_of(step):
    step = step & 3
    return jnp.where(step >= 2, 5 - step, step)


def row_slot(block, y_lo, z):
    return slot_of((block & 3) - z) * 2 + ((block >> 2) ^ y_lo)


def hidden_slot(block, x, y_hi):
    return slot_of((block >> 1) - x) * 2 + ((block & 1) ^ y_hi)


def call(body, outs, out_space, scratch, sems, loads, flops, here, vmem_args, any_args):
    vmem = pl.BlockSpec(memory_space=pltpu.VMEM)
    return pl.pallas_call(
        body,
        out_shape=outs,
        in_specs=[pl.BlockSpec(memory_space=pltpu.SMEM)]
        + [vmem] * len(vmem_args)
        + [pl.BlockSpec(memory_space=pl.ANY)] * len(any_args),
        out_specs=[pl.BlockSpec(memory_space=out_space)] * len(outs),
        scratch_shapes=[*scratch, pltpu.SemaphoreType.DMA((sems,))],
        compiler_params=pltpu.CompilerParams(vmem_limit_bytes=60 * 1024 * 1024),
        cost_estimate=pl.CostEstimate(flops=flops, bytes_accessed=loads, transcendentals=0),
    )(here, *vmem_args, *any_args)


def hid_kernel(ways, here, conv, *refs):
    blocks, outs, (held, sems) = refs[:16], refs[16:18], refs[18:]
    copies = [
        pltpu.make_async_copy(
            ref, held.at[k % 8, :, pl.ds((k // 8) * 512, 512)], sems.at[k]
        )
        for k, ref in enumerate(blocks)
    ]
    for copy in copies:
        copy.start()
    row, y_lo, z, x, y_hi, core = place_of(here)
    ahead = 1 - 2 * core
    for copy in copies:
        copy.wait()
    for j in range(4):
        fixed, way = ways[j // 2]
        block = ((x + fixed + way * ahead) & 3) * 2 + (y_hi ^ (j % 2))
        outs[j // 2][j % 2] = lax.dot_general(
            conv[...], held[row_slot(block, y_lo, z)], (((1,), (1,)), ((), ())),
            preferred_element_type=F32,
        ).astype(BF16)


def hid_partial(here, conv, blocks, beside, ways):
    return call(
        functools.partial(hid_kernel, ways), [jax.ShapeDtypeStruct((2, 768, 256), BF16)] * 2,
        pltpu.VMEM, [pltpu.VMEM((8, 256, 1024), BF16)], 16, 8 << 20, 768 * 1024 * 2048, here,
        [conv], [*blocks, *beside],
    )


def act_copies(own, beside, at, sems, first, core):
    copies = []
    for part, ref in enumerate((own, beside)):
        rows = pl.ds(pl.multiple_of((core ^ part) * 768, 768), 768)
        copies.append(pltpu.make_async_copy(ref, at(rows), sems.at[first + part]))
    return copies


def win_kernel(here, left, *refs):
    blocks, outs, (held, sems) = refs[:16], refs[16:20], refs[20:]
    row, y_lo, z, x, y_hi, core = place_of(here)
    copies = []
    for k in range(8):
        copies += act_copies(
            blocks[k], blocks[8 + k], lambda rows, k=k: held.at[k, rows, :], sems, 2 * k, core
        )
    for copy in copies:
        copy.start()
    for copy in copies:
        copy.wait()
    ahead = 1 - 2 * core
    for j in range(8):
        step = (2, -ahead, ahead, 0)[j // 2]
        block = (y_lo ^ (j % 2)) * 4 + ((z + step) & 3)
        outs[j // 2][j % 2] = jnp.dot(
            left[...], held[hidden_slot(block, x, y_hi)], preferred_element_type=F32
        ).astype(BF16)


def win_partial(here, left, blocks, beside):
    return call(
        win_kernel, [jax.ShapeDtypeStruct((2, 512, 256), BF16)] * 4, pltpu.VMEM,
        [pltpu.VMEM((8, 1536, 256), BF16)], 16, 10 << 20, 2 * 512 * 1536 * 2048, here, [left],
        [*blocks, *beside],
    )


def out_kernel(here, cot, *refs):
    blocks, parts, out = refs[:16], refs[16:20], refs[20]
    held, weights, sems = refs[21:]
    row, y_lo, z, x, y_hi, core = place_of(here)
    copies = [
        pltpu.make_async_copy(ref, weights.at[pl.ds(k * 2, 2)], sems.at[16 + k])
        for k, ref in enumerate(parts)
    ]
    for k in range(8):
        copies += act_copies(
            blocks[k], blocks[8 + k], lambda rows, k=k: held.at[k, rows, :], sems, 2 * k, core
        )
    for copy in copies:
        copy.start()
    for copy in copies:
        copy.wait()
    for at in range(0, 1536, 256):
        total = cot[at : at + 256, :].astype(F32)
        for block in range(8):
            total = total + lax.dot_general(
                held[hidden_slot(block, x, y_hi), at : at + 256, :],
                weights[row_slot(block, y_lo, z)],
                (((1,), (1,)), ((), ())),
                preferred_element_type=F32,
            )
        out[at : at + 256, :] = total.astype(BF16)


def out_gradient(here, cot, blocks, beside, weights):
    return call(
        out_kernel, [jax.ShapeDtypeStruct((1536, 512), BF16)], pltpu.VMEM,
        [pltpu.VMEM((8, 1536, 256), BF16), pltpu.VMEM((8, 512, 256), BF16)], 20, 12 << 20,
        2 * 1536 * 512 * 2048, here, [cot], [*blocks, *beside, *weights],
    )[0]


def tie(*values):
    return lax.optimization_barrier(values)


def add(terms):
    return sum(term.astype(F32) for term in terms)


def local(
    inputs,
    cotangent,
    conv_out,
    pre_act,
    weight_in,
    weight_out,
    scale_mid,
    scale_wide,
    keep_mid,
    keep_wide,
):
    rows = inputs.shape[0]
    half = rows // 2
    scaling = 1.0 / math.sqrt(rows * lax.axis_size("row"))
    row, col = lax.axis_index("row"), lax.axis_index("col")
    y_lo, z = row // 4, row % 4
    x, y_hi, core = col // 4, (col // 2) % 2, col % 2
    place = jnp.stack([row, col]).astype(jnp.int32)

    def mine(v):
        return lax.dynamic_slice_in_dim(v, core * half, half, 0)

    def theirs(v):
        return lax.dynamic_slice_in_dim(v, (1 - core) * half, half, 0)

    mid_gain = scale_mid * keep_mid.astype(F32)
    hidden = jnp.maximum(pre_act.astype(F32) * mid_gain, 0.0).astype(BF16)
    hidden_full = lax.all_gather(hidden, "col", axis=1, tiled=True)
    out_above, out_below = z_shift(weight_out, -1), z_shift(weight_out, 1)
    out_near = y_lo_swap(weight_out)

    wide_gain = scale_wide * keep_wide.astype(F32)
    cot_float = cotangent.astype(F32)
    grad_conv = (cot_float * wide_gain).astype(BF16)
    wide_part = jnp.sum(cot_float * conv_out.astype(F32), axis=0)
    conv_mine = mine(grad_conv)
    conv_sent, input_turned = theirs(grad_conv), inputs.T
    out_near, conv_sent, input_turned, wide_part, pre_act = tie(
        out_near, conv_sent, input_turned, wide_part, pre_act
    )
    near_above, near_below = z_shift(out_near, -1), z_shift(out_near, 1)
    out_across = onward(out_above, out_below, core, z_split)
    conv_both = jnp.concatenate([conv_mine, core_swap(conv_sent)], axis=1)
    near_above, conv_both, weight_in = tie(near_above, conv_both, weight_in)
    in_near = y_lo_swap(weight_in)
    near_across = onward(near_above, near_below, core, z_split)
    out_blocks = [
        weight_out, out_near, out_above, near_above, out_below, near_below, out_across, near_across
    ]

    gain_pair = jnp.stack([scale_mid, keep_mid.astype(F32)])
    gain_beside = core_swap(gain_pair)
    pre_mine = mine(pre_act)
    pre_beside = core_swap(theirs(pre_act))

    def chip_order(a, b):
        return jnp.concatenate(
            [jnp.where(core == 0, a, b), jnp.where(core == 0, b, a)], axis=1
        )

    pre_chip = chip_order(pre_mine, pre_beside).astype(F32)
    gain_chip = chip_order(gain_pair, gain_beside)
    mid_gain = gain_chip[0] * gain_chip[1]

    out_beside = [core_swap(block) for block in out_blocks]
    away, there = hid_partial(place, conv_both, out_blocks, out_beside, ((2, 0), (0, -1)))
    passed, back = x_split(away, 1), x_split(there, -1)
    away, in_near = tie(away, in_near)
    in_here = jnp.stack([weight_in, in_near])
    conv_both, in_here = tie(conv_both, in_here)
    in_above, in_below = z_shift(in_here, -1), z_shift(in_here, 1)
    further, own = hid_partial(place, conv_both, out_blocks, out_beside, ((0, 1), (0, 0)))
    passed, back, own, in_above, in_below = tie(passed, back, own, in_above, in_below)
    further = x_split(add([further, passed]).astype(BF16), 1)
    in_across = onward(in_above, in_below, core, z_split)
    total = add([own, back, further])
    wout = dot(hidden_full, grad_conv, 0, 0).astype(BF16)
    crossed, wout, in_across = tie(y_hi_swap(total[1].astype(BF16)), wout, in_across)
    in_blocks = [in_here, in_above, in_below, in_across]
    grad_hid = add([total[0], crossed])
    alive = (pre_chip > 0) & (gain_chip[1] > 0)[None, :]
    grad_pre = jnp.where(alive, grad_hid, 0.0)
    mid_part = jnp.sum(grad_pre * pre_chip, axis=0).reshape(2, 128)
    grad_act = (grad_pre * mid_gain).astype(BF16)
    act_near = y_hi_swap(grad_act)
    act_above, act_below = x_shift(grad_act, -1), x_shift(grad_act, 1)
    act_near, act_above, act_below, wout, mid_part = tie(
        act_near, act_above, act_below, wout, mid_part
    )
    wout = lax.psum_scatter(wout, "row", scatter_dimension=0, tiled=True)
    near_above, near_below = x_shift(act_near, -1), x_shift(act_near, 1)

    mid_own = lax.dynamic_index_in_dim(mid_part, core, 0, keepdims=False)
    mid_away = lax.dynamic_index_in_dim(mid_part, 1 - core, 0, keepdims=False)
    mid_own = mid_own + core_swap(mid_away)
    sums = jnp.concatenate([mid_own, wide_part]).reshape(5, 128)
    sums = sums + z_flip(sums, 1)

    act_across = onward(act_above, act_below, core, x_split)
    near_above, near_below, act_across, sums = tie(near_above, near_below, act_across, sums)
    sums = sums + z_flip(sums, 2)
    near_across = onward(near_above, near_below, core, x_split)
    act = [
        grad_act, act_near, act_above, near_above, act_below, near_below, act_across, near_across
    ]
    act_beside = [core_swap(block) for block in act]
    act[7], sums = tie(act[7], sums)
    sums = sums + y_lo_swap(sums)

    away, there, further, own = win_partial(place, input_turned, act, act_beside)
    passed, back = z_split(away, 1), z_split(there, -1)
    grad_x = out_gradient(place, cotangent, act, act_beside, in_blocks)
    passed, back, grad_x, sums = tie(passed, back, grad_x, sums)
    further = z_split(add([further, passed]).astype(BF16), 1)
    grad_wout = wout.astype(F32) * scaling
    further, grad_wout = tie(further, grad_wout)
    total = add([own, back, further])
    grad_win = add([total[0], y_lo_swap(total[1].astype(BF16))]) * scaling
    grad_smid = keep_mid.astype(F32) * scaling * sums[0]
    grad_swide = keep_wide.astype(F32) * scaling * sums[1:].reshape(512)
    return (grad_x, grad_win, grad_wout, grad_smid, grad_swide)


def solution(mesh):
    return jax.shard_map(
        local,
        mesh=mesh,
        in_specs=(
            P("row", "col"),
            P("row", "col"),
            P("row", "col"),
            P("row", "col"),
            P("col", "row"),
            P("row", "col"),
            P("col"),
            P("col"),
            P("col"),
            P("col"),
        ),
        out_specs=(P("row", "col"), P("col", "row"), P("row", "col"), P("col"), P("col")),
        check_vma=False,
    )
```

```python
import functools
import math

import jax
import jax.numpy as jnp
from jax import lax
from jax.experimental import pallas as pl
from jax.experimental.pallas import tpu as pltpu
from jax.sharding import PartitionSpec as P

F32 = jnp.float32
BF16 = jnp.bfloat16
AXES = ("row", "col")
STEPS = (0, 1, 3, 2)


def permute(v, target):
    pairs = []
    for row in range(8):
        for col in range(16):
            y_lo, z, x, y_hi, core = target(
                row // 4, row % 4, col // 4, (col // 2) % 2, col % 2
            )
            pairs.append(
                (row * 16 + col, (y_lo * 4 + z % 4) * 16 + (x % 4) * 4 + y_hi * 2 + core)
            )
    return lax.ppermute(v, AXES, pairs)


def core_swap(v):
    return permute(v, lambda yl, z, x, yh, c: (yl, z, x, yh, 1 - c))


def y_hi_swap(v):
    return permute(v, lambda yl, z, x, yh, c: (yl, z, x, 1 - yh, c))


def y_lo_swap(v):
    return permute(v, lambda yl, z, x, yh, c: (1 - yl, z, x, yh, c))


def z_flip(v, mask):
    return permute(v, lambda yl, z, x, yh, c: (yl, z ^ mask, x, yh, c))


def x_shift(v, step):
    return permute(v, lambda yl, z, x, yh, c: (yl, z, x + step, yh, c))


def z_shift(v, step):
    return permute(v, lambda yl, z, x, yh, c: (yl, z + step, x, yh, c))


def x_split(v, way):
    return permute(v, lambda yl, z, x, yh, c: (yl, z, x + way * (1 - 2 * c), yh, c))


def z_split(v, way):
    return permute(v, lambda yl, z, x, yh, c: (yl, z + way * (1 - 2 * c), x, yh, c))


def dot(a, b, ca, cb):
    return lax.dot_general(a, b, (((ca,), (cb,)), ((), ())), preferred_element_type=F32)


def onward(above, below, core, split):
    return split(jnp.where(core == 0, below, above), 1)


def place_of(v):
    row, col = v[0], v[1]
    return row, row >> 2, row & 3, col >> 2, (col >> 1) & 1, col & 1


def slot_of(step):
    step = step & 3
    return jnp.where(step >= 2, 5 - step, step)


def row_slot(block, y_lo, z):
    return slot_of((block & 3) - z) * 2 + ((block >> 2) ^ y_lo)


def hidden_slot(block, x, y_hi):
    return slot_of((block >> 1) - x) * 2 + ((block & 1) ^ y_hi)


def call(body, outs, out_space, scratch, sems, loads, flops, here, vmem_args, any_args):
    vmem = pl.BlockSpec(memory_space=pltpu.VMEM)
    return pl.pallas_call(
        body,
        out_shape=outs,
        in_specs=[pl.BlockSpec(memory_space=pltpu.SMEM)]
        + [vmem] * len(vmem_args)
        + [pl.BlockSpec(memory_space=pl.ANY)] * len(any_args),
        out_specs=[pl.BlockSpec(memory_space=out_space)] * len(outs),
        scratch_shapes=[*scratch, pltpu.SemaphoreType.DMA((sems,))],
        compiler_params=pltpu.CompilerParams(vmem_limit_bytes=60 * 1024 * 1024),
        cost_estimate=pl.CostEstimate(flops=flops, bytes_accessed=loads, transcendentals=0),
    )(here, *vmem_args, *any_args)


def hid_kernel(ways, here, conv, *refs):
    blocks, outs, (held, sems) = refs[:16], refs[16:18], refs[18:]
    copies = [
        pltpu.make_async_copy(
            ref, held.at[k % 8, :, pl.ds((k // 8) * 512, 512)], sems.at[k]
        )
        for k, ref in enumerate(blocks)
    ]
    for copy in copies:
        copy.start()
    row, y_lo, z, x, y_hi, core = place_of(here)
    ahead = 1 - 2 * core
    for copy in copies:
        copy.wait()
    for j in range(4):
        fixed, way = ways[j // 2]
        block = ((x + fixed + way * ahead) & 3) * 2 + (y_hi ^ (j % 2))
        outs[j // 2][j % 2] = lax.dot_general(
            conv[...], held[row_slot(block, y_lo, z)], (((1,), (1,)), ((), ())),
            preferred_element_type=F32,
        ).astype(BF16)


def hid_partial(here, conv, blocks, beside, ways):
    return call(
        functools.partial(hid_kernel, ways), [jax.ShapeDtypeStruct((2, 768, 256), BF16)] * 2,
        pltpu.VMEM, [pltpu.VMEM((8, 256, 1024), BF16)], 16, 8 << 20, 768 * 1024 * 2048, here,
        [conv], [*blocks, *beside],
    )


def act_copies(own, beside, at, sems, first, core):
    copies = []
    for part, ref in enumerate((own, beside)):
        rows = pl.ds(pl.multiple_of((core ^ part) * 768, 768), 768)
        copies.append(pltpu.make_async_copy(ref, at(rows), sems.at[first + part]))
    return copies


def win_kernel(here, left, *refs):
    blocks, outs, (held, sems) = refs[:16], refs[16:20], refs[20:]
    row, y_lo, z, x, y_hi, core = place_of(here)
    copies = []
    for k in range(8):
        copies += act_copies(
            blocks[k], blocks[8 + k], lambda rows, k=k: held.at[k, rows, :], sems, 2 * k, core
        )
    for copy in copies:
        copy.start()
    for copy in copies:
        copy.wait()
    ahead = 1 - 2 * core
    for j in range(8):
        step = (2, -ahead, ahead, 0)[j // 2]
        block = (y_lo ^ (j % 2)) * 4 + ((z + step) & 3)
        outs[j // 2][j % 2] = jnp.dot(
            left[...], held[hidden_slot(block, x, y_hi)], preferred_element_type=F32
        ).astype(BF16)


def win_partial(here, left, blocks, beside):
    return call(
        win_kernel, [jax.ShapeDtypeStruct((2, 512, 256), BF16)] * 4, pltpu.VMEM,
        [pltpu.VMEM((8, 1536, 256), BF16)], 16, 10 << 20, 2 * 512 * 1536 * 2048, here, [left],
        [*blocks, *beside],
    )


def out_kernel(here, cot, *refs):
    blocks, parts, out = refs[:16], refs[16:20], refs[20]
    held, weights, sems = refs[21:]
    row, y_lo, z, x, y_hi, core = place_of(here)
    copies = [
        pltpu.make_async_copy(ref, weights.at[pl.ds(k * 2, 2)], sems.at[16 + k])
        for k, ref in enumerate(parts)
    ]
    for k in range(8):
        copies += act_copies(
            blocks[k], blocks[8 + k], lambda rows, k=k: held.at[k, rows, :], sems, 2 * k, core
        )
    for copy in copies:
        copy.start()
    for copy in copies:
        copy.wait()
    for at in range(0, 1536, 256):
        total = cot[at : at + 256, :].astype(F32)
        for block in range(8):
            total = total + lax.dot_general(
                held[hidden_slot(block, x, y_hi), at : at + 256, :],
                weights[row_slot(block, y_lo, z)],
                (((1,), (1,)), ((), ())),
                preferred_element_type=F32,
            )
        out[at : at + 256, :] = total.astype(BF16)


def out_gradient(here, cot, blocks, beside, weights):
    return call(
        out_kernel, [jax.ShapeDtypeStruct((1536, 512), BF16)], pltpu.VMEM,
        [pltpu.VMEM((8, 1536, 256), BF16), pltpu.VMEM((8, 512, 256), BF16)], 20, 12 << 20,
        2 * 1536 * 512 * 2048, here, [cot], [*blocks, *beside, *weights],
    )[0]


def tie(*values):
    return lax.optimization_barrier(values)


def add(terms):
    return sum(term.astype(F32) for term in terms)


def local(
    inputs,
    cotangent,
    conv_out,
    pre_act,
    weight_in,
    weight_out,
    scale_mid,
    scale_wide,
    keep_mid,
    keep_wide,
):
    rows = inputs.shape[0]
    half = rows // 2
    scaling = 1.0 / math.sqrt(rows * lax.axis_size("row"))
    row, col = lax.axis_index("row"), lax.axis_index("col")
    y_lo, z = row // 4, row % 4
    x, y_hi, core = col // 4, (col // 2) % 2, col % 2
    place = jnp.stack([row, col]).astype(jnp.int32)

    def mine(v):
        return lax.dynamic_slice_in_dim(v, core * half, half, 0)

    def theirs(v):
        return lax.dynamic_slice_in_dim(v, (1 - core) * half, half, 0)

    mid_gain = scale_mid * keep_mid.astype(F32)
    hidden = jnp.maximum(pre_act.astype(F32) * mid_gain, 0.0).astype(BF16)
    hidden_full = lax.all_gather(hidden, "col", axis=1, tiled=True)
    out_above, out_below = z_shift(weight_out, -1), z_shift(weight_out, 1)
    out_near = y_lo_swap(weight_out)

    wide_gain = scale_wide * keep_wide.astype(F32)
    cot_float = cotangent.astype(F32)
    grad_conv = (cot_float * wide_gain).astype(BF16)
    wide_part = jnp.sum(cot_float * conv_out.astype(F32), axis=0)
    conv_mine = mine(grad_conv)
    conv_sent, input_turned = theirs(grad_conv), inputs.T
    out_near, out_above, out_below, conv_sent, pre_act, weight_in = tie(
        out_near, out_above, out_below, conv_sent, pre_act, weight_in
    )
    near_above, near_below = z_shift(out_near, -1), z_shift(out_near, 1)
    out_across = onward(out_above, out_below, core, z_split)
    in_near = y_lo_swap(weight_in)
    conv_both = jnp.concatenate([conv_mine, core_swap(conv_sent)], axis=1)
    near_above, near_below, out_across, conv_both, in_near, input_turned, wide_part, place = tie(
        near_above, near_below, out_across, conv_both, in_near, input_turned, wide_part, place
    )
    near_across = onward(near_above, near_below, core, z_split)
    in_here = jnp.stack([weight_in, in_near])
    out_blocks = [
        weight_out, out_near, out_above, near_above, out_below, near_below, out_across, near_across
    ]

    gain_pair = jnp.stack([scale_mid, keep_mid.astype(F32)])
    gain_beside = core_swap(gain_pair)
    pre_mine = mine(pre_act)
    pre_beside = core_swap(theirs(pre_act))

    def chip_order(a, b):
        return jnp.concatenate(
            [jnp.where(core == 0, a, b), jnp.where(core == 0, b, a)], axis=1
        )

    pre_chip = chip_order(pre_mine, pre_beside).astype(F32)
    gain_chip = chip_order(gain_pair, gain_beside)
    mid_gain = gain_chip[0] * gain_chip[1]

    out_beside = [core_swap(block) for block in out_blocks]
    near_across, in_here = tie(near_across, in_here)
    out_blocks[7] = near_across
    away, there = hid_partial(place, conv_both, out_blocks, out_beside, ((2, 0), (0, -1)))
    passed, back = x_split(away, 1), x_split(there, -1)
    in_above, in_below = z_shift(in_here, -1), z_shift(in_here, 1)
    further, own = hid_partial(place, conv_both, out_blocks, out_beside, ((0, 1), (0, 0)))
    passed, back, own, in_above, in_below = tie(passed, back, own, in_above, in_below)
    far = x_split(add([further[1], passed[1]]).astype(BF16), 1)
    near = x_split(add([further[0], passed[0]]).astype(BF16), 1)
    in_across = onward(in_above, in_below, core, z_split)
    wout = dot(hidden_full, grad_conv, 0, 0).astype(BF16)
    crossed = y_hi_swap(add([own[1], back[1], far]).astype(BF16))
    crossed, near, wout, in_across = tie(crossed, near, wout, in_across)
    in_blocks = [in_here, in_above, in_below, in_across]
    grad_hid = add([own[0], back[0], near, crossed])
    alive = (pre_chip > 0) & (gain_chip[1] > 0)[None, :]
    grad_pre = jnp.where(alive, grad_hid, 0.0)
    mid_part = jnp.sum(grad_pre * pre_chip, axis=0).reshape(2, 128)
    grad_act = (grad_pre * mid_gain).astype(BF16)
    act_near = y_hi_swap(grad_act)
    act_above, act_below = x_shift(grad_act, -1), x_shift(grad_act, 1)
    act_near, act_above, act_below, wout, mid_part = tie(
        act_near, act_above, act_below, wout, mid_part
    )
    wout = lax.psum_scatter(wout, "row", scatter_dimension=0, tiled=True)
    near_above, near_below = x_shift(act_near, -1), x_shift(act_near, 1)

    mid_own = lax.dynamic_index_in_dim(mid_part, core, 0, keepdims=False)
    mid_away = lax.dynamic_index_in_dim(mid_part, 1 - core, 0, keepdims=False)
    mid_own = mid_own + core_swap(mid_away)
    sums = jnp.concatenate([mid_own, wide_part]).reshape(5, 128)
    sums = sums + z_flip(sums, 1)

    act_across = onward(act_above, act_below, core, x_split)
    near_above, near_below, act_across, sums = tie(near_above, near_below, act_across, sums)
    sums = sums + z_flip(sums, 2)
    near_across = onward(near_above, near_below, core, x_split)
    act = [
        grad_act, act_near, act_above, near_above, act_below, near_below, act_across, near_across
    ]
    act_beside = [core_swap(block) for block in act]
    act[7], sums = tie(act[7], sums)
    sums = sums + y_lo_swap(sums)

    away, there, further, own = win_partial(place, input_turned, act, act_beside)
    passed, back = z_split(away, 1), z_split(there, -1)
    grad_x = out_gradient(place, cotangent, act, act_beside, in_blocks)
    passed, back, grad_x = tie(passed, back, grad_x)
    far = z_split(add([further[1], passed[1]]).astype(BF16), 1)
    near = z_split(add([further[0], passed[0]]).astype(BF16), 1)
    grad_wout = wout.astype(F32) * scaling
    far, grad_wout, sums = tie(far, grad_wout, sums)
    crossed = y_lo_swap(add([own[1], back[1], far]).astype(BF16))
    grad_win = add([own[0], back[0], near, crossed]) * scaling
    grad_smid = keep_mid.astype(F32) * scaling * sums[0]
    grad_swide = keep_wide.astype(F32) * scaling * sums[1:].reshape(512)
    return (grad_x, grad_win, grad_wout, grad_smid, grad_swide)


def solution(mesh):
    return jax.shard_map(
        local,
        mesh=mesh,
        in_specs=(
            P("row", "col"),
            P("row", "col"),
            P("row", "col"),
            P("row", "col"),
            P("col", "row"),
            P("row", "col"),
            P("col"),
            P("col"),
            P("col"),
            P("col"),
        ),
        out_specs=(P("row", "col"), P("col", "row"), P("row", "col"), P("col"), P("col")),
        check_vma=False,
    )
```

```python
import functools
import math

import jax
import jax.numpy as jnp
from jax import lax
from jax.experimental import pallas as pl
from jax.experimental.pallas import tpu as pltpu
from jax.sharding import PartitionSpec as P

F32 = jnp.float32
BF16 = jnp.bfloat16
AXES = ("row", "col")
STEPS = (0, 1, 3, 2)


def permute(v, target):
    pairs = []
    for row in range(8):
        for col in range(16):
            y_lo, z, x, y_hi, core = target(
                row // 4, row % 4, col // 4, (col // 2) % 2, col % 2
            )
            pairs.append(
                (row * 16 + col, (y_lo * 4 + z % 4) * 16 + (x % 4) * 4 + y_hi * 2 + core)
            )
    return lax.ppermute(v, AXES, pairs)


def core_swap(v):
    return permute(v, lambda yl, z, x, yh, c: (yl, z, x, yh, 1 - c))


def y_hi_swap(v):
    return permute(v, lambda yl, z, x, yh, c: (yl, z, x, 1 - yh, c))


def y_lo_swap(v):
    return permute(v, lambda yl, z, x, yh, c: (1 - yl, z, x, yh, c))


def z_flip(v, mask):
    return permute(v, lambda yl, z, x, yh, c: (yl, z ^ mask, x, yh, c))


def x_shift(v, step):
    return permute(v, lambda yl, z, x, yh, c: (yl, z, x + step, yh, c))


def z_shift(v, step):
    return permute(v, lambda yl, z, x, yh, c: (yl, z + step, x, yh, c))


def x_split(v, way):
    return permute(v, lambda yl, z, x, yh, c: (yl, z, x + way * (1 - 2 * c), yh, c))


def z_split(v, way):
    return permute(v, lambda yl, z, x, yh, c: (yl, z + way * (1 - 2 * c), x, yh, c))


def dot(a, b, ca, cb):
    return lax.dot_general(a, b, (((ca,), (cb,)), ((), ())), preferred_element_type=F32)


def onward(above, below, core, split):
    return split(jnp.where(core == 0, below, above), 1)


def place_of(v):
    row, col = v[0], v[1]
    return row, row >> 2, row & 3, col >> 2, (col >> 1) & 1, col & 1


def slot_of(step):
    step = step & 3
    return jnp.where(step >= 2, 5 - step, step)


def row_slot(block, y_lo, z):
    return slot_of((block & 3) - z) * 2 + ((block >> 2) ^ y_lo)


def hidden_slot(block, x, y_hi):
    return slot_of((block >> 1) - x) * 2 + ((block & 1) ^ y_hi)


def call(body, outs, out_space, scratch, sems, loads, flops, here, vmem_args, any_args):
    vmem = pl.BlockSpec(memory_space=pltpu.VMEM)
    return pl.pallas_call(
        body,
        out_shape=outs,
        in_specs=[pl.BlockSpec(memory_space=pltpu.SMEM)]
        + [vmem] * len(vmem_args)
        + [pl.BlockSpec(memory_space=pl.ANY)] * len(any_args),
        out_specs=[pl.BlockSpec(memory_space=out_space)] * len(outs),
        scratch_shapes=[*scratch, pltpu.SemaphoreType.DMA((sems,))],
        compiler_params=pltpu.CompilerParams(vmem_limit_bytes=60 * 1024 * 1024),
        cost_estimate=pl.CostEstimate(flops=flops, bytes_accessed=loads, transcendentals=0),
    )(here, *vmem_args, *any_args)


def hid_kernel(ways, here, conv, *refs):
    blocks, outs, (held, sems) = refs[:16], refs[16:18], refs[18:]
    copies = [
        pltpu.make_async_copy(
            ref, held.at[k % 8, :, pl.ds((k // 8) * 512, 512)], sems.at[k]
        )
        for k, ref in enumerate(blocks)
    ]
    for copy in copies:
        copy.start()
    row, y_lo, z, x, y_hi, core = place_of(here)
    ahead = 1 - 2 * core
    for copy in copies:
        copy.wait()
    for j in range(4):
        fixed, way = ways[j // 2]
        block = ((x + fixed + way * ahead) & 3) * 2 + (y_hi ^ (j % 2))
        outs[j // 2][j % 2] = lax.dot_general(
            conv[...], held[row_slot(block, y_lo, z)], (((1,), (1,)), ((), ())),
            preferred_element_type=F32,
        ).astype(BF16)


def hid_partial(here, conv, blocks, beside, ways):
    return call(
        functools.partial(hid_kernel, ways), [jax.ShapeDtypeStruct((2, 768, 256), BF16)] * 2,
        pltpu.VMEM, [pltpu.VMEM((8, 256, 1024), BF16)], 16, 8 << 20, 768 * 1024 * 2048, here,
        [conv], [*blocks, *beside],
    )


def act_copies(own, beside, at, sems, first, core):
    copies = []
    for part, ref in enumerate((own, beside)):
        rows = pl.ds(pl.multiple_of((core ^ part) * 768, 768), 768)
        copies.append(pltpu.make_async_copy(ref, at(rows), sems.at[first + part]))
    return copies


def win_kernel(here, left, *refs):
    blocks, outs, (held, sems) = refs[:16], refs[16:20], refs[20:]
    row, y_lo, z, x, y_hi, core = place_of(here)
    copies = []
    for k in range(8):
        copies += act_copies(
            blocks[k], blocks[8 + k], lambda rows, k=k: held.at[k, rows, :], sems, 2 * k, core
        )
    for copy in copies:
        copy.start()
    for copy in copies:
        copy.wait()
    ahead = 1 - 2 * core
    for j in range(8):
        step = (2, -ahead, ahead, 0)[j // 2]
        block = (y_lo ^ (j % 2)) * 4 + ((z + step) & 3)
        outs[j // 2][j % 2] = jnp.dot(
            left[...], held[hidden_slot(block, x, y_hi)], preferred_element_type=F32
        ).astype(BF16)


def win_partial(here, left, blocks, beside):
    return call(
        win_kernel, [jax.ShapeDtypeStruct((2, 512, 256), BF16)] * 4, pltpu.VMEM,
        [pltpu.VMEM((8, 1536, 256), BF16)], 16, 10 << 20, 2 * 512 * 1536 * 2048, here, [left],
        [*blocks, *beside],
    )


def out_kernel(here, cot, *refs):
    blocks, parts, out = refs[:16], refs[16:20], refs[20]
    held, weights, sems = refs[21:]
    row, y_lo, z, x, y_hi, core = place_of(here)
    copies = [
        pltpu.make_async_copy(ref, weights.at[pl.ds(k * 2, 2)], sems.at[16 + k])
        for k, ref in enumerate(parts)
    ]
    for k in range(8):
        copies += act_copies(
            blocks[k], blocks[8 + k], lambda rows, k=k: held.at[k, rows, :], sems, 2 * k, core
        )
    for copy in copies:
        copy.start()
    for copy in copies:
        copy.wait()
    for at in range(0, 1536, 256):
        total = cot[at : at + 256, :].astype(F32)
        for block in range(8):
            total = total + lax.dot_general(
                held[hidden_slot(block, x, y_hi), at : at + 256, :],
                weights[row_slot(block, y_lo, z)],
                (((1,), (1,)), ((), ())),
                preferred_element_type=F32,
            )
        out[at : at + 256, :] = total.astype(BF16)


def out_gradient(here, cot, blocks, beside, weights):
    return call(
        out_kernel, [jax.ShapeDtypeStruct((1536, 512), BF16)], pltpu.VMEM,
        [pltpu.VMEM((8, 1536, 256), BF16), pltpu.VMEM((8, 512, 256), BF16)], 20, 12 << 20,
        2 * 1536 * 512 * 2048, here, [cot], [*blocks, *beside, *weights],
    )[0]


def tie(*values):
    return lax.optimization_barrier(values)


def add(terms):
    return sum(term.astype(F32) for term in terms)


def local(
    inputs,
    cotangent,
    conv_out,
    pre_act,
    weight_in,
    weight_out,
    scale_mid,
    scale_wide,
    keep_mid,
    keep_wide,
):
    rows = inputs.shape[0]
    half = rows // 2
    scaling = 1.0 / math.sqrt(rows * lax.axis_size("row"))
    row, col = lax.axis_index("row"), lax.axis_index("col")
    y_lo, z = row // 4, row % 4
    x, y_hi, core = col // 4, (col // 2) % 2, col % 2
    place = jnp.stack([row, col]).astype(jnp.int32)

    def mine(v):
        return lax.dynamic_slice_in_dim(v, core * half, half, 0)

    def theirs(v):
        return lax.dynamic_slice_in_dim(v, (1 - core) * half, half, 0)

    mid_gain = scale_mid * keep_mid.astype(F32)
    hidden = jnp.maximum(pre_act.astype(F32) * mid_gain, 0.0).astype(BF16)
    hidden_full = lax.all_gather(hidden, "col", axis=1, tiled=True)
    out_near = y_lo_swap(weight_out)

    wide_gain = scale_wide * keep_wide.astype(F32)
    cot_float = cotangent.astype(F32)
    grad_conv = (cot_float * wide_gain).astype(BF16)
    wide_part = jnp.sum(cot_float * conv_out.astype(F32), axis=0)
    conv_mine = mine(grad_conv)
    weight_out, grad_conv = tie(weight_out, grad_conv)
    out_above, out_below = z_shift(weight_out, -1), z_shift(weight_out, 1)
    conv_sent, input_turned = theirs(grad_conv), inputs.T
    out_near, out_above, out_below, conv_sent, pre_act, weight_in = tie(
        out_near, out_above, out_below, conv_sent, pre_act, weight_in
    )
    near_above, near_below = z_shift(out_near, -1), z_shift(out_near, 1)
    out_across = onward(out_above, out_below, core, z_split)
    in_near = y_lo_swap(weight_in)
    conv_both = jnp.concatenate([conv_mine, core_swap(conv_sent)], axis=1)
    near_above, near_below, out_across, conv_both, in_near, wide_part, place = tie(
        near_above, near_below, out_across, conv_both, in_near, wide_part, place
    )
    near_across = onward(near_above, near_below, core, z_split)
    out_blocks = [
        weight_out, out_near, out_above, near_above, out_below, near_below, out_across, near_across
    ]

    gain_pair = jnp.stack([scale_mid, keep_mid.astype(F32)])
    gain_beside = core_swap(gain_pair)
    pre_mine = mine(pre_act)
    pre_beside = core_swap(theirs(pre_act))

    def chip_order(a, b):
        return jnp.concatenate(
            [jnp.where(core == 0, a, b), jnp.where(core == 0, b, a)], axis=1
        )

    pre_chip = chip_order(pre_mine, pre_beside).astype(F32)
    gain_chip = chip_order(gain_pair, gain_beside)
    mid_gain = gain_chip[0] * gain_chip[1]

    out_beside = [core_swap(block) for block in out_blocks]
    near_across, input_turned = tie(near_across, input_turned)
    out_blocks[7] = near_across
    away, there = hid_partial(place, conv_both, out_blocks, out_beside, ((2, 0), (0, -1)))
    passed, back = x_split(away, 1), x_split(there, -1)
    away, in_near = tie(away, in_near)
    in_here = jnp.stack([weight_in, in_near])
    conv_both, in_here = tie(conv_both, in_here)
    in_above, in_below = z_shift(in_here, -1), z_shift(in_here, 1)
    further, own = hid_partial(place, conv_both, out_blocks, out_beside, ((0, 1), (0, 0)))
    passed, back, own, in_above, in_below = tie(passed, back, own, in_above, in_below)
    far = x_split(add([further[1], passed[1]]).astype(BF16), 1)
    near = x_split(add([further[0], passed[0]]).astype(BF16), 1)
    in_across = onward(in_above, in_below, core, z_split)
    wout = dot(hidden_full, grad_conv, 0, 0).astype(BF16)
    crossed = y_hi_swap(add([own[1], back[1], far]).astype(BF16))
    crossed, near, wout, in_across = tie(crossed, near, wout, in_across)
    in_blocks = [in_here, in_above, in_below, in_across]
    grad_hid = add([own[0], back[0], near, crossed])
    alive = (pre_chip > 0) & (gain_chip[1] > 0)[None, :]
    grad_pre = jnp.where(alive, grad_hid, 0.0)
    mid_part = jnp.sum(grad_pre * pre_chip, axis=0).reshape(2, 128)
    grad_act = (grad_pre * mid_gain).astype(BF16)
    act_near = y_hi_swap(grad_act)
    act_above, act_below = x_shift(grad_act, -1), x_shift(grad_act, 1)
    act_near, act_above, act_below, wout, mid_part = tie(
        act_near, act_above, act_below, wout, mid_part
    )
    wout = lax.psum_scatter(wout, "row", scatter_dimension=0, tiled=True)
    near_above, near_below = x_shift(act_near, -1), x_shift(act_near, 1)

    mid_own = lax.dynamic_index_in_dim(mid_part, core, 0, keepdims=False)
    mid_away = lax.dynamic_index_in_dim(mid_part, 1 - core, 0, keepdims=False)
    mid_own = mid_own + core_swap(mid_away)
    sums = jnp.concatenate([mid_own, wide_part]).reshape(5, 128)
    sums = sums + z_flip(sums, 1)

    act_across = onward(act_above, act_below, core, x_split)
    near_above, near_below, act_across, sums = tie(near_above, near_below, act_across, sums)
    sums = sums + z_flip(sums, 2)
    near_across = onward(near_above, near_below, core, x_split)
    act = [
        grad_act, act_near, act_above, near_above, act_below, near_below, act_across, near_across
    ]
    act_beside = [core_swap(block) for block in act]
    act[7], sums = tie(act[7], sums)

    away, there, further, own = win_partial(place, input_turned, act, act_beside)
    passed, back = z_split(away, 1), z_split(there, -1)
    grad_x = out_gradient(place, cotangent, act, act_beside, in_blocks)
    grad_wout = wout.astype(F32) * scaling
    passed, back, grad_x, grad_wout = tie(passed, back, grad_x, grad_wout)
    far = z_split(add([further[1], passed[1]]).astype(BF16), 1)
    near = z_split(add([further[0], passed[0]]).astype(BF16), 1)
    crossed, sums = tie(add([own[1], back[1], far]).astype(BF16), sums)
    crossed = y_lo_swap(crossed)
    sums = sums + y_lo_swap(sums)
    grad_win = add([own[0], back[0], near, crossed]) * scaling
    grad_smid = keep_mid.astype(F32) * scaling * sums[0]
    grad_swide = keep_wide.astype(F32) * scaling * sums[1:].reshape(512)
    return (grad_x, grad_win, grad_wout, grad_smid, grad_swide)


def solution(mesh):
    return jax.shard_map(
        local,
        mesh=mesh,
        in_specs=(
            P("row", "col"),
            P("row", "col"),
            P("row", "col"),
            P("row", "col"),
            P("col", "row"),
            P("row", "col"),
            P("col"),
            P("col"),
            P("col"),
            P("col"),
        ),
        out_specs=(P("row", "col"), P("col", "row"), P("row", "col"), P("col"), P("col")),
        check_vma=False,
    )
```

```python
import functools
import math

import jax
import jax.numpy as jnp
from jax import lax
from jax.experimental import pallas as pl
from jax.experimental.pallas import tpu as pltpu
from jax.sharding import PartitionSpec as P

F32 = jnp.float32
BF16 = jnp.bfloat16
AXES = ("row", "col")
STEPS = (0, 1, 3, 2)


def permute(v, target):
    pairs = []
    for row in range(8):
        for col in range(16):
            y_lo, z, x, y_hi, core = target(
                row // 4, row % 4, col // 4, (col // 2) % 2, col % 2
            )
            pairs.append(
                (row * 16 + col, (y_lo * 4 + z % 4) * 16 + (x % 4) * 4 + y_hi * 2 + core)
            )
    return lax.ppermute(v, AXES, pairs)


def core_swap(v):
    return permute(v, lambda yl, z, x, yh, c: (yl, z, x, yh, 1 - c))


def y_hi_swap(v):
    return permute(v, lambda yl, z, x, yh, c: (yl, z, x, 1 - yh, c))


def y_lo_swap(v):
    return permute(v, lambda yl, z, x, yh, c: (1 - yl, z, x, yh, c))


def z_flip(v, mask):
    return permute(v, lambda yl, z, x, yh, c: (yl, z ^ mask, x, yh, c))


def x_shift(v, step):
    return permute(v, lambda yl, z, x, yh, c: (yl, z, x + step, yh, c))


def z_shift(v, step):
    return permute(v, lambda yl, z, x, yh, c: (yl, z + step, x, yh, c))


def x_split(v, way):
    return permute(v, lambda yl, z, x, yh, c: (yl, z, x + way * (1 - 2 * c), yh, c))


def z_split(v, way):
    return permute(v, lambda yl, z, x, yh, c: (yl, z + way * (1 - 2 * c), x, yh, c))


def dot(a, b, ca, cb):
    return lax.dot_general(a, b, (((ca,), (cb,)), ((), ())), preferred_element_type=F32)


def onward(above, below, core, split):
    return split(jnp.where(core == 0, below, above), 1)


def place_of(v):
    row, col = v[0], v[1]
    return row, row >> 2, row & 3, col >> 2, (col >> 1) & 1, col & 1


def slot_of(step):
    step = step & 3
    return jnp.where(step >= 2, 5 - step, step)


def row_slot(block, y_lo, z):
    return slot_of((block & 3) - z) * 2 + ((block >> 2) ^ y_lo)


def hidden_slot(block, x, y_hi):
    return slot_of((block >> 1) - x) * 2 + ((block & 1) ^ y_hi)


def call(body, outs, out_space, scratch, sems, loads, flops, here, vmem_args, any_args):
    vmem = pl.BlockSpec(memory_space=pltpu.VMEM)
    return pl.pallas_call(
        body,
        out_shape=outs,
        in_specs=[pl.BlockSpec(memory_space=pltpu.SMEM)]
        + [vmem] * len(vmem_args)
        + [pl.BlockSpec(memory_space=pl.ANY)] * len(any_args),
        out_specs=[pl.BlockSpec(memory_space=out_space)] * len(outs),
        scratch_shapes=[*scratch, pltpu.SemaphoreType.DMA((sems,))],
        compiler_params=pltpu.CompilerParams(vmem_limit_bytes=60 * 1024 * 1024),
        cost_estimate=pl.CostEstimate(flops=flops, bytes_accessed=loads, transcendentals=0),
    )(here, *vmem_args, *any_args)


def hid_kernel(ways, here, conv, *refs):
    blocks, outs, (held, sems) = refs[:16], refs[16:18], refs[18:]
    copies = [
        pltpu.make_async_copy(
            ref, held.at[k % 8, :, pl.ds((k // 8) * 512, 512)], sems.at[k]
        )
        for k, ref in enumerate(blocks)
    ]
    for copy in copies:
        copy.start()
    row, y_lo, z, x, y_hi, core = place_of(here)
    ahead = 1 - 2 * core
    for copy in copies:
        copy.wait()
    for j in range(4):
        fixed, way = ways[j // 2]
        block = ((x + fixed + way * ahead) & 3) * 2 + (y_hi ^ (j % 2))
        outs[j // 2][j % 2] = lax.dot_general(
            conv[...], held[row_slot(block, y_lo, z)], (((1,), (1,)), ((), ())),
            preferred_element_type=F32,
        ).astype(BF16)


def hid_partial(here, conv, blocks, beside, ways):
    return call(
        functools.partial(hid_kernel, ways), [jax.ShapeDtypeStruct((2, 768, 256), BF16)] * 2,
        pltpu.VMEM, [pltpu.VMEM((8, 256, 1024), BF16)], 16, 8 << 20, 768 * 1024 * 2048, here,
        [conv], [*blocks, *beside],
    )


def act_copies(own, beside, at, sems, first, core):
    copies = []
    for part, ref in enumerate((own, beside)):
        rows = pl.ds(pl.multiple_of((core ^ part) * 768, 768), 768)
        copies.append(pltpu.make_async_copy(ref, at(rows), sems.at[first + part]))
    return copies


def win_kernel(here, left, *refs):
    blocks, outs, (held, sems) = refs[:16], refs[16:20], refs[20:]
    row, y_lo, z, x, y_hi, core = place_of(here)
    copies = []
    for k in range(8):
        copies += act_copies(
            blocks[k], blocks[8 + k], lambda rows, k=k: held.at[k, rows, :], sems, 2 * k, core
        )
    for copy in copies:
        copy.start()
    for copy in copies:
        copy.wait()
    ahead = 1 - 2 * core
    for j in range(8):
        step = (2, -ahead, ahead, 0)[j // 2]
        block = (y_lo ^ (j % 2)) * 4 + ((z + step) & 3)
        outs[j // 2][j % 2] = jnp.dot(
            left[...], held[hidden_slot(block, x, y_hi)], preferred_element_type=F32
        ).astype(BF16)


def win_partial(here, left, blocks, beside):
    return call(
        win_kernel, [jax.ShapeDtypeStruct((2, 512, 256), BF16)] * 4, pltpu.VMEM,
        [pltpu.VMEM((8, 1536, 256), BF16)], 16, 10 << 20, 2 * 512 * 1536 * 2048, here, [left],
        [*blocks, *beside],
    )


def out_kernel(here, cot, *refs):
    blocks, parts, out = refs[:16], refs[16:20], refs[20]
    held, weights, sems = refs[21:]
    row, y_lo, z, x, y_hi, core = place_of(here)
    copies = [
        pltpu.make_async_copy(ref, weights.at[pl.ds(k * 2, 2)], sems.at[16 + k])
        for k, ref in enumerate(parts)
    ]
    for k in range(8):
        copies += act_copies(
            blocks[k], blocks[8 + k], lambda rows, k=k: held.at[k, rows, :], sems, 2 * k, core
        )
    for copy in copies:
        copy.start()
    for copy in copies:
        copy.wait()
    for at in range(0, 1536, 256):
        total = cot[at : at + 256, :].astype(F32)
        for block in range(8):
            total = total + lax.dot_general(
                held[hidden_slot(block, x, y_hi), at : at + 256, :],
                weights[row_slot(block, y_lo, z)],
                (((1,), (1,)), ((), ())),
                preferred_element_type=F32,
            )
        out[at : at + 256, :] = total.astype(BF16)


def out_gradient(here, cot, blocks, beside, weights):
    return call(
        out_kernel, [jax.ShapeDtypeStruct((1536, 512), BF16)], pltpu.VMEM,
        [pltpu.VMEM((8, 1536, 256), BF16), pltpu.VMEM((8, 512, 256), BF16)], 20, 12 << 20,
        2 * 1536 * 512 * 2048, here, [cot], [*blocks, *beside, *weights],
    )[0]


def tie(*values):
    return lax.optimization_barrier(values)


def add(terms):
    return sum(term.astype(F32) for term in terms)


def local(
    inputs,
    cotangent,
    conv_out,
    pre_act,
    weight_in,
    weight_out,
    scale_mid,
    scale_wide,
    keep_mid,
    keep_wide,
):
    rows = inputs.shape[0]
    half = rows // 2
    scaling = 1.0 / math.sqrt(rows * lax.axis_size("row"))
    row, col = lax.axis_index("row"), lax.axis_index("col")
    y_lo, z = row // 4, row % 4
    x, y_hi, core = col // 4, (col // 2) % 2, col % 2
    place = jnp.stack([row, col]).astype(jnp.int32)

    def mine(v):
        return lax.dynamic_slice_in_dim(v, core * half, half, 0)

    def theirs(v):
        return lax.dynamic_slice_in_dim(v, (1 - core) * half, half, 0)

    mid_gain = scale_mid * keep_mid.astype(F32)
    hidden = jnp.maximum(pre_act.astype(F32) * mid_gain, 0.0).astype(BF16)
    hidden_full = lax.all_gather(hidden, "col", axis=1, tiled=True)
    out_above, out_below = z_shift(weight_out, -1), z_shift(weight_out, 1)
    out_near = y_lo_swap(weight_out)

    wide_gain = scale_wide * keep_wide.astype(F32)
    cot_float = cotangent.astype(F32)
    grad_conv = (cot_float * wide_gain).astype(BF16)
    wide_part = jnp.sum(cot_float * conv_out.astype(F32), axis=0)
    conv_mine = mine(grad_conv)
    conv_sent, input_turned = theirs(grad_conv), inputs.T
    out_near, out_above, out_below, conv_sent, pre_act, weight_in = tie(
        out_near, out_above, out_below, conv_sent, pre_act, weight_in
    )
    near_above, near_below = z_shift(out_near, -1), z_shift(out_near, 1)
    out_across = onward(out_above, out_below, core, z_split)
    in_near = y_lo_swap(weight_in)
    conv_both = jnp.concatenate([conv_mine, core_swap(conv_sent)], axis=1)
    near_above, near_below, out_across, conv_both, in_near, wide_part, place = tie(
        near_above, near_below, out_across, conv_both, in_near, wide_part, place
    )
    near_across = onward(near_above, near_below, core, z_split)
    out_blocks = [
        weight_out, out_near, out_above, near_above, out_below, near_below, out_across, near_across
    ]

    gain_pair = jnp.stack([scale_mid, keep_mid.astype(F32)])
    gain_beside = core_swap(gain_pair)
    pre_mine = mine(pre_act)
    pre_beside = core_swap(theirs(pre_act))

    def chip_order(a, b):
        return jnp.concatenate(
            [jnp.where(core == 0, a, b), jnp.where(core == 0, b, a)], axis=1
        )

    pre_chip = chip_order(pre_mine, pre_beside).astype(F32)
    gain_chip = chip_order(gain_pair, gain_beside)
    mid_gain = gain_chip[0] * gain_chip[1]

    out_beside = [core_swap(block) for block in out_blocks]
    near_across, input_turned = tie(near_across, input_turned)
    out_blocks[7] = near_across
    away, there = hid_partial(place, conv_both, out_blocks, out_beside, ((2, 0), (0, -1)))
    passed, back = x_split(away, 1), x_split(there, -1)
    away, in_near = tie(away, in_near)
    in_here = jnp.stack([weight_in, in_near])
    conv_both, in_here = tie(conv_both, in_here)
    in_above, in_below = z_shift(in_here, -1), z_shift(in_here, 1)
    further, own = hid_partial(place, conv_both, out_blocks, out_beside, ((0, 1), (0, 0)))
    passed, back, own, in_above, in_below = tie(passed, back, own, in_above, in_below)
    far = x_split(add([further[1], passed[1]]).astype(BF16), 1)
    near = x_split(add([further[0], passed[0]]).astype(BF16), 1)
    in_across = onward(in_above, in_below, core, z_split)
    wout = dot(hidden_full, grad_conv, 0, 0).astype(BF16)
    crossed = y_hi_swap(add([own[1], back[1], far]).astype(BF16))
    crossed, near, wout, in_across = tie(crossed, near, wout, in_across)
    in_blocks = [in_here, in_above, in_below, in_across]
    grad_hid = add([own[0], back[0], near, crossed])
    alive = (pre_chip > 0) & (gain_chip[1] > 0)[None, :]
    grad_pre = jnp.where(alive, grad_hid, 0.0)
    mid_part = jnp.sum(grad_pre * pre_chip, axis=0).reshape(2, 128)
    grad_act = (grad_pre * mid_gain).astype(BF16)
    act_near = y_hi_swap(grad_act)
    act_above, act_below = x_shift(grad_act, -1), x_shift(grad_act, 1)
    act_near, act_above, act_below, wout, mid_part = tie(
        act_near, act_above, act_below, wout, mid_part
    )
    wout = lax.psum_scatter(wout, "row", scatter_dimension=0, tiled=True)
    near_above, near_below = x_shift(act_near, -1), x_shift(act_near, 1)

    mid_own = lax.dynamic_index_in_dim(mid_part, core, 0, keepdims=False)
    mid_away = lax.dynamic_index_in_dim(mid_part, 1 - core, 0, keepdims=False)
    mid_own = mid_own + core_swap(mid_away)
    sums = jnp.concatenate([mid_own, wide_part]).reshape(5, 128)
    sums = sums + z_flip(sums, 1)

    act_across = onward(act_above, act_below, core, x_split)
    near_above, near_below, act_across, sums = tie(near_above, near_below, act_across, sums)
    sums = sums + z_flip(sums, 2)
    near_across = onward(near_above, near_below, core, x_split)
    act = [
        grad_act, act_near, act_above, near_above, act_below, near_below, act_across, near_across
    ]
    act_beside = [core_swap(block) for block in act]
    act[7], sums = tie(act[7], sums)

    away, there, further, own = win_partial(place, input_turned, act, act_beside)
    passed, back = z_split(away, 1), z_split(there, -1)
    grad_x = out_gradient(place, cotangent, act, act_beside, in_blocks)
    grad_wout = wout.astype(F32) * scaling
    passed, back, grad_x, grad_wout = tie(passed, back, grad_x, grad_wout)
    far = z_split(add([further[1], passed[1]]).astype(BF16), 1)
    near = z_split(add([further[0], passed[0]]).astype(BF16), 1)
    crossed, sums = tie(add([own[1], back[1], far]).astype(BF16), sums)
    crossed = y_lo_swap(crossed)
    sums = sums + y_lo_swap(sums)
    grad_win = add([own[0], back[0], near, crossed]) * scaling
    grad_smid = keep_mid.astype(F32) * scaling * sums[0]
    grad_swide = keep_wide.astype(F32) * scaling * sums[1:].reshape(512)
    return (grad_x, grad_win, grad_wout, grad_smid, grad_swide)


def solution(mesh):
    return jax.shard_map(
        local,
        mesh=mesh,
        in_specs=(
            P("row", "col"),
            P("row", "col"),
            P("row", "col"),
            P("row", "col"),
            P("col", "row"),
            P("row", "col"),
            P("col"),
            P("col"),
            P("col"),
            P("col"),
        ),
        out_specs=(P("row", "col"), P("col", "row"), P("row", "col"), P("col"), P("col")),
        check_vma=False,
    )
```

```python
import functools
import math

import jax
import jax.numpy as jnp
from jax import lax
from jax.experimental import pallas as pl
from jax.experimental.pallas import tpu as pltpu
from jax.sharding import PartitionSpec as P

F32 = jnp.float32
BF16 = jnp.bfloat16
AXES = ("row", "col")
STEPS = (0, 1, 3, 2)


def permute(v, target):
    pairs = []
    for row in range(8):
        for col in range(16):
            y_lo, z, x, y_hi, core = target(
                row // 4, row % 4, col // 4, (col // 2) % 2, col % 2
            )
            pairs.append(
                (row * 16 + col, (y_lo * 4 + z % 4) * 16 + (x % 4) * 4 + y_hi * 2 + core)
            )
    return lax.ppermute(v, AXES, pairs)


def core_swap(v):
    return permute(v, lambda yl, z, x, yh, c: (yl, z, x, yh, 1 - c))


def y_hi_swap(v):
    return permute(v, lambda yl, z, x, yh, c: (yl, z, x, 1 - yh, c))


def y_lo_swap(v):
    return permute(v, lambda yl, z, x, yh, c: (1 - yl, z, x, yh, c))


def z_flip(v, mask):
    return permute(v, lambda yl, z, x, yh, c: (yl, z ^ mask, x, yh, c))


def x_shift(v, step):
    return permute(v, lambda yl, z, x, yh, c: (yl, z, x + step, yh, c))


def z_shift(v, step):
    return permute(v, lambda yl, z, x, yh, c: (yl, z + step, x, yh, c))


def x_split(v, way):
    return permute(v, lambda yl, z, x, yh, c: (yl, z, x + way * (1 - 2 * c), yh, c))


def z_split(v, way):
    return permute(v, lambda yl, z, x, yh, c: (yl, z + way * (1 - 2 * c), x, yh, c))


def dot(a, b, ca, cb):
    return lax.dot_general(a, b, (((ca,), (cb,)), ((), ())), preferred_element_type=F32)


def onward(above, below, core, split):
    return split(jnp.where(core == 0, below, above), 1)


def place_of(v):
    row, col = v[0], v[1]
    return row, row >> 2, row & 3, col >> 2, (col >> 1) & 1, col & 1


def slot_of(step):
    step = step & 3
    return jnp.where(step >= 2, 5 - step, step)


def row_slot(block, y_lo, z):
    return slot_of((block & 3) - z) * 2 + ((block >> 2) ^ y_lo)


def hidden_slot(block, x, y_hi):
    return slot_of((block >> 1) - x) * 2 + ((block & 1) ^ y_hi)


def call(body, outs, out_space, scratch, sems, loads, flops, here, vmem_args, any_args):
    vmem = pl.BlockSpec(memory_space=pltpu.VMEM)
    return pl.pallas_call(
        body,
        out_shape=outs,
        in_specs=[pl.BlockSpec(memory_space=pltpu.SMEM)]
        + [vmem] * len(vmem_args)
        + [pl.BlockSpec(memory_space=pltpu.HBM)] * len(any_args),
        out_specs=[pl.BlockSpec(memory_space=out_space)] * len(outs),
        scratch_shapes=[*scratch, pltpu.SemaphoreType.DMA((sems,))],
        compiler_params=pltpu.CompilerParams(vmem_limit_bytes=60 * 1024 * 1024),
        cost_estimate=pl.CostEstimate(flops=flops, bytes_accessed=loads, transcendentals=0),
    )(here, *vmem_args, *any_args)


def hid_kernel(ways, here, conv, *refs):
    blocks, outs, (held, sems) = refs[:16], refs[16:18], refs[18:]
    copies = [
        pltpu.make_async_copy(
            ref, held.at[k % 8, :, pl.ds((k // 8) * 512, 512)], sems.at[k]
        )
        for k, ref in enumerate(blocks)
    ]
    for copy in copies:
        copy.start()
    row, y_lo, z, x, y_hi, core = place_of(here)
    ahead = 1 - 2 * core
    for copy in copies:
        copy.wait()
    for j in range(4):
        fixed, way = ways[j // 2]
        block = ((x + fixed + way * ahead) & 3) * 2 + (y_hi ^ (j % 2))
        outs[j // 2][j % 2] = lax.dot_general(
            conv[...], held[row_slot(block, y_lo, z)], (((1,), (1,)), ((), ())),
            preferred_element_type=F32,
        ).astype(BF16)


def hid_partial(here, conv, blocks, beside, ways):
    return call(
        functools.partial(hid_kernel, ways), [jax.ShapeDtypeStruct((2, 768, 256), BF16)] * 2,
        pltpu.VMEM, [pltpu.VMEM((8, 256, 1024), BF16)], 16, 8 << 20, 768 * 1024 * 2048, here,
        [conv], [*blocks, *beside],
    )


def act_copies(own, beside, at, sems, first, core):
    copies = []
    for part, ref in enumerate((own, beside)):
        rows = pl.ds(pl.multiple_of((core ^ part) * 768, 768), 768)
        copies.append(pltpu.make_async_copy(ref, at(rows), sems.at[first + part]))
    return copies


def win_kernel(here, left, *refs):
    blocks, outs, (held, sems) = refs[:16], refs[16:20], refs[20:]
    row, y_lo, z, x, y_hi, core = place_of(here)
    copies = []
    for k in range(8):
        copies += act_copies(
            blocks[k], blocks[8 + k], lambda rows, k=k: held.at[k, rows, :], sems, 2 * k, core
        )
    for copy in copies:
        copy.start()
    for copy in copies:
        copy.wait()
    ahead = 1 - 2 * core
    for j in range(8):
        step = (2, -ahead, ahead, 0)[j // 2]
        block = (y_lo ^ (j % 2)) * 4 + ((z + step) & 3)
        outs[j // 2][j % 2] = jnp.dot(
            left[...], held[hidden_slot(block, x, y_hi)], preferred_element_type=F32
        ).astype(BF16)


def win_partial(here, left, blocks, beside):
    return call(
        win_kernel, [jax.ShapeDtypeStruct((2, 512, 256), BF16)] * 4, pltpu.VMEM,
        [pltpu.VMEM((8, 1536, 256), BF16)], 16, 10 << 20, 2 * 512 * 1536 * 2048, here, [left],
        [*blocks, *beside],
    )


def out_kernel(here, cot, *refs):
    blocks, parts, out = refs[:16], refs[16:20], refs[20]
    held, weights, sems = refs[21:]
    row, y_lo, z, x, y_hi, core = place_of(here)
    copies = [
        pltpu.make_async_copy(ref, weights.at[pl.ds(k * 2, 2)], sems.at[16 + k])
        for k, ref in enumerate(parts)
    ]
    for k in range(8):
        copies += act_copies(
            blocks[k], blocks[8 + k], lambda rows, k=k: held.at[k, rows, :], sems, 2 * k, core
        )
    for copy in copies:
        copy.start()
    for copy in copies:
        copy.wait()
    for at in range(0, 1536, 256):
        total = cot[at : at + 256, :].astype(F32)
        for block in range(8):
            total = total + lax.dot_general(
                held[hidden_slot(block, x, y_hi), at : at + 256, :],
                weights[row_slot(block, y_lo, z)],
                (((1,), (1,)), ((), ())),
                preferred_element_type=F32,
            )
        out[at : at + 256, :] = total.astype(BF16)


def out_gradient(here, cot, blocks, beside, weights):
    return call(
        out_kernel, [jax.ShapeDtypeStruct((1536, 512), BF16)], pltpu.VMEM,
        [pltpu.VMEM((8, 1536, 256), BF16), pltpu.VMEM((8, 512, 256), BF16)], 20, 12 << 20,
        2 * 1536 * 512 * 2048, here, [cot], [*blocks, *beside, *weights],
    )[0]


def tie(*values):
    return lax.optimization_barrier(values)


def add(terms):
    return sum(term.astype(F32) for term in terms)


def local(
    inputs,
    cotangent,
    conv_out,
    pre_act,
    weight_in,
    weight_out,
    scale_mid,
    scale_wide,
    keep_mid,
    keep_wide,
):
    rows = inputs.shape[0]
    half = rows // 2
    scaling = 1.0 / math.sqrt(rows * lax.axis_size("row"))
    row, col = lax.axis_index("row"), lax.axis_index("col")
    y_lo, z = row // 4, row % 4
    x, y_hi, core = col // 4, (col // 2) % 2, col % 2
    place = jnp.stack([row, col]).astype(jnp.int32)

    def mine(v):
        return lax.dynamic_slice_in_dim(v, core * half, half, 0)

    def theirs(v):
        return lax.dynamic_slice_in_dim(v, (1 - core) * half, half, 0)

    mid_gain = scale_mid * keep_mid.astype(F32)
    hidden = jnp.maximum(pre_act.astype(F32) * mid_gain, 0.0).astype(BF16)
    hidden_full = lax.all_gather(hidden, "col", axis=1, tiled=True)
    out_above, out_below = z_shift(weight_out, -1), z_shift(weight_out, 1)
    out_near = y_lo_swap(weight_out)

    wide_gain = scale_wide * keep_wide.astype(F32)
    cot_float = cotangent.astype(F32)
    grad_conv = (cot_float * wide_gain).astype(BF16)
    wide_part = jnp.sum(cot_float * conv_out.astype(F32), axis=0)
    conv_mine = mine(grad_conv)
    conv_sent, input_turned = theirs(grad_conv), inputs.T
    out_near, out_above, out_below, conv_sent, pre_act, weight_in = tie(
        out_near, out_above, out_below, conv_sent, pre_act, weight_in
    )
    near_above, near_below = z_shift(out_near, -1), z_shift(out_near, 1)
    out_across = onward(out_above, out_below, core, z_split)
    in_near = y_lo_swap(weight_in)
    conv_both = jnp.concatenate([conv_mine, core_swap(conv_sent)], axis=1)
    near_above, near_below, out_across, conv_both, in_near, wide_part, place = tie(
        near_above, near_below, out_across, conv_both, in_near, wide_part, place
    )
    near_across = onward(near_above, near_below, core, z_split)
    out_blocks = [
        weight_out, out_near, out_above, near_above, out_below, near_below, out_across, near_across
    ]

    gain_pair = jnp.stack([scale_mid, keep_mid.astype(F32)])
    gain_beside = core_swap(gain_pair)
    pre_mine = mine(pre_act)
    pre_beside = core_swap(theirs(pre_act))

    def chip_order(a, b):
        return jnp.concatenate(
            [jnp.where(core == 0, a, b), jnp.where(core == 0, b, a)], axis=1
        )

    pre_chip = chip_order(pre_mine, pre_beside).astype(F32)
    gain_chip = chip_order(gain_pair, gain_beside)
    mid_gain = gain_chip[0] * gain_chip[1]

    out_beside = [core_swap(block) for block in out_blocks]
    near_across, input_turned = tie(near_across, input_turned)
    out_blocks[7] = near_across
    away, there = hid_partial(place, conv_both, out_blocks, out_beside, ((2, 0), (0, -1)))
    passed, back = x_split(away, 1), x_split(there, -1)
    away, in_near = tie(away, in_near)
    in_here = jnp.stack([weight_in, in_near])
    conv_both, in_here = tie(conv_both, in_here)
    in_above, in_below = z_shift(in_here, -1), z_shift(in_here, 1)
    further, own = hid_partial(place, conv_both, out_blocks, out_beside, ((0, 1), (0, 0)))
    passed, back, own, in_above, in_below = tie(passed, back, own, in_above, in_below)
    far = x_split(add([further[1], passed[1]]).astype(BF16), 1)
    near = x_split(add([further[0], passed[0]]).astype(BF16), 1)
    in_across = onward(in_above, in_below, core, z_split)
    wout = dot(hidden_full, grad_conv, 0, 0).astype(BF16)
    crossed = y_hi_swap(add([own[1], back[1], far]).astype(BF16))
    crossed, near, wout, in_across = tie(crossed, near, wout, in_across)
    in_blocks = [in_here, in_above, in_below, in_across]
    grad_hid = add([own[0], back[0], near, crossed])
    alive = (pre_chip > 0) & (gain_chip[1] > 0)[None, :]
    grad_pre = jnp.where(alive, grad_hid, 0.0)
    mid_part = jnp.sum(grad_pre * pre_chip, axis=0).reshape(2, 128)
    grad_act = (grad_pre * mid_gain).astype(BF16)
    act_near = y_hi_swap(grad_act)
    act_above, act_below = x_shift(grad_act, -1), x_shift(grad_act, 1)
    act_near, act_above, act_below, wout, mid_part = tie(
        act_near, act_above, act_below, wout, mid_part
    )
    wout = lax.psum_scatter(wout, "row", scatter_dimension=0, tiled=True)
    near_above, near_below = x_shift(act_near, -1), x_shift(act_near, 1)

    mid_own = lax.dynamic_index_in_dim(mid_part, core, 0, keepdims=False)
    mid_away = lax.dynamic_index_in_dim(mid_part, 1 - core, 0, keepdims=False)
    mid_own = mid_own + core_swap(mid_away)
    sums = jnp.concatenate([mid_own, wide_part]).reshape(5, 128)
    sums = sums + z_flip(sums, 1)

    act_across = onward(act_above, act_below, core, x_split)
    near_above, near_below, act_across, sums = tie(near_above, near_below, act_across, sums)
    sums = sums + z_flip(sums, 2)
    near_across = onward(near_above, near_below, core, x_split)
    act = [
        grad_act, act_near, act_above, near_above, act_below, near_below, act_across, near_across
    ]
    act_beside = [core_swap(block) for block in act]
    act[7], sums = tie(act[7], sums)

    away, there, further, own = win_partial(place, input_turned, act, act_beside)
    passed, back = z_split(away, 1), z_split(there, -1)
    grad_x = out_gradient(place, cotangent, act, act_beside, in_blocks)
    grad_wout = wout.astype(F32) * scaling
    passed, back, grad_x, grad_wout = tie(passed, back, grad_x, grad_wout)
    onward_sum = z_split(add([further, passed]).astype(BF16), 1)
    total = add([own, back, onward_sum])
    crossed, sums = tie(total[1].astype(BF16), sums)
    crossed = y_lo_swap(crossed)
    sums = sums + y_lo_swap(sums)
    grad_win = add([total[0], crossed]) * scaling
    grad_smid = keep_mid.astype(F32) * scaling * sums[0]
    grad_swide = keep_wide.astype(F32) * scaling * sums[1:].reshape(512)
    return (grad_x, grad_win, grad_wout, grad_smid, grad_swide)


def solution(mesh):
    return jax.shard_map(
        local,
        mesh=mesh,
        in_specs=(
            P("row", "col"),
            P("row", "col"),
            P("row", "col"),
            P("row", "col"),
            P("col", "row"),
            P("row", "col"),
            P("col"),
            P("col"),
            P("col"),
            P("col"),
        ),
        out_specs=(P("row", "col"), P("col", "row"), P("row", "col"), P("col"), P("col")),
        check_vma=False,
    )
```

```python
import functools
import math

import jax
import jax.numpy as jnp
from jax import lax
from jax.experimental import pallas as pl
from jax.experimental.pallas import tpu as pltpu
from jax.sharding import PartitionSpec as P

F32 = jnp.float32
BF16 = jnp.bfloat16
AXES = ("row", "col")
STEPS = (0, 1, 3, 2)


def permute(v, target):
    pairs = []
    for row in range(8):
        for col in range(16):
            y_lo, z, x, y_hi, core = target(
                row // 4, row % 4, col // 4, (col // 2) % 2, col % 2
            )
            pairs.append(
                (row * 16 + col, (y_lo * 4 + z % 4) * 16 + (x % 4) * 4 + y_hi * 2 + core)
            )
    return lax.ppermute(v, AXES, pairs)


def core_swap(v):
    return permute(v, lambda yl, z, x, yh, c: (yl, z, x, yh, 1 - c))


def y_hi_swap(v):
    return permute(v, lambda yl, z, x, yh, c: (yl, z, x, 1 - yh, c))


def y_lo_swap(v):
    return permute(v, lambda yl, z, x, yh, c: (1 - yl, z, x, yh, c))


def z_flip(v, mask):
    return permute(v, lambda yl, z, x, yh, c: (yl, z ^ mask, x, yh, c))


def x_shift(v, step):
    return permute(v, lambda yl, z, x, yh, c: (yl, z, x + step, yh, c))


def z_shift(v, step):
    return permute(v, lambda yl, z, x, yh, c: (yl, z + step, x, yh, c))


def x_split(v, way):
    return permute(v, lambda yl, z, x, yh, c: (yl, z, x + way * (1 - 2 * c), yh, c))


def z_split(v, way):
    return permute(v, lambda yl, z, x, yh, c: (yl, z + way * (1 - 2 * c), x, yh, c))


def dot(a, b, ca, cb):
    return lax.dot_general(a, b, (((ca,), (cb,)), ((), ())), preferred_element_type=F32)


def onward(above, below, core, split):
    return split(jnp.where(core == 0, below, above), 1)


def place_of(v):
    row, col = v[0], v[1]
    return row, row >> 2, row & 3, col >> 2, (col >> 1) & 1, col & 1


def slot_of(step):
    step = step & 3
    return jnp.where(step >= 2, 5 - step, step)


def row_slot(block, y_lo, z):
    return slot_of((block & 3) - z) * 2 + ((block >> 2) ^ y_lo)


def hidden_slot(block, x, y_hi):
    return slot_of((block >> 1) - x) * 2 + ((block & 1) ^ y_hi)


def call(body, outs, out_space, scratch, sems, loads, flops, here, vmem_args, any_args):
    vmem = pl.BlockSpec(memory_space=pltpu.VMEM)
    return pl.pallas_call(
        body,
        out_shape=outs,
        in_specs=[pl.BlockSpec(memory_space=pltpu.SMEM)]
        + [vmem] * len(vmem_args)
        + [pl.BlockSpec(memory_space=pl.ANY)] * len(any_args),
        out_specs=[pl.BlockSpec(memory_space=out_space)] * len(outs),
        scratch_shapes=[*scratch, pltpu.SemaphoreType.DMA((sems,))],
        compiler_params=pltpu.CompilerParams(vmem_limit_bytes=62 * 1024 * 1024),
        cost_estimate=pl.CostEstimate(flops=flops, bytes_accessed=loads, transcendentals=0),
    )(here, *vmem_args, *any_args)


def hid_kernel(ways, here, conv, *refs):
    blocks, outs, (held, sems) = refs[:16], refs[16:18], refs[18:]
    copies = [
        pltpu.make_async_copy(
            ref, held.at[k % 8, :, pl.ds((k // 8) * 512, 512)], sems.at[k]
        )
        for k, ref in enumerate(blocks)
    ]
    for copy in copies:
        copy.start()
    row, y_lo, z, x, y_hi, core = place_of(here)
    ahead = 1 - 2 * core
    for copy in copies:
        copy.wait()
    for j in range(4):
        fixed, way = ways[j // 2]
        block = ((x + fixed + way * ahead) & 3) * 2 + (y_hi ^ (j % 2))
        outs[j // 2][j % 2] = lax.dot_general(
            conv[...], held[row_slot(block, y_lo, z)], (((1,), (1,)), ((), ())),
            preferred_element_type=F32,
        ).astype(BF16)


def hid_partial(here, conv, blocks, beside, ways):
    return call(
        functools.partial(hid_kernel, ways), [jax.ShapeDtypeStruct((2, 768, 256), BF16)] * 2,
        pltpu.VMEM, [pltpu.VMEM((8, 256, 1024), BF16)], 16, 8 << 20, 768 * 1024 * 2048, here,
        [conv], [*blocks, *beside],
    )


def act_copies(own, beside, at, sems, first, core):
    copies = []
    for part, ref in enumerate((own, beside)):
        rows = pl.ds(pl.multiple_of((core ^ part) * 768, 768), 768)
        copies.append(pltpu.make_async_copy(ref, at(rows), sems.at[first + part]))
    return copies


def win_kernel(here, left, *refs):
    blocks, outs, (held, sems) = refs[:16], refs[16:20], refs[20:]
    row, y_lo, z, x, y_hi, core = place_of(here)
    copies = []
    for k in range(8):
        copies += act_copies(
            blocks[k], blocks[8 + k], lambda rows, k=k: held.at[k, rows, :], sems, 2 * k, core
        )
    for copy in copies:
        copy.start()
    for copy in copies:
        copy.wait()
    ahead = 1 - 2 * core
    for j in range(8):
        step = (2, -ahead, ahead, 0)[j // 2]
        block = (y_lo ^ (j % 2)) * 4 + ((z + step) & 3)
        outs[j // 2][j % 2] = jnp.dot(
            left[...], held[hidden_slot(block, x, y_hi)], preferred_element_type=F32
        ).astype(BF16)


def win_partial(here, left, blocks, beside):
    return call(
        win_kernel, [jax.ShapeDtypeStruct((2, 512, 256), BF16)] * 4, pltpu.VMEM,
        [pltpu.VMEM((8, 1536, 256), BF16)], 16, 10 << 20, 2 * 512 * 1536 * 2048, here, [left],
        [*blocks, *beside],
    )


def out_kernel(here, cot, *refs):
    blocks, parts, out = refs[:16], refs[16:20], refs[20]
    held, weights, sems = refs[21:]
    row, y_lo, z, x, y_hi, core = place_of(here)
    copies = [
        pltpu.make_async_copy(ref, weights.at[pl.ds(k * 2, 2)], sems.at[16 + k])
        for k, ref in enumerate(parts)
    ]
    for k in range(8):
        copies += act_copies(
            blocks[k], blocks[8 + k], lambda rows, k=k: held.at[k, rows, :], sems, 2 * k, core
        )
    for copy in copies:
        copy.start()
    for copy in copies:
        copy.wait()
    for at in range(0, 1536, 256):
        total = cot[at : at + 256, :].astype(F32)
        for block in range(8):
            total = total + lax.dot_general(
                held[hidden_slot(block, x, y_hi), at : at + 256, :],
                weights[row_slot(block, y_lo, z)],
                (((1,), (1,)), ((), ())),
                preferred_element_type=F32,
            )
        out[at : at + 256, :] = total.astype(BF16)


def out_gradient(here, cot, blocks, beside, weights):
    return call(
        out_kernel, [jax.ShapeDtypeStruct((1536, 512), BF16)], pltpu.VMEM,
        [pltpu.VMEM((8, 1536, 256), BF16), pltpu.VMEM((8, 512, 256), BF16)], 20, 12 << 20,
        2 * 1536 * 512 * 2048, here, [cot], [*blocks, *beside, *weights],
    )[0]


def tie(*values):
    return lax.optimization_barrier(values)


def add(terms):
    return sum(term.astype(F32) for term in terms)


def local(
    inputs,
    cotangent,
    conv_out,
    pre_act,
    weight_in,
    weight_out,
    scale_mid,
    scale_wide,
    keep_mid,
    keep_wide,
):
    rows = inputs.shape[0]
    half = rows // 2
    scaling = 1.0 / math.sqrt(rows * lax.axis_size("row"))
    row, col = lax.axis_index("row"), lax.axis_index("col")
    y_lo, z = row // 4, row % 4
    x, y_hi, core = col // 4, (col // 2) % 2, col % 2
    place = jnp.stack([row, col]).astype(jnp.int32)

    def mine(v):
        return lax.dynamic_slice_in_dim(v, core * half, half, 0)

    def theirs(v):
        return lax.dynamic_slice_in_dim(v, (1 - core) * half, half, 0)

    mid_gain = scale_mid * keep_mid.astype(F32)
    hidden = jnp.maximum(pre_act.astype(F32) * mid_gain, 0.0).astype(BF16)
    hidden_full = lax.all_gather(hidden, "col", axis=1, tiled=True)
    out_above, out_below = z_shift(weight_out, -1), z_shift(weight_out, 1)
    out_near = y_lo_swap(weight_out)

    wide_gain = scale_wide * keep_wide.astype(F32)
    cot_float = cotangent.astype(F32)
    grad_conv = (cot_float * wide_gain).astype(BF16)
    wide_part = jnp.sum(cot_float * conv_out.astype(F32), axis=0)
    conv_mine = mine(grad_conv)
    conv_sent, input_turned = theirs(grad_conv), inputs.T
    out_near, out_above, out_below, conv_sent, pre_act, weight_in = tie(
        out_near, out_above, out_below, conv_sent, pre_act, weight_in
    )
    near_above, near_below = z_shift(out_near, -1), z_shift(out_near, 1)
    out_across = onward(out_above, out_below, core, z_split)
    in_near = y_lo_swap(weight_in)
    conv_both = jnp.concatenate([conv_mine, core_swap(conv_sent)], axis=1)
    near_above, near_below, out_across, conv_both, in_near, wide_part, place = tie(
        near_above, near_below, out_across, conv_both, in_near, wide_part, place
    )
    near_across = onward(near_above, near_below, core, z_split)
    out_blocks = [
        weight_out, out_near, out_above, near_above, out_below, near_below, out_across, near_across
    ]

    gain_pair = jnp.stack([scale_mid, keep_mid.astype(F32)])
    gain_beside = core_swap(gain_pair)
    pre_mine = mine(pre_act)
    pre_beside = core_swap(theirs(pre_act))

    def chip_order(a, b):
        return jnp.concatenate(
            [jnp.where(core == 0, a, b), jnp.where(core == 0, b, a)], axis=1
        )

    pre_chip = chip_order(pre_mine, pre_beside).astype(F32)
    gain_chip = chip_order(gain_pair, gain_beside)
    mid_gain = gain_chip[0] * gain_chip[1]

    out_beside = [core_swap(block) for block in out_blocks]
    near_across, input_turned = tie(near_across, input_turned)
    out_blocks[7] = near_across
    away, there = hid_partial(place, conv_both, out_blocks, out_beside, ((2, 0), (0, -1)))
    passed, back = x_split(away, 1), x_split(there, -1)
    away, in_near = tie(away, in_near)
    in_here = jnp.stack([weight_in, in_near])
    conv_both, in_here = tie(conv_both, in_here)
    in_above, in_below = z_shift(in_here, -1), z_shift(in_here, 1)
    further, own = hid_partial(place, conv_both, out_blocks, out_beside, ((0, 1), (0, 0)))
    passed, back, own, in_above, in_below = tie(passed, back, own, in_above, in_below)
    far = x_split(add([further[1], passed[1]]).astype(BF16), 1)
    near = x_split(add([further[0], passed[0]]).astype(BF16), 1)
    in_across = onward(in_above, in_below, core, z_split)
    wout = dot(hidden_full, grad_conv, 0, 0).astype(BF16)
    crossed = y_hi_swap(add([own[1], back[1], far]).astype(BF16))
    crossed, near, wout, in_across = tie(crossed, near, wout, in_across)
    in_blocks = [in_here, in_above, in_below, in_across]
    grad_hid = add([own[0], back[0], near, crossed])
    alive = (pre_chip > 0) & (gain_chip[1] > 0)[None, :]
    grad_pre = jnp.where(alive, grad_hid, 0.0)
    mid_part = jnp.sum(grad_pre * pre_chip, axis=0).reshape(2, 128)
    grad_act = (grad_pre * mid_gain).astype(BF16)
    act_near = y_hi_swap(grad_act)
    act_above, act_below = x_shift(grad_act, -1), x_shift(grad_act, 1)
    act_near, act_above, act_below, wout, mid_part = tie(
        act_near, act_above, act_below, wout, mid_part
    )
    wout = lax.psum_scatter(wout, "row", scatter_dimension=0, tiled=True)
    near_above, near_below = x_shift(act_near, -1), x_shift(act_near, 1)

    mid_own = lax.dynamic_index_in_dim(mid_part, core, 0, keepdims=False)
    mid_away = lax.dynamic_index_in_dim(mid_part, 1 - core, 0, keepdims=False)
    mid_own = mid_own + core_swap(mid_away)
    sums = jnp.concatenate([mid_own, wide_part]).reshape(5, 128)
    sums = sums + z_flip(sums, 1)

    act_across = onward(act_above, act_below, core, x_split)
    near_above, near_below, act_across, sums = tie(near_above, near_below, act_across, sums)
    sums = sums + z_flip(sums, 2)
    near_across = onward(near_above, near_below, core, x_split)
    act = [
        grad_act, act_near, act_above, near_above, act_below, near_below, act_across, near_across
    ]
    act_beside = [core_swap(block) for block in act]
    act[7], sums = tie(act[7], sums)

    away, there, further, own = win_partial(place, input_turned, act, act_beside)
    passed, back = z_split(away, 1), z_split(there, -1)
    grad_x = out_gradient(place, cotangent, act, act_beside, in_blocks)
    grad_wout = wout.astype(F32) * scaling
    passed, back, grad_x, grad_wout = tie(passed, back, grad_x, grad_wout)
    far = z_split(add([further[1], passed[1]]).astype(BF16), 1)
    near = z_split(add([further[0], passed[0]]).astype(BF16), 1)
    crossed, sums = tie(add([own[1], back[1], far]).astype(BF16), sums)
    crossed = y_lo_swap(crossed)
    sums = sums + y_lo_swap(sums)
    grad_win = add([own[0], back[0], near, crossed]) * scaling
    grad_smid = keep_mid.astype(F32) * scaling * sums[0]
    grad_swide = keep_wide.astype(F32) * scaling * sums[1:].reshape(512)
    return (grad_x, grad_win, grad_wout, grad_smid, grad_swide)


def solution(mesh):
    return jax.shard_map(
        local,
        mesh=mesh,
        in_specs=(
            P("row", "col"),
            P("row", "col"),
            P("row", "col"),
            P("row", "col"),
            P("col", "row"),
            P("row", "col"),
            P("col"),
            P("col"),
            P("col"),
            P("col"),
        ),
        out_specs=(P("row", "col"), P("col", "row"), P("row", "col"), P("col"), P("col")),
        check_vma=False,
    )
```

```python
import functools
import math

import jax
import jax.numpy as jnp
from jax import lax
from jax.experimental import pallas as pl
from jax.experimental.pallas import tpu as pltpu
from jax.sharding import PartitionSpec as P

F32 = jnp.float32
BF16 = jnp.bfloat16
AXES = ("row", "col")
STEPS = (0, 1, 3, 2)


def permute(v, target):
    pairs = []
    for row in range(8):
        for col in range(16):
            y_lo, z, x, y_hi, core = target(
                row // 4, row % 4, col // 4, (col // 2) % 2, col % 2
            )
            pairs.append(
                (row * 16 + col, (y_lo * 4 + z % 4) * 16 + (x % 4) * 4 + y_hi * 2 + core)
            )
    return lax.ppermute(v, AXES, pairs)


def core_swap(v):
    return permute(v, lambda yl, z, x, yh, c: (yl, z, x, yh, 1 - c))


def y_hi_swap(v):
    return permute(v, lambda yl, z, x, yh, c: (yl, z, x, 1 - yh, c))


def y_lo_swap(v):
    return permute(v, lambda yl, z, x, yh, c: (1 - yl, z, x, yh, c))


def z_flip(v, mask):
    return permute(v, lambda yl, z, x, yh, c: (yl, z ^ mask, x, yh, c))


def x_shift(v, step):
    return permute(v, lambda yl, z, x, yh, c: (yl, z, x + step, yh, c))


def z_shift(v, step):
    return permute(v, lambda yl, z, x, yh, c: (yl, z + step, x, yh, c))


def x_split(v, way):
    return permute(v, lambda yl, z, x, yh, c: (yl, z, x + way * (1 - 2 * c), yh, c))


def z_split(v, way):
    return permute(v, lambda yl, z, x, yh, c: (yl, z + way * (1 - 2 * c), x, yh, c))


def dot(a, b, ca, cb):
    return lax.dot_general(a, b, (((ca,), (cb,)), ((), ())), preferred_element_type=F32)


def onward(above, below, core, split):
    return split(jnp.where(core == 0, below, above), 1)


def place_of(v):
    row, col = v[0], v[1]
    return row, row >> 2, row & 3, col >> 2, (col >> 1) & 1, col & 1


def slot_of(step):
    step = step & 3
    return jnp.where(step >= 2, 5 - step, step)


def row_slot(block, y_lo, z):
    return slot_of((block & 3) - z) * 2 + ((block >> 2) ^ y_lo)


def hidden_slot(block, x, y_hi):
    return slot_of((block >> 1) - x) * 2 + ((block & 1) ^ y_hi)


def call(body, outs, out_space, scratch, sems, loads, flops, here, vmem_args, any_args):
    vmem = pl.BlockSpec(memory_space=pltpu.VMEM)
    return pl.pallas_call(
        body,
        out_shape=outs,
        in_specs=[pl.BlockSpec(memory_space=pltpu.SMEM)]
        + [vmem] * len(vmem_args)
        + [pl.BlockSpec(memory_space=pl.ANY)] * len(any_args),
        out_specs=[pl.BlockSpec(memory_space=out_space)] * len(outs),
        scratch_shapes=[*scratch, pltpu.SemaphoreType.DMA((sems,))],
        compiler_params=pltpu.CompilerParams(vmem_limit_bytes=60 * 1024 * 1024),
        cost_estimate=pl.CostEstimate(flops=flops, bytes_accessed=loads, transcendentals=0),
    )(here, *vmem_args, *any_args)


def hid_kernel(ways, here, conv, *refs):
    blocks, outs, (held, sems) = refs[:16], refs[16:18], refs[18:]
    copies = [
        pltpu.make_async_copy(
            ref, held.at[k % 8, :, pl.ds((k // 8) * 512, 512)], sems.at[k]
        )
        for k, ref in enumerate(blocks)
    ]
    for copy in copies:
        copy.start()
    row, y_lo, z, x, y_hi, core = place_of(here)
    ahead = 1 - 2 * core
    for copy in copies:
        copy.wait()
    for j in range(4):
        fixed, way = ways[j // 2]
        block = ((x + fixed + way * ahead) & 3) * 2 + (y_hi ^ (j % 2))
        outs[j // 2][j % 2] = lax.dot_general(
            conv[...], held[row_slot(block, y_lo, z)], (((1,), (1,)), ((), ())),
            preferred_element_type=F32,
        ).astype(BF16)


def hid_partial(here, conv, blocks, beside, ways):
    return call(
        functools.partial(hid_kernel, ways), [jax.ShapeDtypeStruct((2, 768, 256), BF16)] * 2,
        pltpu.VMEM, [pltpu.VMEM((8, 256, 1024), BF16)], 16, 8 << 20, 768 * 1024 * 2048, here,
        [conv], [*blocks, *beside],
    )


def act_copies(own, beside, at, sems, first, core):
    copies = []
    for part, ref in enumerate((own, beside)):
        rows = pl.ds(pl.multiple_of((core ^ part) * 768, 768), 768)
        copies.append(pltpu.make_async_copy(ref, at(rows), sems.at[first + part]))
    return copies


def win_kernel(here, left, *refs):
    blocks, outs, (held, sems) = refs[:16], refs[16:20], refs[20:]
    row, y_lo, z, x, y_hi, core = place_of(here)
    copies = []
    for k in range(8):
        copies += act_copies(
            blocks[k], blocks[8 + k], lambda rows, k=k: held.at[k, rows, :], sems, 2 * k, core
        )
    for copy in copies:
        copy.start()
    for copy in copies:
        copy.wait()
    ahead = 1 - 2 * core
    for j in range(8):
        step = (2, -ahead, ahead, 0)[j // 2]
        block = (y_lo ^ (j % 2)) * 4 + ((z + step) & 3)
        outs[j // 2][j % 2] = jnp.dot(
            left[...], held[hidden_slot(block, x, y_hi)], preferred_element_type=F32
        ).astype(BF16)


def win_partial(here, left, blocks, beside):
    return call(
        win_kernel, [jax.ShapeDtypeStruct((2, 512, 256), BF16)] * 4, pltpu.VMEM,
        [pltpu.VMEM((8, 1536, 256), BF16)], 16, 10 << 20, 2 * 512 * 1536 * 2048, here, [left],
        [*blocks, *beside],
    )


def out_kernel(here, cot, *refs):
    blocks, parts, out = refs[:16], refs[16:20], refs[20]
    held, weights, sems = refs[21:]
    row, y_lo, z, x, y_hi, core = place_of(here)
    copies = [
        pltpu.make_async_copy(ref, weights.at[pl.ds(k * 2, 2)], sems.at[16 + k])
        for k, ref in enumerate(parts)
    ]
    for k in range(8):
        copies += act_copies(
            blocks[k], blocks[8 + k], lambda rows, k=k: held.at[k, rows, :], sems, 2 * k, core
        )
    for copy in copies:
        copy.start()
    for copy in copies:
        copy.wait()
    for at in range(0, 1536, 256):
        total = cot[at : at + 256, :].astype(F32)
        for block in range(8):
            total = total + lax.dot_general(
                held[hidden_slot(block, x, y_hi), at : at + 256, :],
                weights[row_slot(block, y_lo, z)],
                (((1,), (1,)), ((), ())),
                preferred_element_type=F32,
            )
        out[at : at + 256, :] = total.astype(BF16)


def out_gradient(here, cot, blocks, beside, weights):
    return call(
        out_kernel, [jax.ShapeDtypeStruct((1536, 512), BF16)], pltpu.VMEM,
        [pltpu.VMEM((8, 1536, 256), BF16), pltpu.VMEM((8, 512, 256), BF16)], 20, 12 << 20,
        2 * 1536 * 512 * 2048, here, [cot], [*blocks, *beside, *weights],
    )[0]


def tie(*values):
    return lax.optimization_barrier(values)


def add(terms):
    return sum(term.astype(F32) for term in terms)


def local(
    inputs,
    cotangent,
    conv_out,
    pre_act,
    weight_in,
    weight_out,
    scale_mid,
    scale_wide,
    keep_mid,
    keep_wide,
):
    rows = inputs.shape[0]
    half = rows // 2
    scaling = 1.0 / math.sqrt(rows * lax.axis_size("row"))
    row, col = lax.axis_index("row"), lax.axis_index("col")
    y_lo, z = row // 4, row % 4
    x, y_hi, core = col // 4, (col // 2) % 2, col % 2
    place = jnp.stack([row, col]).astype(jnp.int32)

    def mine(v):
        return lax.dynamic_slice_in_dim(v, core * half, half, 0)

    def theirs(v):
        return lax.dynamic_slice_in_dim(v, (1 - core) * half, half, 0)

    mid_gain = scale_mid * keep_mid.astype(F32)
    hidden = jnp.maximum(pre_act.astype(F32) * mid_gain, 0.0).astype(BF16)
    hidden_full = lax.all_gather(hidden, "col", axis=1, tiled=True)
    out_above, out_below = z_shift(weight_out, -1), z_shift(weight_out, 1)
    out_near = y_lo_swap(weight_out)

    wide_gain = scale_wide * keep_wide.astype(F32)
    cot_float = cotangent.astype(F32)
    grad_conv = (cot_float * wide_gain).astype(BF16)
    wide_part = jnp.sum(cot_float * conv_out.astype(F32), axis=0)
    conv_mine = mine(grad_conv)
    conv_sent, input_turned = theirs(grad_conv), inputs.T
    out_near, out_above, out_below, conv_sent, pre_act, weight_in = tie(
        out_near, out_above, out_below, conv_sent, pre_act, weight_in
    )
    near_above, near_below = z_shift(out_near, -1), z_shift(out_near, 1)
    out_across = onward(out_above, out_below, core, z_split)
    in_near = y_lo_swap(weight_in)
    conv_both = jnp.concatenate([conv_mine, core_swap(conv_sent)], axis=1)
    near_above, near_below, out_across, conv_both, in_near, wide_part, place = tie(
        near_above, near_below, out_across, conv_both, in_near, wide_part, place
    )
    near_across = onward(near_above, near_below, core, z_split)
    out_blocks = [
        weight_out, out_near, out_above, near_above, out_below, near_below, out_across, near_across
    ]

    gain_pair = jnp.stack([scale_mid, keep_mid.astype(F32)])
    gain_beside = core_swap(gain_pair)
    pre_mine = mine(pre_act)
    pre_beside = core_swap(theirs(pre_act))

    def chip_order(a, b):
        return jnp.concatenate(
            [jnp.where(core == 0, a, b), jnp.where(core == 0, b, a)], axis=1
        )

    pre_chip = chip_order(pre_mine, pre_beside).astype(F32)
    gain_chip = chip_order(gain_pair, gain_beside)
    mid_gain = gain_chip[0] * gain_chip[1]

    out_beside = [core_swap(block) for block in out_blocks]
    near_across, input_turned = tie(near_across, input_turned)
    out_blocks[7] = near_across
    away, there = hid_partial(place, conv_both, out_blocks, out_beside, ((2, 0), (0, -1)))
    passed, back = x_split(away, 1), x_split(there, -1)
    away, in_near = tie(away, in_near)
    in_here = jnp.stack([weight_in, in_near])
    conv_both, in_here = tie(conv_both, in_here)
    in_above, in_below = z_shift(in_here, -1), z_shift(in_here, 1)
    further, own = hid_partial(place, conv_both, out_blocks, out_beside, ((0, 1), (0, 0)))
    passed, back, own, in_above, in_below = tie(passed, back, own, in_above, in_below)
    far = x_split(add([further[1], passed[1]]).astype(BF16), 1)
    near = x_split(add([further[0], passed[0]]).astype(BF16), 1)
    in_across = onward(in_above, in_below, core, z_split)
    wout = dot(hidden_full, grad_conv, 0, 0).astype(BF16)
    crossed = y_hi_swap(add([own[1], back[1], far]).astype(BF16))
    crossed, near, wout, in_across = tie(crossed, near, wout, in_across)
    in_blocks = [in_here, in_above, in_below, in_across]
    grad_hid = add([own[0], back[0], near, crossed])
    alive = (pre_chip > 0) & (gain_chip[1] > 0)[None, :]
    grad_pre = jnp.where(alive, grad_hid, 0.0)
    mid_part = jnp.sum(grad_pre * pre_chip, axis=0).reshape(2, 128)
    grad_act = (grad_pre * mid_gain).astype(BF16)
    act_near = y_hi_swap(grad_act)
    act_above, act_below = x_shift(grad_act, -1), x_shift(grad_act, 1)
    act_near, act_above, act_below, wout, mid_part = tie(
        act_near, act_above, act_below, wout, mid_part
    )
    wout = lax.psum_scatter(wout, "row", scatter_dimension=0, tiled=True)
    near_above, near_below = x_shift(act_near, -1), x_shift(act_near, 1)

    mid_own = lax.dynamic_index_in_dim(mid_part, core, 0, keepdims=False)
    mid_away = lax.dynamic_index_in_dim(mid_part, 1 - core, 0, keepdims=False)
    mid_own = mid_own + core_swap(mid_away)
    sums = jnp.concatenate([mid_own, wide_part]).reshape(5, 128)
    sums = sums + z_flip(sums, 1)

    act_across = onward(act_above, act_below, core, x_split)
    near_above, near_below, act_across, sums = tie(near_above, near_below, act_across, sums)
    sums = sums + z_flip(sums, 2)
    near_across = onward(near_above, near_below, core, x_split)
    act = [
        grad_act, act_near, act_above, near_above, act_below, near_below, act_across, near_across
    ]
    act_beside = [core_swap(block) for block in act]
    act[7], sums = tie(act[7], sums)

    away, there, further, own = win_partial(place, input_turned, act, act_beside)
    passed, back = z_split(away, 1), z_split(there, -1)
    grad_x = out_gradient(place, cotangent, act, act_beside, in_blocks)
    grad_wout = wout.astype(F32) * scaling
    passed, back, grad_x, grad_wout = tie(passed, back, grad_x, grad_wout)
    far = z_split(add([further[1], passed[1]]).astype(BF16), 1)
    near = z_split(add([further[0], passed[0]]).astype(BF16), 1)
    crossed = y_lo_swap(add([own[1], back[1], far]).astype(BF16))
    sums = sums + y_lo_swap(sums)
    grad_win = add([own[0], back[0], near, crossed]) * scaling
    grad_smid = keep_mid.astype(F32) * scaling * sums[0]
    grad_swide = keep_wide.astype(F32) * scaling * sums[1:].reshape(512)
    return (grad_x, grad_win, grad_wout, grad_smid, grad_swide)


def solution(mesh):
    return jax.shard_map(
        local,
        mesh=mesh,
        in_specs=(
            P("row", "col"),
            P("row", "col"),
            P("row", "col"),
            P("row", "col"),
            P("col", "row"),
            P("row", "col"),
            P("col"),
            P("col"),
            P("col"),
            P("col"),
        ),
        out_specs=(P("row", "col"), P("col", "row"), P("row", "col"), P("col"), P("col")),
        check_vma=False,
    )
```
